32 devices in a mesh: seq: 4 (over y, x), dp: 8 (over z, core).
Axes of the slice: x: 2, y: 2, z: 4, core: 2. Of those that a mesh axis runs over, the one named last changes fastest.
Arguments:
- hidden_in: bfloat16 [32, 1024, 768], P('dp', 'seq'), may hold values from -6 to 6
- positions: int32 [32, 1024], P('dp', 'seq'), may hold values from 0 to 3069, as said below
- attn_gain: float32 [768], replicated, may hold values from 0.1 to 1.9
- attn_shift: float32 [768], replicated, may hold values from -1.75 to 1.75
- qkv_weight: bfloat16 [768, 2304], replicated, may hold values from -0.21875 to 0.21875
- qkv_bias: float32 [2304], replicated, may hold values from -1.75 to 1.75
- dense_weight: bfloat16 [768, 768], replicated, may hold values from -1.25 to 1.25
- dense_bias: float32 [768], replicated, may hold values from -1.75 to 1.75
- mlp_gain: float32 [768], replicated, may hold values from 0.1 to 1.9
- mlp_shift: float32 [768], replicated, may hold values from -1.75 to 1.75
- up_weight: bfloat16 [768, 3072], replicated, may hold values from -0.21875 to 0.21875
- up_bias: float32 [3072], replicated, may hold values from -1.75 to 1.75
- down_weight: bfloat16 [3072, 768], replicated, may hold values from -0.109375 to 0.109375
- down_bias: float32 [768], replicated, may hold values from -1.75 to 1.75
- out_grad: bfloat16 [32, 1024, 768], P('dp', 'seq'), may hold values from -6 to 6
Outputs:
- layer_out: bfloat16 [32, 1024, 768], P('dp', 'seq')
- input_grad: bfloat16 [32, 1024, 768], P('dp', 'seq')
- attn_gain_grad: float32 [768], replicated
- attn_shift_grad: float32 [768], replicated
- qkv_weight_grad: float32 [768, 2304], replicated
- qkv_bias_grad: float32 [2304], replicated
- dense_weight_grad: float32 [768, 768], replicated
- dense_bias_grad: float32 [768], replicated
- mlp_gain_grad: float32 [768], replicated
- mlp_shift_grad: float32 [768], replicated
- up_weight_grad: float32 [768, 3072], replicated
- up_bias_grad: float32 [3072], replicated
- down_weight_grad: float32 [3072, 768], replicated
- down_bias_grad: float32 [768], replicated
The draws below stay inside these ranges and needn't reach their ends.
Inputs may be any that keep to these rules, and one draw needn't show every extreme that they name: Along each sentence, positions start at 0 and rise by 1 to 3 from one token to the next; in one sentence of each draw they rise by 3 throughout.
All inputs are finite; a program needn't handle non-finite values.
Results may differ from the reference program's by a relative error of at most 0.014.
Values may be sent and summed in bfloat16 or wider, within the bound.
A program may use at most 320 MiB of HBM per device.

```python
import jax
import jax.numpy as jnp
from jax import lax

D = 768
HEADS = 12
HEAD = 64
ROT = 16
FF = 3072
LEN = 1024
SEQUENCES = 32


def draw_positions(key, part):
    key = jax.random.fold_in(key, 7)
    steps = jax.random.randint(key, (SEQUENCES, LEN), 1, 4).astype(jnp.int32)
    chosen = jax.random.randint(jax.random.fold_in(key, 11), (), 0, SEQUENCES).astype(jnp.int32)
    steady = jnp.arange(SEQUENCES, dtype=jnp.int32)[:, None] == chosen
    steps = jnp.where(steady, jnp.int32(3), steps).astype(jnp.int32)
    return (jnp.cumsum(steps, axis=1) - steps[:, 0:1]).astype(jnp.int32)


def block_scale(own_key, extent, pieces, smallest, high):
    def one(axis_at, parts):
        steps = jax.random.uniform(jax.random.fold_in(jax.random.fold_in(own_key, 6), axis_at), (parts,), jnp.float32, smallest / len(pieces), high / len(pieces))
        return jnp.repeat(jnp.exp(steps), extent[axis_at] // parts).reshape((-1,) + (1,) * (len(extent) - axis_at - 1))

    level = one(*pieces[0])
    for cut in pieces[1:]:
        level = level * one(*cut)
    return level


def gaussian(stream_key, dims, scale, most, cuts=(), kind=jnp.bfloat16):
    array = jax.random.normal(stream_key, dims, jnp.float32) * scale
    if len(cuts) > 0:
        array = block_scale(stream_key, dims, cuts, -0.22, 0.18) * array
    return jnp.clip(array, min=-most, max=most).astype(kind)


def setup_inputs(seed: int = 0) -> dict:
    splits = jax.random.split(jax.random.key(seed), 16)
    hidden_in = gaussian(splits[0], (SEQUENCES, LEN, D), 1.0, 6.0, ((0, 8), (1, 4)))
    positions = draw_positions(jax.random.fold_in(splits[15], 71), 0)
    attn_gain = jnp.clip(1.0 + 0.18 * jax.random.normal(splits[2], (D,), jnp.float32), 0.1, 1.9)
    attn_shift = gaussian(splits[3], (D,), 0.3, 1.75, (), jnp.float32)
    qkv_weight = gaussian(splits[4], (D, 3 * D), D ** -0.5, 0.21875)
    qkv_bias = gaussian(splits[5], (3 * D,), 0.3, 1.75, (), jnp.float32)
    dense_weight = gaussian(splits[6], (D, D), (D // 32) ** -0.5, 1.25)
    dense_bias = gaussian(splits[7], (D,), 0.3, 1.75, (), jnp.float32)
    mlp_gain = jnp.clip(1.0 + 0.18 * jax.random.normal(splits[8], (D,), jnp.float32), 0.1, 1.9)
    mlp_shift = gaussian(splits[9], (D,), 0.3, 1.75, (), jnp.float32)
    up_weight = gaussian(splits[10], (D, FF), D ** -0.5, 0.21875)
    up_bias = gaussian(splits[11], (FF,), 0.3, 1.75, (), jnp.float32)
    down_weight = gaussian(splits[12], (FF, D), FF ** -0.5, 0.109375)
    down_bias = gaussian(splits[13], (D,), 0.3, 1.75, (), jnp.float32)
    out_grad = gaussian(splits[14], (SEQUENCES, LEN, D), 1.0, 6.0, ((0, 8), (1, 4)))
    return dict(hidden_in=hidden_in, positions=positions, attn_gain=attn_gain, attn_shift=attn_shift, qkv_weight=qkv_weight, qkv_bias=qkv_bias, dense_weight=dense_weight, dense_bias=dense_bias, mlp_gain=mlp_gain, mlp_shift=mlp_shift, up_weight=up_weight, up_bias=up_bias, down_weight=down_weight, down_bias=down_bias, out_grad=out_grad)


@jax.custom_vjp
def low(v):
    return lax.optimization_barrier(v.astype(jnp.bfloat16)).astype(jnp.float32)

@jax.custom_vjp
def low_back(v):
    return v

def low_keep(v):
    return (low(v), None)

def low_pass(kept, grad):
    return (grad,)

def back_keep(v):
    return (v, None)

def back_low(kept, grad):
    return (low(grad),)
low.defvjp(low_keep, low_pass)
low_back.defvjp(back_keep, back_low)
EPSILON = 1e-05
NEGATIVE = -1e+30
HIGH = lax.Precision.HIGHEST

def normalize(values, gain, shift):
    center = values - lax.optimization_barrier(jnp.mean(values, axis=-1, keepdims=True))
    spread = lax.optimization_barrier(jnp.mean(center * center, axis=-1, keepdims=True))
    return center * lax.rsqrt(spread + EPSILON) * gain + shift

def angles_of(positions, half_dims):
    freqs = jnp.power(10000.0, -2.0 * jnp.arange(half_dims, dtype=jnp.float32) / (2 * half_dims))
    return positions.astype(jnp.float32)[..., None] * freqs

def rotate(values, angles):
    half_dims = angles.shape[-1]
    cosine = jnp.cos(angles)[..., None, :]
    sine = jnp.sin(angles)[..., None, :]
    first = values[..., :half_dims]
    second = values[..., half_dims:2 * half_dims]
    return jnp.concatenate([first * cosine - second * sine, second * cosine + first * sine, values[..., 2 * half_dims:]], axis=-1)

def one_sentence(params, hidden, positions):
    attn_gain, attn_shift, qkv_weight, qkv_bias, dense_weight, dense_bias, mlp_gain, mlp_shift, up_weight, up_bias, down_weight, down_bias = params
    length = hidden.shape[0]
    scale = HEAD ** (-0.5)
    normed = low(normalize(hidden, attn_gain, attn_shift))
    mixed = low_back(jnp.dot(normed, qkv_weight, precision=HIGH) + qkv_bias)
    angles = angles_of(positions, ROT // 2)
    queries = low(rotate(mixed[:, :D].reshape(length, HEADS, HEAD), angles))
    keys = low(rotate(mixed[:, D:2 * D].reshape(length, HEADS, HEAD), angles))
    values = low(mixed[:, 2 * D:].reshape(length, HEADS, HEAD))
    scores = low_back(jnp.einsum('qhd,khd->hqk', queries, keys, precision=HIGH) * scale)
    index = jnp.arange(length)
    allowed = index[:, None] >= index[None, :]
    masked = jnp.where(allowed, scores, NEGATIVE)
    top = lax.optimization_barrier(jnp.max(masked, axis=-1, keepdims=True))
    weights = jnp.where(allowed, jnp.exp(masked - top), 0.0)
    total = lax.optimization_barrier(jnp.sum(weights, axis=-1))
    attended = jnp.einsum('hqk,khd->qhd', low(weights), values, precision=HIGH) / jnp.transpose(total)[:, :, None]
    attended = low(low_back(attended.reshape(length, D)))
    attn = jnp.dot(attended, dense_weight, precision=HIGH) + dense_bias
    normed_mlp = low(normalize(hidden, mlp_gain, mlp_shift))
    upper = low_back(jnp.dot(normed_mlp, up_weight, precision=HIGH) + up_bias)
    active = low(jax.nn.gelu(upper, approximate=False))
    return hidden + attn + jnp.dot(active, down_weight, precision=HIGH) + down_bias

def reference(hidden_in, positions, attn_gain, attn_shift, qkv_weight, qkv_bias, dense_weight, dense_bias, mlp_gain, mlp_shift, up_weight, up_bias, down_weight, down_bias, out_grad):
    params = tuple((p.astype(jnp.float32) for p in (attn_gain, attn_shift, qkv_weight, qkv_bias, dense_weight, dense_bias, mlp_gain, mlp_shift, up_weight, up_bias, down_weight, down_bias)))
    hidden = hidden_in.astype(jnp.float32)

    def forward(hidden_all, *weights):

        def step(item):
            return one_sentence(weights, item[0], item[1])
        return lax.map(jax.checkpoint(step), (hidden_all, positions))
    result, pullback = jax.vjp(forward, hidden, *params)
    grads = pullback(out_grad.astype(jnp.float32))
    return (result.astype(jnp.bfloat16), grads[0].astype(jnp.bfloat16), grads[1], grads[2], grads[3], grads[4], grads[5], grads[6], grads[7], grads[8], grads[9], grads[10], grads[11], grads[12])
```

```python
import functools
import jax, jax.numpy as jnp
from jax import lax
from jax.experimental import pallas as pl
from jax.experimental.pallas import tpu as pltpu

HEADS, HEAD, ROT = 12, 64, 16
EPSILON = 1e-5
BF, F32 = jnp.bfloat16, jnp.float32
BLK = 256

def nn(a, b): return lax.dot_general(a, b, (((1,), (0,)), ((), ())), preferred_element_type=F32)
def nt(a, b): return lax.dot_general(a, b, (((1,), (1,)), ((), ())), preferred_element_type=F32)
def tn(a, b): return lax.dot_general(a, b, (((0,), (0,)), ((), ())), preferred_element_type=F32)

def norm_parts(x):
    mean = jnp.mean(x, axis=-1, keepdims=True)
    c = x - mean
    rstd = lax.rsqrt(jnp.mean(c * c, axis=-1, keepdims=True) + EPSILON)
    return c * rstd, rstd

def attn_kernel(x_ref, g_ref, cos_ref, sin_ref, gain_ref, shift_ref, wqkv_ref, bqkv_ref, wd_ref,
                attn_ref, ga_ref, dwqkv_ref, dwd_ref, small_ref, dbq_ref,
                wT, xaT, qkvT, kn, vn, dOT, obT, dmT):
    T, W = x_ref.shape
    nblk = T // BLK
    gain = gain_ref[...]; shift = shift_ref[...]
    for j in range(9):
        wT[j*256:(j+1)*256, :] = wqkv_ref[:, j*256:(j+1)*256].T

    @pl.loop(0, nblk)
    def _(b):
        rows = pl.ds(pl.multiple_of(b * BLK, BLK), BLK)
        x = x_ref[rows, :].astype(F32)
        xhat, _ = norm_parts(x)
        xa = (xhat * gain + shift).astype(BF)
        xaT[:, rows] = xa.T
        cos = cos_ref[:, rows]; sin = sin_ref[:, rows]
        for j in range(9):
            m = nt(wT[j*256:(j+1)*256, :], xa) + bqkv_ref[j*256:(j+1)*256, :]
            if j < 6:
                parts = []
                for h in range(4):
                    u = m[h*64:(h+1)*64]
                    u0, u1 = u[:8], u[8:16]
                    parts += [u0 * cos - u1 * sin, u1 * cos + u0 * sin, u[16:]]
                m = jnp.concatenate(parts, axis=0)
                if j < 3: m = m * (HEAD ** -0.5)
            mb = m.astype(BF)
            qkvT[j*256:(j+1)*256, rows] = mb
            if 3 <= j < 6: kn[rows, (j-3)*256:(j-2)*256] = mb.T
            if j >= 6: vn[rows, (j-6)*256:(j-5)*256] = mb.T
        g = g_ref[rows, :]
        for j in range(3):
            dOT[j*256:(j+1)*256, rows] = nt(wd_ref[j*256:(j+1)*256, :], g).astype(BF)

    sub = lax.broadcasted_iota(jnp.int32, (BLK, BLK), 0)
    lane = lax.broadcasted_iota(jnp.int32, (BLK, BLK), 1)
    keep = sub <= lane
    rowid = lax.broadcasted_iota(jnp.int32, (128, 1), 0)

    @pl.loop(0, HEADS // 2)
    def _(hp):
        r0 = pl.multiple_of(hp * 128, 128)
        cols = pl.ds(r0, 128)
        for hh in range(2):
            hr = pl.ds(pl.multiple_of(r0 + hh * 64, 64), 64)
            kr = pl.ds(pl.multiple_of(W + r0 + hh * 64, 64), 64)
            vr = pl.ds(pl.multiple_of(2 * W + r0 + hh * 64, 64), 64)
            msk = (rowid // 64 == hh)
            dk = [None] * nblk; dv = [None] * nblk
            for i in range(nblk):
                n = (i + 1) * BLK
                qs = slice(i * BLK, (i + 1) * BLK)
                qT2 = jnp.where(msk, qkvT[pl.ds(r0, 128), qs], 0).astype(BF)
                dO2 = jnp.where(msk, dOT[pl.ds(r0, 128), qs], 0).astype(BF)
                s = nn(kn[0:n, cols], qT2)
                d = jnp.where(keep, s[n-BLK:], -1e30)
                if n > BLK: s = jnp.concatenate([s[:n-BLK], d], axis=0)
                else: s = d
                m = jnp.max(s, axis=0, keepdims=True)
                e = jnp.exp(s - m)
                l = jnp.sum(e, axis=0, keepdims=True)
                inv = 1.0 / l
                p = e.astype(BF)
                oT = nn(qkvT[vr, 0:n], p) * inv
                dO = dOT[hr, qs].astype(F32)
                delta = jnp.sum(dO * oT, axis=0, keepdims=True)
                obT[hr, qs] = oT.astype(BF)
                dp = nn(vn[0:n, cols], dO2)
                ds = (e * ((dp - delta) * inv)).astype(BF)
                dqT = nn(qkvT[kr, 0:n], ds) * (HEAD ** -0.5)
                dkT = nt(qkvT[hr, qs], ds)
                dvT = nt((dO * inv).astype(BF), p)
                cos = cos_ref[:, qs]; sin = sin_ref[:, qs]
                d0, d1 = dqT[:8], dqT[8:16]
                dqT = jnp.concatenate([d0 * cos + d1 * sin, d1 * cos - d0 * sin, dqT[16:]], axis=0)
                dmT[hr, qs] = dqT.astype(BF)
                for b in range(i + 1):
                    sl = slice(b * BLK, (b + 1) * BLK)
                    dk[b] = dkT[:, sl] if dk[b] is None else dk[b] + dkT[:, sl]
                    dv[b] = dvT[:, sl] if dv[b] is None else dv[b] + dvT[:, sl]
            for b in range(nblk):
                sl = slice(b * BLK, (b + 1) * BLK)
                cos = cos_ref[:, sl]; sin = sin_ref[:, sl]
                d0, d1 = dk[b][:8], dk[b][8:16]
                dmT[kr, sl] = jnp.concatenate([d0 * cos + d1 * sin, d1 * cos - d0 * sin, dk[b][16:]], axis=0).astype(BF)
                dmT[vr, sl] = dv[b].astype(BF)

    small_ref[...] = jnp.zeros_like(small_ref)
    @pl.loop(0, nblk)
    def _(b):
        rows = pl.ds(pl.multiple_of(b * BLK, BLK), BLK)
        ob = obT[:, rows].T
        attn_ref[rows, :] = nn(ob, wd_ref[...]).astype(BF)
        dxa = nn(wqkv_ref[...], dmT[:, rows]).T
        xhat, rstd = norm_parts(x_ref[rows, :].astype(F32))
        small_ref[0:1, :] += jnp.sum(dxa * xhat, axis=0, keepdims=True)
        small_ref[1:2, :] += jnp.sum(dxa, axis=0, keepdims=True)
        small_ref[2:3, :] += jnp.sum(g_ref[rows, :].astype(F32), axis=0, keepdims=True)
        dn = dxa * gain
        ga = rstd * (dn - jnp.mean(dn, axis=-1, keepdims=True) - xhat * jnp.mean(dn * xhat, axis=-1, keepdims=True))
        ga_ref[rows, :] = ga.astype(BF)
    dwd_ref[...] = nn(obT[...], g_ref[...]).astype(BF)
    @pl.loop(0, 9)
    def _(j):
        c = pl.ds(pl.multiple_of(j * 256, 256), 256)
        dm = dmT[c, :]
        dwqkv_ref[:, c] = nt(xaT[...], dm).astype(BF)
        dbq_ref[:, c] = nt(jnp.ones((8, T), BF), dm)

def attn_call(x, g, cosT, sinT, gain, shift, wqkv, bqkv, wd):
    T, W = x.shape
    vm = pl.BlockSpec(memory_space=pltpu.VMEM)
    return pl.pallas_call(
        attn_kernel,
        out_shape=(jax.ShapeDtypeStruct((T, W), BF), jax.ShapeDtypeStruct((T, W), BF),
                   jax.ShapeDtypeStruct((W, 3*W), BF), jax.ShapeDtypeStruct((W, W), BF),
                   jax.ShapeDtypeStruct((8, W), F32), jax.ShapeDtypeStruct((8, 3*W), F32)),
        in_specs=[vm]*9, out_specs=(vm,)*6,
        scratch_shapes=[pltpu.VMEM((3*W, W), BF), pltpu.VMEM((W, T), BF), pltpu.VMEM((3*W, T), BF),
                        pltpu.VMEM((T, W), BF), pltpu.VMEM((T, W), BF), pltpu.VMEM((W, T), BF), pltpu.VMEM((W, T), BF),
                        pltpu.VMEM((3*W, T), BF)],
        compiler_params=pltpu.CompilerParams(vmem_limit_bytes=60 << 20),
    )(x, g, cosT, sinT, gain.reshape(1, W), shift.reshape(1, W), wqkv, bqkv.reshape(3*W, 1), wd)
from jax.sharding import PartitionSpec as P

def erf_parts(h):
    z = jnp.abs(h) * (0.5 ** 0.5)
    t = 1.0 / (1.0 + 0.3275911 * z)
    ez = jnp.exp(-0.5 * h * h)
    poly = t * (0.254829592 + t * (-0.284496736 + t * (1.421413741 + t * (-1.453152027 + t * 1.061405429))))
    tail = 0.5 * poly * ez
    return jnp.where(h >= 0, 1.0 - tail, tail), ez * 0.3989422804014327

def mlp_kernel(x_ref, g_ref, gain_ref, shift_ref, wu_ref, bu_ref, wd_ref, bias_ref,
               y_ref, gm_ref, dwu_ref, dwd_ref, small_ref, dbu_ref,
               xm, xmT, yacc, dxm):
    T, W = x_ref.shape
    FF = wu_ref.shape[1]
    C = 256
    nblk = T // BLK
    gain = gain_ref[...]; shift = shift_ref[...]
    @pl.loop(0, nblk)
    def _(b):
        rows = pl.ds(pl.multiple_of(b * BLK, BLK), BLK)
        x = x_ref[rows, :].astype(F32)
        xhat, _ = norm_parts(x)
        v = (xhat * gain + shift).astype(BF)
        xm[rows, :] = v
        xmT[:, rows] = v.T
        yacc[rows, :] = x + bias_ref[...]
    dxm[...] = jnp.zeros_like(dxm)

    @pl.loop(0, FF // C)
    def _(j):
        c = pl.ds(pl.multiple_of(j * C, C), C)
        wu = wu_ref[:, c]
        wd = wd_ref[c, :]
        bu = bu_ref[:, c]
        a_l, dh_l = [], []
        dbu = jnp.zeros((1, C), F32)
        for b in range(nblk):
            rows = slice(b * BLK, (b + 1) * BLK)
            h = nn(xm[rows, :], wu) + bu
            cdf, pdf = erf_parts(h)
            a = (h * cdf).astype(BF)
            da = nt(g_ref[rows, :], wd)
            dh = (da * (cdf + h * pdf)).astype(BF)
            dbu += jnp.sum(dh.astype(F32), axis=0, keepdims=True)
            a_l.append(a); dh_l.append(dh)
        a = jnp.concatenate(a_l, 0); dh = jnp.concatenate(dh_l, 0)
        dbu_ref[:, c] = dbu
        yacc[...] += nn(a, wd)
        dxm[...] += nt(dh, wu)
        dwu_ref[:, c] = nn(xmT[...], dh).astype(BF)
        dwd_ref[c, :] = tn(a, g_ref[...]).astype(BF)

    small_ref[...] = jnp.zeros_like(small_ref)
    @pl.loop(0, nblk)
    def _(b):
        rows = pl.ds(pl.multiple_of(b * BLK, BLK), BLK)
        y_ref[rows, :] = yacc[rows, :]
        xhat, rstd = norm_parts(x_ref[rows, :].astype(F32))
        dxa = dxm[rows, :]
        gf = g_ref[rows, :].astype(F32)
        small_ref[0:1, :] += jnp.sum(dxa * xhat, axis=0, keepdims=True)
        small_ref[1:2, :] += jnp.sum(dxa, axis=0, keepdims=True)
        small_ref[2:3, :] += jnp.sum(gf, axis=0, keepdims=True)
        dn = dxa * gain
        gm = rstd * (dn - jnp.mean(dn, axis=-1, keepdims=True) - xhat * jnp.mean(dn * xhat, axis=-1, keepdims=True))
        gm_ref[rows, :] = gm + gf

def mlp_call(x, g, gain, shift, wu, bu, wd, bias):
    T, W = x.shape
    FF = wu.shape[1]
    vm = pl.BlockSpec(memory_space=pltpu.VMEM)
    S = jax.ShapeDtypeStruct
    return pl.pallas_call(
        mlp_kernel,
        out_shape=(S((T, W), F32), S((T, W), F32), S((W, FF), BF), S((FF, W), BF), S((8, W), F32), S((1, FF), F32)),
        in_specs=[vm]*8, out_specs=(vm,)*6,
        scratch_shapes=[pltpu.VMEM((T, W), BF), pltpu.VMEM((W, T), BF), pltpu.VMEM((T, W), F32), pltpu.VMEM((T, W), F32)],
        compiler_params=pltpu.CompilerParams(vmem_limit_bytes=60 << 20),
    )(x, g, gain.reshape(1, W), shift.reshape(1, W), wu, bu.reshape(1, FF), wd, bias.reshape(1, W))


def on_device(hidden_in, positions, attn_gain, attn_shift, qkv_weight, qkv_bias, dense_weight, dense_bias,
              mlp_gain, mlp_shift, up_weight, up_bias, down_weight, down_bias, out_grad):
    sentences, local_len, width = hidden_in.shape
    seq = lax.axis_size("seq")
    assert sentences == seq
    tokens = sentences * local_len

    def to_sentence(v):
        return lax.all_to_all(v, "seq", 0, 1, tiled=True)[0]

    def to_rows(v):
        return lax.all_to_all(v[None], "seq", 1, 0, tiled=True)

    x_s = to_sentence(hidden_in)
    g_s = to_sentence(out_grad)
    pos = to_sentence(positions)
    freqs = jnp.power(10000.0, -2.0 * jnp.arange(ROT // 2, dtype=F32) / ROT)
    angles = freqs[:, None] * pos.astype(F32)[None, :]
    y, gm, dwu, dwd, small_m, dbu = mlp_call(
        hidden_in.reshape(tokens, width), out_grad.reshape(tokens, width), mlp_gain, mlp_shift,
        up_weight, up_bias, down_weight, dense_bias + down_bias)
    dwu, dwd = lax.psum((dwu, dwd), ("seq", "dp"))
    attn, ga, dwqkv, ddw, small_a, dbq = attn_call(
        x_s, g_s, jnp.cos(angles), jnp.sin(angles), attn_gain, attn_shift, qkv_weight, qkv_bias, dense_weight)
    attn = to_rows(attn)
    ga = to_rows(ga)
    layer_out = (y.reshape(hidden_in.shape) + attn.astype(F32)).astype(BF)
    input_grad = (gm.reshape(hidden_in.shape) + ga.astype(F32)).astype(BF)
    dwqkv, ddw = lax.psum((dwqkv, ddw), ("seq", "dp"))
    s = lax.psum((small_a[0], small_a[1], dbq[0], small_m[0], small_m[1], small_m[2], dbu[0]), ("seq", "dp"))
    return (layer_out, input_grad, s[0], s[1], dwqkv.astype(F32), s[2], ddw.astype(F32), s[5], s[3], s[4],
            dwu.astype(F32), s[6], dwd.astype(F32), s[5])


def solution(mesh):
    act, rep = P("dp", "seq", None), P()
    return jax.shard_map(
        on_device, mesh=mesh,
        in_specs=(act, P("dp", "seq")) + (rep,) * 12 + (act,),
        out_specs=(act, act) + (rep,) * 12,
        check_vma=False)
```

```python
import functools
import jax, jax.numpy as jnp
from jax import lax
from jax.experimental import pallas as pl
from jax.experimental.pallas import tpu as pltpu
from jax.sharding import PartitionSpec as P

HEADS, HEAD, ROT = 12, 64, 16
EPSILON = 1e-5
BF, F32 = jnp.bfloat16, jnp.float32
BLK = 256

def nn(a, b): return lax.dot_general(a, b, (((1,), (0,)), ((), ())), preferred_element_type=F32)
def nt(a, b): return lax.dot_general(a, b, (((1,), (1,)), ((), ())), preferred_element_type=F32)
def tn(a, b): return lax.dot_general(a, b, (((0,), (0,)), ((), ())), preferred_element_type=F32)

def norm_parts(x):
    mean = jnp.mean(x, axis=-1, keepdims=True)
    c = x - mean
    rstd = lax.rsqrt(jnp.mean(c * c, axis=-1, keepdims=True) + EPSILON)
    return c * rstd, rstd

def attn_kernel(x_ref, g_ref, cs_ref, gain_ref, shift_ref, wqkv_ref, bqkv_ref, wd_ref,
                attn_ref, ga_ref, da_ref, small_ref, dbq_ref,
                wT, xaT, qkvT, kn, vn, dOT, obT, dmT):
    T, W = x_ref.shape
    nblk = T // BLK
    gain = gain_ref[...]; shift = shift_ref[...]
    for j in range(9):
        wT[j*256:(j+1)*256, :] = wqkv_ref[:, j*256:(j+1)*256].T

    @pl.loop(0, nblk)
    def _(b):
        rows = pl.ds(pl.multiple_of(b * BLK, BLK), BLK)
        x = x_ref[rows, :].astype(F32)
        xhat, _ = norm_parts(x)
        xa = (xhat * gain + shift).astype(BF)
        xaT[:, rows] = xa.T
        cos = cs_ref[b, :8, :]; sin = cs_ref[b, 8:, :]
        for j in range(9):
            m = nt(wT[j*256:(j+1)*256, :], xa) + bqkv_ref[j*256:(j+1)*256, :]
            if j < 6:
                parts = []
                for h in range(4):
                    u = m[h*64:(h+1)*64]
                    u0, u1 = u[:8], u[8:16]
                    parts += [u0 * cos - u1 * sin, u1 * cos + u0 * sin, u[16:]]
                m = jnp.concatenate(parts, axis=0)
                if j < 3: m = m * (HEAD ** -0.5)
            mb = m.astype(BF)
            qkvT[j*256:(j+1)*256, rows] = mb
            if 3 <= j < 6: kn[rows, (j-3)*256:(j-2)*256] = mb.T
            if j >= 6: vn[rows, (j-6)*256:(j-5)*256] = mb.T
        g = g_ref[rows, :]
        for j in range(3):
            dOT[j*256:(j+1)*256, rows] = nt(wd_ref[j*256:(j+1)*256, :], g).astype(BF)

    sub = lax.broadcasted_iota(jnp.int32, (BLK, BLK), 0)
    lane = lax.broadcasted_iota(jnp.int32, (BLK, BLK), 1)
    keep = sub <= lane
    rowid = lax.broadcasted_iota(jnp.int32, (128, 1), 0)

    @pl.loop(0, HEADS // 2)
    def _(hp):
        r0 = pl.multiple_of(hp * 128, 128)
        cols = pl.ds(r0, 128)
        for hh in range(2):
            hr = pl.ds(pl.multiple_of(r0 + hh * 64, 64), 64)
            kr = pl.ds(pl.multiple_of(W + r0 + hh * 64, 64), 64)
            vr = pl.ds(pl.multiple_of(2 * W + r0 + hh * 64, 64), 64)
            msk = (rowid // 64 == hh)
            dk = [None] * nblk; dv = [None] * nblk
            for i in range(nblk):
                n = (i + 1) * BLK
                qs = slice(i * BLK, (i + 1) * BLK)
                qT2 = jnp.where(msk, qkvT[pl.ds(r0, 128), qs], 0).astype(BF)
                dO2 = jnp.where(msk, dOT[pl.ds(r0, 128), qs], 0).astype(BF)
                s = nn(kn[0:n, cols], qT2)
                d = jnp.where(keep, s[n-BLK:], -1e30)
                if n > BLK: s = jnp.concatenate([s[:n-BLK], d], axis=0)
                else: s = d
                m = jnp.max(s, axis=0, keepdims=True)
                e = jnp.exp(s - m)
                l = jnp.sum(e, axis=0, keepdims=True)
                inv = 1.0 / l
                p = e.astype(BF)
                oT = nn(qkvT[vr, 0:n], p) * inv
                dO = dOT[hr, qs].astype(F32)
                delta = jnp.sum(dO * oT, axis=0, keepdims=True)
                obT[hr, qs] = oT.astype(BF)
                dp = nn(vn[0:n, cols], dO2)
                ds = (e * ((dp - delta) * inv)).astype(BF)
                dqT = nn(qkvT[kr, 0:n], ds) * (HEAD ** -0.5)
                dkT = nt(qkvT[hr, qs], ds)
                dvT = nt((dO * inv).astype(BF), p)
                cos = cs_ref[i, :8, :]; sin = cs_ref[i, 8:, :]
                d0, d1 = dqT[:8], dqT[8:16]
                dqT = jnp.concatenate([d0 * cos + d1 * sin, d1 * cos - d0 * sin, dqT[16:]], axis=0)
                dmT[hr, qs] = dqT.astype(BF)
                for b in range(i + 1):
                    sl = slice(b * BLK, (b + 1) * BLK)
                    dk[b] = dkT[:, sl] if dk[b] is None else dk[b] + dkT[:, sl]
                    dv[b] = dvT[:, sl] if dv[b] is None else dv[b] + dvT[:, sl]
            for b in range(nblk):
                sl = slice(b * BLK, (b + 1) * BLK)
                cos = cs_ref[b, :8, :]; sin = cs_ref[b, 8:, :]
                d0, d1 = dk[b][:8], dk[b][8:16]
                dmT[kr, sl] = jnp.concatenate([d0 * cos + d1 * sin, d1 * cos - d0 * sin, dk[b][16:]], axis=0).astype(BF)
                dmT[vr, sl] = dv[b].astype(BF)

        dm = jnp.concatenate([dmT[pl.ds(r0, 128), :], dmT[pl.ds(W + r0, 128), :], dmT[pl.ds(2 * W + r0, 128), :]], axis=0)
        da_ref[hp, :384, :] = nt(dm, xaT[...]).astype(BF)
        da_ref[hp, 384:, :] = nn(obT[pl.ds(r0, 128), :], g_ref[...]).astype(BF)

    small_ref[...] = jnp.zeros_like(small_ref)
    @pl.loop(0, nblk)
    def _(b):
        rows = pl.ds(pl.multiple_of(b * BLK, BLK), BLK)
        ob = obT[:, rows].T
        attn_ref[rows, :] = nn(ob, wd_ref[...]).astype(BF)
        dxa = nn(wqkv_ref[...], dmT[:, rows]).T
        xhat, rstd = norm_parts(x_ref[rows, :].astype(F32))
        small_ref[0:1, :] += jnp.sum(dxa * xhat, axis=0, keepdims=True)
        small_ref[1:2, :] += jnp.sum(dxa, axis=0, keepdims=True)
        small_ref[2:3, :] += jnp.sum(g_ref[rows, :].astype(F32), axis=0, keepdims=True)
        dn = dxa * gain
        ga = rstd * (dn - jnp.mean(dn, axis=-1, keepdims=True) - xhat * jnp.mean(dn * xhat, axis=-1, keepdims=True))
        ga_ref[rows, :] = ga.astype(BF)
    @pl.loop(0, 9)
    def _(j):
        c = pl.ds(pl.multiple_of(j * 256, 256), 256)
        dbq_ref[:, c] = nt(jnp.ones((8, T), BF), dmT[c, :])


def attn_call(x, g, cs, gain, shift, wqkv, bqkv, wd):
    T, W = x.shape
    assert T // cs.shape[0] == BLK
    vm = pl.BlockSpec(memory_space=pltpu.VMEM)
    S = jax.ShapeDtypeStruct
    return pl.pallas_call(
        attn_kernel,
        out_shape=(S((T, W), BF), S((T, W), BF), S((HEADS // 2, 512, W), BF), S((8, W), F32), S((8, 3 * W), F32)),
        in_specs=[vm] * 8, out_specs=(vm,) * 5,
        scratch_shapes=[pltpu.VMEM((3 * W, W), BF), pltpu.VMEM((W, T), BF), pltpu.VMEM((3 * W, T), BF),
                        pltpu.VMEM((T, W), BF), pltpu.VMEM((T, W), BF), pltpu.VMEM((W, T), BF),
                        pltpu.VMEM((W, T), BF), pltpu.VMEM((3 * W, T), BF)],
        compiler_params=pltpu.CompilerParams(vmem_limit_bytes=60 << 20),
    )(x, g, cs, gain.reshape(1, W), shift.reshape(1, W), wqkv, bqkv.reshape(3 * W, 1), wd)


MESH = pl.DeviceIdType.MESH


class Place:
    def __init__(self, sizes):
        self.seq_n, self.dp_n = sizes
        self.seq = lax.axis_index("seq")
        self.dp = lax.axis_index("dp")
        self.core = [("dp", 1)]
        self.seq_bits = [("seq", 1 << b) for b in range(self.seq_n.bit_length() - 1)]
        self.dp_bits = [("dp", 1 << b) for b in range(1, self.dp_n.bit_length() - 1)]

    def mine(self, bit):
        at = self.seq if bit[0] == "seq" else self.dp
        return lax.rem(at // bit[1], 2)

    def partner(self, bit):
        step = bit[1] * (1 - 2 * self.mine(bit))
        if bit[0] == "seq":
            return (self.seq + step, self.dp)
        return (self.seq, self.dp + step)

    def peer(self, k):
        at = self.seq
        for b in range(self.seq_n.bit_length() - 1):
            if k >> b & 1:
                at = at + (1 << b) * (1 - 2 * self.mine(("seq", 1 << b)))
        return at

    def enter(self):
        targets = [(self.peer(k), self.dp) for k in range(1, self.seq_n)]
        targets += [self.partner(bit) for bit in self.core + self.dp_bits]
        bar = pltpu.get_barrier_semaphore()
        for t in targets:
            pl.semaphore_signal(bar, inc=1, device_id=t, device_id_type=MESH)
        pl.semaphore_wait(bar, len(targets))


class Halving:
    def __init__(self, place, rows, bits, unit=16):
        self.place, self.rows, self.bits = place, rows, bits
        self.plan = []
        lo, n, off = 0, rows, 0
        for bit in bits:
            halve = n % (2 * unit) == 0
            part = n // 2 if halve else n
            keep = lo + place.mine(bit) * part if halve else lo
            give = lo + (1 - place.mine(bit)) * part if halve else lo
            self.plan.append((bit, halve, part, keep, give, off))
            lo, n, off = keep, part, off + part
        self.lo, self.n, self.land_rows = lo, n, off

    @staticmethod
    def land(rows, count, unit=16):
        n, off = rows, 0
        for _ in range(count):
            n = n // 2 if n % (2 * unit) == 0 else n
            off += n
        return off

    def copy(self, i, buf, land, send, recv):
        bit, _, part, _, give, off = self.plan[i]
        return pltpu.make_async_remote_copy(
            buf.at[pl.ds(pl.multiple_of(give, 16), part)], land.at[pl.ds(off, part)], send, recv,
            device_id=self.place.partner(bit), device_id_type=MESH)

    def add(self, i, buf, land):
        _, _, part, keep, _, off = self.plan[i]
        rows = pl.ds(pl.multiple_of(keep, 16), part)
        buf[rows] = (buf[rows].astype(F32) + land[pl.ds(off, part)].astype(F32)).astype(buf.dtype)

    def spread(self, i, buf, send, recv):
        bit, halve, part, keep, _, _ = self.plan[i]
        if not halve:
            return None
        at = (slice(None),) * (len(buf.shape) - 2) + (pl.ds(pl.multiple_of(keep, 16), part),)
        return pltpu.make_async_remote_copy(
            buf.at[at], buf.at[at], send, recv, device_id=self.place.partner(bit), device_id_type=MESH)


def cdf_pdf(h):
    t = 1.0 / (1.0 + (0.3275911 * 0.5 ** 0.5) * jnp.abs(h))
    ez = jnp.exp(-0.5 * h * h)
    poly = t * (0.5 * 0.254829592 + t * (0.5 * -0.284496736 + t * (
        0.5 * 1.421413741 + t * (0.5 * -1.453152027 + t * (0.5 * 1.061405429)))))
    tail = poly * ez
    return jnp.where(h >= 0, 1.0 - tail, tail), ez * 0.3989422804014327


def mlp_kernel(sizes, x_ref, g_ref, cs_ref, gain_ref, shift_ref, wu_ref, bu_ref, wd_ref, bias_ref,
               y_ref, gm_ref, xs_ref, gs_ref, css_ref, du_ref, dd_ref, small_ref, dbu_ref,
               xm, xmT, dxm, land_u, land_d, a_s, dh_s, su, ru, sd, rd, sa, ra, sl):
    place = Place(sizes)
    ns = place.seq_n
    L, W = x_ref.shape[1:]
    T = ns * L
    n_chunk, _, C = du_ref.shape
    hu = Halving(place, W, place.core + place.dp_bits + place.seq_bits)
    hd = Halving(place, C, place.core + place.seq_bits + place.dp_bits)
    steps = len(hu.bits)
    place.enter()

    moves = []
    me = pl.ds(pl.multiple_of(place.seq * L, L), L)
    for a, (src, dst) in enumerate(((x_ref, xs_ref), (g_ref, gs_ref), (cs_ref, css_ref))):
        for k in range(ns - 1, 0, -1):
            to = place.peer(k)
            moves.append(pltpu.make_async_remote_copy(
                src.at[to], dst.at[place.seq] if a == 2 else dst.at[me], sa.at[a, k], ra.at[a, k],
                device_id=(to, place.dp), device_id_type=MESH))
        moves.append(pltpu.make_async_copy(
            src.at[place.seq], dst.at[place.seq] if a == 2 else dst.at[me], sl.at[a]))
    for m in moves:
        m.start()

    gain = gain_ref[...]
    shift = shift_ref[...]
    for b in range(ns):
        rows = slice(b * L, (b + 1) * L)
        x = x_ref[b].astype(F32)
        xhat, _ = norm_parts(x)
        v = (xhat * gain + shift).astype(BF)
        xm[rows, :] = v
        xmT[:, rows] = v.T
        y_ref[rows, :] = x + bias_ref[...]
    dxm[...] = jnp.zeros_like(dxm)
    small_ref[...] = jnp.zeros_like(small_ref)

    def finish(p, s):
        for h, buf, land, send, recv in ((hu, du_ref, land_u, su, ru), (hd, dd_ref, land_d, sd, rd)):
            h.copy(s, buf.at[p], land.at[p], send.at[p, s], recv.at[p, s]).wait()
            h.add(s, buf.at[p], land.at[p])

    def begin(p, s):
        for h, buf, land, send, recv in ((hu, du_ref, land_u, su, ru), (hd, dd_ref, land_d, sd, rd)):
            h.copy(s, buf.at[p], land.at[p], send.at[p, s], recv.at[p, s]).start()

    @pl.loop(0, n_chunk + steps)
    def _(j):
        c = pl.ds(pl.multiple_of(jnp.minimum(j, n_chunk - 1) * C, C), C)

        @pl.when(j < n_chunk)
        def _():
            wu = wu_ref[:, c]
            wd = wd_ref[c, :]
            bu = bu_ref[:, c]
            dbu = jnp.zeros((1, C), F32)
            for b in range(ns):
                rows = slice(b * L, (b + 1) * L)
                h = nn(xm[rows, :], wu) + bu
                cdf, pdf = cdf_pdf(h)
                a_s[rows, :] = (h * cdf).astype(BF)
                dh = (nt(g_ref[b], wd) * (cdf + h * pdf)).astype(BF)
                dh_s[rows, :] = dh
                dbu += jnp.sum(dh.astype(F32), axis=0, keepdims=True)
            dbu_ref[:, c] = dbu

        for s in range(1, steps + 1):
            p = j - s

            @pl.when((p >= 0) & (p < n_chunk))
            def _():
                finish(p, s - 1)
                if s < steps:
                    begin(p, s)

        @pl.when(j < n_chunk)
        def _():
            wu = wu_ref[:, c]
            wd = wd_ref[c, :]
            dh = dh_s[...]
            a = a_s[...]
            du_ref[j] = nn(xmT[...], dh).astype(BF)
            dd_ref[j] = tn(a, g_ref[...].reshape(T, W)).astype(BF)
            begin(j, 0)
            y_ref[...] += nn(a, wd)
            dxm[...] += nt(dh, wu)

        @pl.when((j >= n_chunk) & (j < n_chunk + ns))
        def _():
            b = j - n_chunk
            rows = pl.ds(pl.multiple_of(b * L, L), L)
            xhat, rstd = norm_parts(x_ref[b].astype(F32))
            dxa = dxm[rows, :]
            gf = g_ref[b].astype(F32)
            small_ref[0:1, :] += jnp.sum(dxa * xhat, axis=0, keepdims=True)
            small_ref[1:2, :] += jnp.sum(dxa, axis=0, keepdims=True)
            small_ref[2:3, :] += jnp.sum(gf, axis=0, keepdims=True)
            dn = dxa * gain
            gm_ref[rows, :] = gf + rstd * (dn - jnp.mean(dn, axis=-1, keepdims=True)
                                           - xhat * jnp.mean(dn * xhat, axis=-1, keepdims=True))

    for m in moves:
        m.wait()


def mlp_call(sizes, x, g, cs, gain, shift, wu, bu, wd, bias):
    ns, L, W = x.shape
    T = ns * L
    FF = wu.shape[1]
    C = 256
    n = FF // C
    steps = sum(s.bit_length() - 1 for s in sizes)
    vm = pl.BlockSpec(memory_space=pltpu.VMEM)
    hbm = pl.BlockSpec(memory_space=pl.ANY)
    S = jax.ShapeDtypeStruct
    dma = pltpu.SemaphoreType.DMA
    return pl.pallas_call(
        functools.partial(mlp_kernel, sizes),
        out_shape=(S((T, W), F32), S((T, W), F32), S((T, W), BF), S((T, W), BF), S(cs.shape, F32),
                   S((n, W, C), BF), S((n, C, W), BF), S((8, W), F32), S((1, FF), F32)),
        in_specs=[vm] * 9, out_specs=(vm, vm, hbm, hbm, hbm, vm, vm, vm, vm),
        scratch_shapes=[pltpu.VMEM((T, W), BF), pltpu.VMEM((W, T), BF), pltpu.VMEM((T, W), F32),
                        pltpu.VMEM((n, Halving.land(W, steps), C), BF),
                        pltpu.VMEM((n, Halving.land(C, steps), W), BF),
                        pltpu.VMEM((T, C), BF), pltpu.VMEM((T, C), BF),
                        dma((n, steps)), dma((n, steps)), dma((n, steps)), dma((n, steps)),
                        dma((3, ns)), dma((3, ns)), dma((3,))],
        compiler_params=pltpu.CompilerParams(vmem_limit_bytes=60 << 20, collective_id=0, has_side_effects=True),
    )(x, g, cs, gain.reshape(1, W), shift.reshape(1, W), wu, bu.reshape(1, FF), wd, bias.reshape(1, W))


def tail_kernel(sizes, groups, du_in, dd_in, da_in, small_in, attn_ref, ga_ref,
                du_ref, dd_ref, da_ref, small_ref, attn_out, ga_out,
                buf, land_x, land_y, land_s, *sems):
    s_ag, r_ag, s_x, r_x, s_y, r_y, s_s, r_s, sa, ra, sl = sems
    place = Place(sizes)
    ns = place.seq_n
    L = attn_ref.shape[0] // ns
    n_u, W, C = du_in.shape
    hu = Halving(place, W, place.core + place.dp_bits + place.seq_bits)
    hd = Halving(place, C, place.core + place.seq_bits + place.dp_bits)
    n_a, R, _ = da_in.shape
    hx = Halving(place, R // 2, place.core + place.seq_bits + place.dp_bits)
    hy = Halving(place, R // 2, place.core + place.seq_bits[::-1] + place.dp_bits)
    steps = len(hu.bits)
    place.enter()
    moves = []
    me = pl.ds(pl.multiple_of(place.seq * L, L), L)
    for a, (src, dst) in enumerate(((attn_ref, attn_out), (ga_ref, ga_out))):
        for k in range(ns - 1, 0, -1):
            to = place.peer(k)
            moves.append(pltpu.make_async_remote_copy(
                src.at[pl.ds(pl.multiple_of(to * L, L), L)], dst.at[place.seq], sa.at[a, k], ra.at[a, k],
                device_id=(to, place.dp), device_id_type=MESH))
        moves.append(pltpu.make_async_copy(src.at[me], dst.at[place.seq], sl.at[a]))
    loads = [pltpu.make_async_copy(da_in, buf, sl.at[2])]
    for n, (h, src, dst) in enumerate(((hu, du_in, du_ref), (hd, dd_in, dd_ref))):
        at = (slice(None), pl.ds(pl.multiple_of(h.lo, 16), h.n))
        loads.append(pltpu.make_async_copy(src.at[at], dst.at[at], sl.at[3 + n]))
    small_ref[...] = small_in[...]
    for m in loads:
        m.start()
    for m in loads:
        m.wait()
    half = R // 2
    size = n_u // groups
    pieces = []

    def gather(h, buf_of, at):
        ops = []
        for i in reversed(range(steps)):
            c = h.spread(i, buf_of, s_ag.at[at, i], r_ag.at[at, i])
            if c is not None:
                ops.append((c, None))
        return ops

    seqs = []
    for p in range(n_a):
        for h, lo, land, send, recv in ((hx, 0, land_x, s_x, r_x), (hy, half, land_y, s_y, r_y)):
            ops = []
            b = buf.at[p, pl.ds(lo, half)]
            for i in range(steps):
                c = h.copy(i, b, land.at[p], send.at[p, i], recv.at[p, i])
                ops.append((c, functools.partial(h.add, i, b, land.at[p])))
            seqs.append(ops)
    small_ops = []
    for i, bit in enumerate(hx.bits):
        c = pltpu.make_async_remote_copy(small_ref, land_s.at[i], s_s.at[i], r_s.at[i],
                                         device_id=place.partner(bit), device_id_type=MESH)

        def add(i=i):
            small_ref[...] += land_s[i]
        small_ops.append((c, add))
    seqs.append(small_ops)
    for gidx in range(groups):
        g = pl.ds(gidx * size, size)
        seqs.append(gather(hu, du_ref.at[g], 2 * gidx))
        seqs.append(gather(hd, dd_ref.at[g], 2 * gidx + 1))
    for ops in seqs:
        ops[0][0].start()
    for i in range(max(len(o) for o in seqs)):
        for ops in seqs:
            if i < len(ops):
                ops[i][0].wait()
                if ops[i][1] is not None:
                    ops[i][1]()
                if i + 1 < len(ops):
                    ops[i + 1][0].start()
    for m in moves:
        m.start()
    outs = []
    for n, (h, lo) in enumerate(((hx, 0), (hy, half))):
        at = (slice(None), pl.ds(pl.multiple_of(lo + h.lo, 16), h.n))
        outs.append(pltpu.make_async_copy(buf.at[at], da_ref.at[at], sl.at[3 + n]))
    for m in outs:
        m.start()
    for m in outs:
        m.wait()
    seqs = [gather(hx, da_ref.at[:, pl.ds(0, half)], 2 * groups), gather(hy, da_ref.at[:, pl.ds(half, half)], 2 * groups + 1)]
    for ops in seqs:
        ops[0][0].start()
    for i in range(max(len(o) for o in seqs)):
        for ops in seqs:
            if i < len(ops):
                ops[i][0].wait()
                if i + 1 < len(ops):
                    ops[i + 1][0].start()
    for m in moves:
        m.wait()


def tail_call(sizes, du, dd, da, small, attn, ga):
    ns = sizes[0]
    T, W = attn.shape
    L = T // ns
    n_a, R, _ = da.shape
    groups = 3
    steps = sum(s.bit_length() - 1 for s in sizes)
    vm = pl.BlockSpec(memory_space=pltpu.VMEM)
    hbm = pl.BlockSpec(memory_space=pl.ANY)
    S = jax.ShapeDtypeStruct
    dma = pltpu.SemaphoreType.DMA
    nl = Halving.land(R // 2, steps)
    return pl.pallas_call(
        functools.partial(tail_kernel, sizes, groups),
        out_shape=(S(du.shape, BF), S(dd.shape, BF), S(da.shape, BF), S(small.shape, F32),
                   S((ns, L, W), BF), S((ns, L, W), BF)),
        in_specs=[hbm, hbm, hbm, vm, vm, vm], out_specs=(hbm, hbm, hbm, vm, hbm, hbm),
        scratch_shapes=[pltpu.VMEM(da.shape, BF), pltpu.VMEM((n_a, nl, W), BF), pltpu.VMEM((n_a, nl, W), BF),
                        pltpu.VMEM((steps,) + small.shape, F32),
                        dma((2 * groups + 2, steps)), dma((2 * groups + 2, steps)),
                        dma((n_a, steps)), dma((n_a, steps)), dma((n_a, steps)), dma((n_a, steps)),
                        dma((steps,)), dma((steps,)), dma((2, ns)), dma((2, ns)), dma((5,))],
        compiler_params=pltpu.CompilerParams(vmem_limit_bytes=60 << 20, collective_id=1, has_side_effects=True),
    )(du, dd, da, small, attn, ga)


def on_device(hidden_in, positions, attn_gain, attn_shift, qkv_weight, qkv_bias, dense_weight, dense_bias,
              mlp_gain, mlp_shift, up_weight, up_bias, down_weight, down_bias, out_grad):
    sentences, local_len, width = hidden_in.shape
    sizes = (lax.axis_size("seq"), lax.axis_size("dp"))
    assert sentences == sizes[0]
    freqs = jnp.power(10000.0, -2.0 * jnp.arange(ROT // 2, dtype=F32) / ROT)
    angles = freqs[:, None] * positions.astype(F32)[:, None, :]
    cs = jnp.concatenate([jnp.cos(angles), jnp.sin(angles)], axis=1)
    y, gm, x_s, g_s, cs_s, du, dd, small_m, dbu = mlp_call(
        sizes, hidden_in, out_grad, cs, mlp_gain, mlp_shift, up_weight, up_bias, down_weight, dense_bias + down_bias)
    attn, ga, da, small_a, dbq = attn_call(
        x_s, g_s, cs_s, attn_gain, attn_shift, qkv_weight, qkv_bias, dense_weight)
    small = jnp.concatenate([small_a[0], small_a[1], small_m[0], small_m[1], small_m[2], dbq[0], dbu[0]]).reshape(-1, 128)
    du, dd, da, small, attn, ga = tail_call(sizes, du, dd, da, small, attn, ga)
    layer_out = (y.reshape(hidden_in.shape) + attn.astype(F32)).astype(BF)
    input_grad = (gm.reshape(hidden_in.shape) + ga.astype(F32)).astype(BF)
    s = small.reshape(-1)
    W = width
    n_u, _, C = du.shape
    dwu = jnp.transpose(du, (1, 0, 2)).reshape(W, n_u * C).astype(F32)
    dwd = dd.reshape(-1, W).astype(F32)
    da = da.reshape(-1, 4, 128, W)
    dwqkv = jnp.transpose(da[:, :3], (3, 1, 0, 2)).reshape(W, 3 * W).astype(F32)
    ddw = da[:, 3].reshape(W, W).astype(F32)
    db = s[4 * W:5 * W]
    return (layer_out, input_grad, s[:W], s[W:2 * W], dwqkv, s[5 * W:8 * W], ddw, db, s[2 * W:3 * W], s[3 * W:4 * W],
            dwu, s[8 * W:], dwd, db)


def solution(mesh):
    act, rep = P("dp", "seq", None), P()
    return jax.shard_map(
        on_device, mesh=mesh,
        in_specs=(act, P("dp", "seq")) + (rep,) * 12 + (act,),
        out_specs=(act, act) + (rep,) * 12,
        check_vma=False)
```

```python
import functools
import jax, jax.numpy as jnp
from jax import lax
from jax.experimental import pallas as pl
from jax.experimental.pallas import tpu as pltpu
from jax.sharding import PartitionSpec as P

HEADS, HEAD, ROT = 12, 64, 16
EPSILON = 1e-5
BF, F32 = jnp.bfloat16, jnp.float32
BLK = 256

def nn(a, b): return lax.dot_general(a, b, (((1,), (0,)), ((), ())), preferred_element_type=F32)
def nt(a, b): return lax.dot_general(a, b, (((1,), (1,)), ((), ())), preferred_element_type=F32)
def tn(a, b): return lax.dot_general(a, b, (((0,), (0,)), ((), ())), preferred_element_type=F32)

def norm_parts(x):
    mean = jnp.mean(x, axis=-1, keepdims=True)
    c = x - mean
    rstd = lax.rsqrt(jnp.mean(c * c, axis=-1, keepdims=True) + EPSILON)
    return c * rstd, rstd

GROUPS = 3


def attn_kernel(sizes, x_ref, g_ref, cs_ref, gain_ref, shift_ref, wqkv_ref, bqkv_ref, wd_ref, du_in, dd_in,
                attn_ref, ga_ref, da_out, du_ref, dd_ref, small_ref, dbq_ref,
                wT, xaT, qkvT, kn, vn, dOT, obT, dmT, da_ref, land_x, land_y,
                s_x, r_x, s_y, r_y, s_u, r_u, s_d, r_d, sl):
    T, W = x_ref.shape
    nblk = T // BLK
    place = Place(sizes)
    n_u, _, C = du_ref.shape
    hu = Halving(place, W, place.core + place.dp_bits + place.seq_bits)
    hd = Halving(place, C, place.core + place.seq_bits + place.dp_bits)
    pairs, R, _ = da_ref.shape
    hx = Halving(place, R // 2, place.core + place.seq_bits + place.dp_bits)
    hy = Halving(place, R // 2, place.core + place.seq_bits[::-1] + place.dp_bits)
    steps = len(hx.bits)
    place.enter()
    loads = []
    for n, (h, src, dst) in enumerate(((hu, du_in, du_ref), (hd, dd_in, dd_ref))):
        loads.append(pltpu.make_async_copy(src, dst.at[:, pl.ds(pl.multiple_of(h.lo, 16), h.n)], sl.at[n]))
    for m in loads:
        m.start()

    size = n_u // GROUPS
    plan = {}
    for gi in range(GROUPS):
        grp = pl.ds(gi * size, size)
        for h, buf, send, recv in ((hu, du_ref, s_u, r_u), (hd, dd_ref, s_d, r_d)):
            ops = h.chain(buf.at[grp], send.at[gi], recv.at[gi])
            at = gi * 4
            for k in range(len(ops) + 1):
                plan.setdefault(at, []).append(functools.partial(advance, ops, k))
                if k < len(ops):
                    at += 2 if k in (1, 2) else 1
    last = max(plan)
    assert last < nblk + 2 * pairs

    def tick(slot, lo, hi):
        for at in range(lo, hi + 1):
            if at in plan:
                @pl.when(slot == at)
                def _():
                    for act in plan[at]:
                        act()

    def each(p):
        return ((hx, da_ref.at[p, pl.ds(0, R // 2)], land_x.at[p], s_x.at[p], r_x.at[p]),
                (hy, da_ref.at[p, pl.ds(R // 2, R // 2)], land_y.at[p], s_y.at[p], r_y.at[p]))

    def halve(p, s):
        @pl.when((p >= 0) & (p < pairs))
        def _():
            for h, buf, land, send, recv in each(p):
                if s > 0:
                    h.copy(s - 1, buf, land, send.at[s - 1], recv.at[s - 1]).wait()
                    h.add(s - 1, buf, land)
                if s < steps:
                    h.copy(s, buf, land, send.at[s], recv.at[s]).start()

    def halves(i, second):
        for s in range(1, steps + 1):
            if (s % 2 == 0) == second:
                halve(i - (s + 1) // 2, s)

    gain = gain_ref[...]; shift = shift_ref[...]
    for j in range(9):
        wT[j*256:(j+1)*256, :] = wqkv_ref[:, j*256:(j+1)*256].T

    @pl.loop(0, nblk)
    def _(b):
        rows = pl.ds(pl.multiple_of(b * BLK, BLK), BLK)
        x = x_ref[rows, :].astype(F32)
        xhat, _ = norm_parts(x)
        xa = (xhat * gain + shift).astype(BF)
        xaT[:, rows] = xa.T
        cos = cs_ref[b, :8, :]; sin = cs_ref[b, 8:, :]
        for j in range(9):
            m = nt(wT[j*256:(j+1)*256, :], xa) + bqkv_ref[j*256:(j+1)*256, :]
            if j < 6:
                parts = []
                for h in range(4):
                    u = m[h*64:(h+1)*64]
                    u0, u1 = u[:8], u[8:16]
                    parts += [u0 * cos - u1 * sin, u1 * cos + u0 * sin, u[16:]]
                m = jnp.concatenate(parts, axis=0)
                if j < 3: m = m * (HEAD ** -0.5)
            mb = m.astype(BF)
            qkvT[j*256:(j+1)*256, rows] = mb
            if 3 <= j < 6: kn[rows, (j-3)*256:(j-2)*256] = mb.T
            if j >= 6: vn[rows, (j-6)*256:(j-5)*256] = mb.T
        g = g_ref[rows, :]
        for j in range(3):
            dOT[j*256:(j+1)*256, rows] = nt(wd_ref[j*256:(j+1)*256, :], g).astype(BF)

        @pl.when(b == 0)
        def _():
            for m in loads:
                m.wait()
        tick(b, 0, nblk - 1)

    sub = lax.broadcasted_iota(jnp.int32, (BLK, BLK), 0)
    lane = lax.broadcasted_iota(jnp.int32, (BLK, BLK), 1)
    keep = sub <= lane
    rowid = lax.broadcasted_iota(jnp.int32, (128, 1), 0)

    @pl.loop(0, HEADS // 2)
    def _(hp):
        r0 = pl.multiple_of(hp * 128, 128)
        cols = pl.ds(r0, 128)
        for hh in range(2):
            hr = pl.ds(pl.multiple_of(r0 + hh * 64, 64), 64)
            kr = pl.ds(pl.multiple_of(W + r0 + hh * 64, 64), 64)
            vr = pl.ds(pl.multiple_of(2 * W + r0 + hh * 64, 64), 64)
            msk = (rowid // 64 == hh)
            dk = [None] * nblk; dv = [None] * nblk
            for i in range(nblk):
                n = (i + 1) * BLK
                qs = slice(i * BLK, (i + 1) * BLK)
                qT2 = jnp.where(msk, qkvT[pl.ds(r0, 128), qs], 0).astype(BF)
                dO2 = jnp.where(msk, dOT[pl.ds(r0, 128), qs], 0).astype(BF)
                s = nn(kn[0:n, cols], qT2)
                d = jnp.where(keep, s[n-BLK:], -1e30)
                if n > BLK: s = jnp.concatenate([s[:n-BLK], d], axis=0)
                else: s = d
                m = jnp.max(s, axis=0, keepdims=True)
                e = jnp.exp(s - m)
                l = jnp.sum(e, axis=0, keepdims=True)
                inv = 1.0 / l
                p = e.astype(BF)
                oT = nn(qkvT[vr, 0:n], p) * inv
                dO = dOT[hr, qs].astype(F32)
                delta = jnp.sum(dO * oT, axis=0, keepdims=True)
                obT[hr, qs] = oT.astype(BF)
                dp = nn(vn[0:n, cols], dO2)
                ds = (e * ((dp - delta) * inv)).astype(BF)
                dqT = nn(qkvT[kr, 0:n], ds) * (HEAD ** -0.5)
                dkT = nt(qkvT[hr, qs], ds)
                dvT = nt((dO * inv).astype(BF), p)
                cos = cs_ref[i, :8, :]; sin = cs_ref[i, 8:, :]
                d0, d1 = dqT[:8], dqT[8:16]
                dqT = jnp.concatenate([d0 * cos + d1 * sin, d1 * cos - d0 * sin, dqT[16:]], axis=0)
                dmT[hr, qs] = dqT.astype(BF)
                for b in range(i + 1):
                    sl = slice(b * BLK, (b + 1) * BLK)
                    dk[b] = dkT[:, sl] if dk[b] is None else dk[b] + dkT[:, sl]
                    dv[b] = dvT[:, sl] if dv[b] is None else dv[b] + dvT[:, sl]
            for b in range(nblk):
                sl = slice(b * BLK, (b + 1) * BLK)
                cos = cs_ref[b, :8, :]; sin = cs_ref[b, 8:, :]
                d0, d1 = dk[b][:8], dk[b][8:16]
                dmT[kr, sl] = jnp.concatenate([d0 * cos + d1 * sin, d1 * cos - d0 * sin, dk[b][16:]], axis=0).astype(BF)
                dmT[vr, sl] = dv[b].astype(BF)
            if hh == 0:
                tick(nblk + 2 * hp, nblk, last)
                halves(hp, False)

        dm = jnp.concatenate([dmT[pl.ds(r0, 128), :], dmT[pl.ds(W + r0, 128), :], dmT[pl.ds(2 * W + r0, 128), :]], axis=0)
        da_ref[hp, :384, :] = nt(dm, xaT[...]).astype(BF)
        da_ref[hp, 384:, :] = nn(obT[pl.ds(r0, 128), :], g_ref[...]).astype(BF)
        tick(nblk + 2 * hp + 1, nblk, last)
        halves(hp, True)
        halve(hp, 0)

    small_ref[...] = jnp.zeros_like(small_ref)
    @pl.loop(0, nblk)
    def _(b):
        rows = pl.ds(pl.multiple_of(b * BLK, BLK), BLK)
        ob = obT[:, rows].T
        attn_ref[rows, :] = nn(ob, wd_ref[...]).astype(BF)
        dxa = nn(wqkv_ref[...], dmT[:, rows]).T
        xhat, rstd = norm_parts(x_ref[rows, :].astype(F32))
        small_ref[0:1, :] += jnp.sum(dxa * xhat, axis=0, keepdims=True)
        small_ref[1:2, :] += jnp.sum(dxa, axis=0, keepdims=True)
        small_ref[2:3, :] += jnp.sum(g_ref[rows, :].astype(F32), axis=0, keepdims=True)
        dn = dxa * gain
        ga = rstd * (dn - jnp.mean(dn, axis=-1, keepdims=True) - xhat * jnp.mean(dn * xhat, axis=-1, keepdims=True))
        ga_ref[rows, :] = ga.astype(BF)

        @pl.when(lax.rem(b, 2) == 0)
        def _():
            halves(pairs + b // 2, False)

        @pl.when(lax.rem(b, 2) == 1)
        def _():
            halves(pairs + b // 2, True)
    @pl.loop(0, 9)
    def _(j):
        c = pl.ds(pl.multiple_of(j * 256, 256), 256)
        dbq_ref[:, c] = nt(jnp.ones((8, T), BF), dmT[c, :])
    for i in range(nblk, 2 * ((steps + 1) // 2) + 1):
        halves(pairs + i // 2, i % 2 == 1)
    outs = []
    for n, (h, lo) in enumerate(((hx, 0), (hy, R // 2))):
        outs.append(pltpu.make_async_copy(da_ref.at[:, pl.ds(pl.multiple_of(lo + h.lo, 16), h.n)], da_out.at[:, n], sl.at[n]))
    for m in outs:
        m.start()
    for m in outs:
        m.wait()


def attn_call(sizes, x, g, cs, gain, shift, wqkv, bqkv, wd, du, dd):
    T, W = x.shape
    assert T // cs.shape[0] == BLK
    n, C = du.shape[0], du.shape[2]
    assert dd.shape[0] == n
    pairs, R = HEADS // 2, 512
    steps = sum(s.bit_length() - 1 for s in sizes)
    vm = pl.BlockSpec(memory_space=pltpu.VMEM)
    hbm = pl.BlockSpec(memory_space=pl.ANY)
    S = jax.ShapeDtypeStruct
    dma = pltpu.SemaphoreType.DMA
    land = Halving.land(R // 2, steps)
    return pl.pallas_call(
        functools.partial(attn_kernel, sizes),
        out_shape=(S((T, W), BF), S((T, W), BF), S((pairs, 2, Halving.left(R // 2, steps), W), BF),
                   S((n, W, C), BF), S((n, C, W), BF), S((8, W), F32), S((8, 3 * W), F32)),
        in_specs=[vm] * 8 + [hbm] * 2, out_specs=(vm, vm, hbm, hbm, hbm, vm, vm),
        scratch_shapes=[pltpu.VMEM((3 * W, W), BF), pltpu.VMEM((W, T), BF), pltpu.VMEM((3 * W, T), BF),
                        pltpu.VMEM((T, W), BF), pltpu.VMEM((T, W), BF), pltpu.VMEM((W, T), BF),
                        pltpu.VMEM((W, T), BF), pltpu.VMEM((3 * W, T), BF),
                        pltpu.VMEM((pairs, R, W), BF), pltpu.VMEM((pairs, land, W), BF), pltpu.VMEM((pairs, land, W), BF),
                        dma((pairs, steps)), dma((pairs, steps)), dma((pairs, steps)), dma((pairs, steps)),
                        dma((GROUPS, steps)), dma((GROUPS, steps)), dma((GROUPS, steps)), dma((GROUPS, steps)), dma((2,))],
        compiler_params=pltpu.CompilerParams(vmem_limit_bytes=60 << 20, collective_id=1, has_side_effects=True),
    )(x, g, cs, gain.reshape(1, W), shift.reshape(1, W), wqkv, bqkv.reshape(3 * W, 1), wd, du, dd)


MESH = pl.DeviceIdType.MESH


class Place:
    def __init__(self, sizes):
        self.seq_n, self.dp_n = sizes
        self.seq = lax.axis_index("seq")
        self.dp = lax.axis_index("dp")
        self.core = [("dp", 1)]
        self.seq_bits = [("seq", 1 << b) for b in range(self.seq_n.bit_length() - 1)]
        self.dp_bits = [("dp", 1 << b) for b in range(1, self.dp_n.bit_length() - 1)]

    def mine(self, bit):
        at = self.seq if bit[0] == "seq" else self.dp
        return lax.rem(at // bit[1], 2)

    def partner(self, bit):
        step = bit[1] * (1 - 2 * self.mine(bit))
        if bit[0] == "seq":
            return (self.seq + step, self.dp)
        return (self.seq, self.dp + step)

    def peer(self, k):
        at = self.seq
        for b in range(self.seq_n.bit_length() - 1):
            if k >> b & 1:
                at = at + (1 << b) * (1 - 2 * self.mine(("seq", 1 << b)))
        return at

    def enter(self):
        targets = [(self.peer(k), self.dp) for k in range(1, self.seq_n)]
        targets += [self.partner(bit) for bit in self.core + self.dp_bits]
        bar = pltpu.get_barrier_semaphore()
        for t in targets:
            pl.semaphore_signal(bar, inc=1, device_id=t, device_id_type=MESH)
        pl.semaphore_wait(bar, len(targets))


def advance(ops, k):
    if k > 0:
        ops[k - 1].wait()
    if k < len(ops):
        ops[k].start()


class Halving:
    def __init__(self, place, rows, bits, unit=16):
        self.place, self.rows, self.bits = place, rows, bits
        self.plan = []
        lo, n, off = 0, rows, 0
        for bit in bits:
            halve = n % (2 * unit) == 0
            part = n // 2 if halve else n
            keep = lo + place.mine(bit) * part if halve else lo
            give = lo + (1 - place.mine(bit)) * part if halve else lo
            self.plan.append((bit, halve, part, keep, give, off))
            lo, n, off = keep, part, off + part
        self.lo, self.n, self.land_rows = lo, n, off

    @staticmethod
    def land(rows, count, unit=16):
        n, off = rows, 0
        for _ in range(count):
            n = n // 2 if n % (2 * unit) == 0 else n
            off += n
        return off

    @staticmethod
    def left(rows, count, unit=16):
        for _ in range(count):
            rows = rows // 2 if rows % (2 * unit) == 0 else rows
        return rows

    def copy(self, i, buf, land, send, recv):
        bit, _, part, _, give, off = self.plan[i]
        return pltpu.make_async_remote_copy(
            buf.at[pl.ds(pl.multiple_of(give, 16), part)], land.at[pl.ds(off, part)], send, recv,
            device_id=self.place.partner(bit), device_id_type=MESH)

    def add(self, i, buf, land):
        _, _, part, keep, _, off = self.plan[i]
        rows = pl.ds(pl.multiple_of(keep, 16), part)
        buf[rows] = (buf[rows].astype(F32) + land[pl.ds(off, part)].astype(F32)).astype(buf.dtype)

    def spread(self, i, buf, send, recv):
        bit, halve, part, keep, _, _ = self.plan[i]
        if not halve:
            return None
        at = (slice(None),) * (len(buf.shape) - 2) + (pl.ds(pl.multiple_of(keep, 16), part),)
        return pltpu.make_async_remote_copy(
            buf.at[at], buf.at[at], send, recv, device_id=self.place.partner(bit), device_id_type=MESH)

    def chain(self, buf, send, recv):
        ops = [self.spread(i, buf, send.at[i], recv.at[i]) for i in reversed(range(len(self.bits)))]
        return [c for c in ops if c is not None]


def cdf_pdf(h):
    t = 1.0 / (1.0 + (0.3275911 * 0.5 ** 0.5) * jnp.abs(h))
    ez = jnp.exp(-0.5 * h * h)
    poly = t * (0.5 * 0.254829592 + t * (0.5 * -0.284496736 + t * (
        0.5 * 1.421413741 + t * (0.5 * -1.453152027 + t * (0.5 * 1.061405429)))))
    tail = poly * ez
    return jnp.where(h >= 0, 1.0 - tail, tail), ez * 0.3989422804014327


MOVES = 8


def mlp_kernel(sizes, x_ref, g_ref, cs_ref, gain_ref, shift_ref, wu_ref, bu_ref, wd_ref, bias_ref,
               y_ref, gm_ref, xs_ref, gs_ref, css_ref, du_out, dd_out, small_ref, dbu_ref,
               xm, xmT, dxm, du_ref, dd_ref, land_u, land_d, a_s, dh_s, su, ru, sd, rd, sa, ra, sc, rc, sl):
    place = Place(sizes)
    ns = place.seq_n
    L, W = x_ref.shape[1:]
    T = ns * L
    n_chunk, _, C = du_ref.shape
    hu = Halving(place, W, place.core + place.dp_bits + place.seq_bits)
    hd = Halving(place, C, place.core + place.seq_bits + place.dp_bits)
    steps = len(hu.bits)
    place.enter()

    part = L // MOVES

    def moves(i):
        out = []
        for a, (src, dst) in enumerate(((x_ref, xs_ref), (g_ref, gs_ref))):
            for k in range(ns - 1, 0, -1):
                to = place.peer(k)
                out.append(pltpu.make_async_remote_copy(
                    src.at[to, pl.ds(pl.multiple_of(i * part, part), part)],
                    dst.at[pl.ds(pl.multiple_of(place.seq * L + i * part, part), part)],
                    sa.at[a, k, i], ra.at[a, k, i], device_id=(to, place.dp), device_id_type=MESH))
        return out

    once = []
    me = pl.ds(pl.multiple_of(place.seq * L, L), L)
    for k in range(ns - 1, 0, -1):
        to = place.peer(k)
        once.append(pltpu.make_async_remote_copy(
            cs_ref.at[to], css_ref.at[place.seq], sc.at[k], rc.at[k], device_id=(to, place.dp), device_id_type=MESH))
    for a, (src, dst) in enumerate(((x_ref, xs_ref.at[me]), (g_ref, gs_ref.at[me]), (cs_ref, css_ref.at[place.seq]))):
        once.append(pltpu.make_async_copy(src.at[place.seq], dst, sl.at[a]))
    for m in once + moves(0):
        m.start()

    gain = gain_ref[...]
    shift = shift_ref[...]
    for b in range(ns):
        rows = slice(b * L, (b + 1) * L)
        x = x_ref[b].astype(F32)
        xhat, _ = norm_parts(x)
        v = (xhat * gain + shift).astype(BF)
        xm[rows, :] = v
        xmT[:, rows] = v.T
        y_ref[rows, :] = x + bias_ref[...]
    dxm[...] = jnp.zeros_like(dxm)
    small_ref[...] = jnp.zeros_like(small_ref)

    def finish(p, s):
        for h, buf, land, send, recv in ((hu, du_ref, land_u, su, ru), (hd, dd_ref, land_d, sd, rd)):
            h.copy(s, buf.at[p], land.at[p], send.at[p, s], recv.at[p, s]).wait()
            h.add(s, buf.at[p], land.at[p])

    def begin(p, s):
        for h, buf, land, send, recv in ((hu, du_ref, land_u, su, ru), (hd, dd_ref, land_d, sd, rd)):
            h.copy(s, buf.at[p], land.at[p], send.at[p, s], recv.at[p, s]).start()

    @pl.loop(0, n_chunk + steps)
    def _(j):
        c = pl.ds(pl.multiple_of(jnp.minimum(j, n_chunk - 1) * C, C), C)

        @pl.when((j > 0) & (j < MOVES))
        def _():
            for m in moves(j):
                m.start()

        @pl.when(j < n_chunk)
        def _():
            wu = wu_ref[:, c]
            wd = wd_ref[c, :]
            bu = bu_ref[:, c]
            dbu = jnp.zeros((1, C), F32)
            for b in range(ns):
                rows = slice(b * L, (b + 1) * L)
                h = nn(xm[rows, :], wu) + bu
                cdf, pdf = cdf_pdf(h)
                a_s[rows, :] = (h * cdf).astype(BF)
                dh = (nt(g_ref[b], wd) * (cdf + h * pdf)).astype(BF)
                dh_s[rows, :] = dh
                dbu += jnp.sum(dh.astype(F32), axis=0, keepdims=True)
            dbu_ref[:, c] = dbu

        for s in range(1, steps + 1):
            p = j - s

            @pl.when((p >= 0) & (p < n_chunk))
            def _():
                finish(p, s - 1)
                if s < steps:
                    begin(p, s)

        @pl.when(j < n_chunk)
        def _():
            wu = wu_ref[:, c]
            wd = wd_ref[c, :]
            dh = dh_s[...]
            a = a_s[...]
            du_ref[j] = nn(xmT[...], dh).astype(BF)
            dd_ref[j] = tn(a, g_ref[...].reshape(T, W)).astype(BF)
            begin(j, 0)
            y_ref[...] += nn(a, wd)
            dxm[...] += nt(dh, wu)

        @pl.when((j >= n_chunk) & (j < n_chunk + ns))
        def _():
            b = j - n_chunk
            rows = pl.ds(pl.multiple_of(b * L, L), L)
            xhat, rstd = norm_parts(x_ref[b].astype(F32))
            dxa = dxm[rows, :]
            gf = g_ref[b].astype(F32)
            small_ref[0:1, :] += jnp.sum(dxa * xhat, axis=0, keepdims=True)
            small_ref[1:2, :] += jnp.sum(dxa, axis=0, keepdims=True)
            small_ref[2:3, :] += jnp.sum(gf, axis=0, keepdims=True)
            dn = dxa * gain
            gm_ref[rows, :] = gf + rstd * (dn - jnp.mean(dn, axis=-1, keepdims=True)
                                           - xhat * jnp.mean(dn * xhat, axis=-1, keepdims=True))

    outs = []
    for n, (h, src, dst) in enumerate(((hu, du_ref, du_out), (hd, dd_ref, dd_out))):
        outs.append(pltpu.make_async_copy(src.at[:, pl.ds(pl.multiple_of(h.lo, 16), h.n)], dst, sl.at[3 + n]))
    for m in outs:
        m.start()

    @pl.loop(0, MOVES)
    def _(i):
        for m in moves(i):
            m.wait()
    for m in once + outs:
        m.wait()


def mlp_call(sizes, x, g, cs, gain, shift, wu, bu, wd, bias):
    ns, L, W = x.shape
    T = ns * L
    FF = wu.shape[1]
    C = 256
    n = FF // C
    steps = sum(s.bit_length() - 1 for s in sizes)
    vm = pl.BlockSpec(memory_space=pltpu.VMEM)
    hbm = pl.BlockSpec(memory_space=pl.ANY)
    S = jax.ShapeDtypeStruct
    dma = pltpu.SemaphoreType.DMA
    return pl.pallas_call(
        functools.partial(mlp_kernel, sizes),
        out_shape=(S((T, W), F32), S((T, W), F32), S((T, W), BF), S((T, W), BF), S(cs.shape, F32),
                   S((n, Halving.left(W, steps), C), BF), S((n, Halving.left(C, steps), W), BF), S((8, W), F32), S((1, FF), F32)),
        in_specs=[vm] * 9, out_specs=(vm, vm, hbm, hbm, hbm, hbm, hbm, vm, vm),
        scratch_shapes=[pltpu.VMEM((T, W), BF), pltpu.VMEM((W, T), BF), pltpu.VMEM((T, W), F32),
                        pltpu.VMEM((n, W, C), BF), pltpu.VMEM((n, C, W), BF),
                        pltpu.VMEM((n, Halving.land(W, steps), C), BF),
                        pltpu.VMEM((n, Halving.land(C, steps), W), BF),
                        pltpu.VMEM((T, C), BF), pltpu.VMEM((T, C), BF),
                        dma((n, steps)), dma((n, steps)), dma((n, steps)), dma((n, steps)),
                        dma((2, ns, MOVES)), dma((2, ns, MOVES)), dma((ns,)), dma((ns,)), dma((5,))],
        compiler_params=pltpu.CompilerParams(vmem_limit_bytes=60 << 20, collective_id=0, has_side_effects=True),
    )(x, g, cs, gain.reshape(1, W), shift.reshape(1, W), wu, bu.reshape(1, FF), wd, bias.reshape(1, W))


def tail_kernel(sizes, da_in, small_in, attn_ref, ga_ref,
                da_ref, small_ref, attn_out, ga_out,
                land_s, s_ag, r_ag, s_s, r_s, sa, ra, sl):
    place = Place(sizes)
    ns = place.seq_n
    L = attn_ref.shape[0] // ns
    n_a, R, _ = da_ref.shape
    half = R // 2
    hx = Halving(place, half, place.core + place.seq_bits + place.dp_bits)
    hy = Halving(place, half, place.core + place.seq_bits[::-1] + place.dp_bits)
    place.enter()
    loads = []
    for n, (h, lo) in enumerate(((hx, 0), (hy, half))):
        at = (slice(None), pl.ds(pl.multiple_of(lo + h.lo, 16), h.n))
        loads.append(pltpu.make_async_copy(da_in.at[:, n], da_ref.at[at], sl.at[2 + n]))
    small_ref[...] = small_in[...]
    for m in loads:
        m.start()
    moves = []
    me = pl.ds(pl.multiple_of(place.seq * L, L), L)
    for a, (src, dst) in enumerate(((attn_ref, attn_out), (ga_ref, ga_out))):
        for k in range(ns - 1, 0, -1):
            to = place.peer(k)
            moves.append(pltpu.make_async_remote_copy(
                src.at[pl.ds(pl.multiple_of(to * L, L), L)], dst.at[place.seq], sa.at[a, k], ra.at[a, k],
                device_id=(to, place.dp), device_id_type=MESH))
        moves.append(pltpu.make_async_copy(src.at[me], dst.at[place.seq], sl.at[a]))
    for m in loads:
        m.wait()
    chains = [hx.chain(da_ref.at[:, pl.ds(0, half)], s_ag.at[0], r_ag.at[0]),
              hy.chain(da_ref.at[:, pl.ds(half, half)], s_ag.at[1], r_ag.at[1])]
    small = [pltpu.make_async_remote_copy(small_ref, land_s.at[i], s_s.at[i], r_s.at[i],
                                          device_id=place.partner(bit), device_id_type=MESH)
             for i, bit in enumerate(hx.bits)]
    for i in range(len(small) + 1):
        for ops in chains:
            if i <= len(ops):
                advance(ops, i)
        if i > 0:
            small[i - 1].wait()
            small_ref[...] += land_s[i - 1]
        if i < len(small):
            small[i].start()
        if i == 0:
            for m in moves:
                m.start()
    for m in moves:
        m.wait()


def tail_call(sizes, da, small, attn, ga):
    ns = sizes[0]
    T, W = attn.shape
    L = T // ns
    pairs, R = da.shape[0], 512
    steps = sum(s.bit_length() - 1 for s in sizes)
    vm = pl.BlockSpec(memory_space=pltpu.VMEM)
    hbm = pl.BlockSpec(memory_space=pl.ANY)
    S = jax.ShapeDtypeStruct
    dma = pltpu.SemaphoreType.DMA
    return pl.pallas_call(
        functools.partial(tail_kernel, sizes),
        out_shape=(S((pairs, R, W), BF), S(small.shape, F32), S((ns, L, W), BF), S((ns, L, W), BF)),
        in_specs=[hbm, vm, hbm, hbm], out_specs=(hbm, vm, hbm, hbm),
        scratch_shapes=[pltpu.VMEM((steps,) + small.shape, F32), dma((2, steps)), dma((2, steps)),
                        dma((steps,)), dma((steps,)), dma((2, ns)), dma((2, ns)), dma((4,))],
        compiler_params=pltpu.CompilerParams(collective_id=2, has_side_effects=True),
    )(da, small, attn, ga)


def finish_kernel(du, dd, da, y, gm, attn, ga, dwu, dwd, dwqkv, ddw, out, grad,
                  vu, vd, va, ou, od, oq, ow, vy, vm, vo, vg, s_in, s_out):
    n, W, C = du.shape
    pairs = da.shape[0]
    tokens = y.shape[0]
    ins, outs = [], []

    def fetch(src, dst):
        c = pltpu.make_async_copy(src, dst, s_in.at[len(ins)])
        ins.append(c)
        c.start()
        return c

    def store(src, dst):
        c = pltpu.make_async_copy(src, dst, s_out.at[len(outs)])
        outs.append(c)
        c.start()

    fu = [fetch(du.at[i], vu.at[i]) for i in range(n)]
    fd = [fetch(dd.at[i], vd.at[i]) for i in range(n)]
    fa = [fetch(da.at[i], va.at[i]) for i in range(pairs)]
    fy = [fetch(a, b) for a, b in ((y, vy), (attn, vo), (gm, vm), (ga, vg))]
    for i in range(n):
        c = slice(i * C, (i + 1) * C)
        fu[i].wait()
        ou[:, c] = vu[i].astype(F32)
        store(ou.at[:, c], dwu.at[:, c])
        fd[i].wait()
        od[c, :] = vd[i].astype(F32)
        store(od.at[c, :], dwd.at[c, :])
    for i in range(pairs):
        fa[i].wait()
        for k in range(3):
            c = slice(k * W + i * 128, k * W + (i + 1) * 128)
            oq[:, c] = va[i, k * 128:(k + 1) * 128, :].astype(F32).T
            store(oq.at[:, c], dwqkv.at[:, c])
        c = slice(i * 128, (i + 1) * 128)
        ow[c, :] = va[i, 384:, :].astype(F32)
        store(ow.at[c, :], ddw.at[c, :])
    for f in fy:
        f.wait()
    vo[...] = (vy[...] + vo[...].astype(F32)).astype(BF)
    store(vo, out)
    vg[...] = (vm[...] + vg[...].astype(F32)).astype(BF)
    store(vg, grad)
    for c in outs:
        c.wait()


def finish_call(du, dd, da, y, gm, attn, ga):
    n, W, C = du.shape
    pairs, R, _ = da.shape
    FF = n * C
    tokens = y.shape[0]
    hbm = pl.BlockSpec(memory_space=pl.ANY)
    S = jax.ShapeDtypeStruct
    V = pltpu.VMEM
    dma = pltpu.SemaphoreType.DMA
    return pl.pallas_call(
        finish_kernel,
        out_shape=(S((W, FF), F32), S((FF, W), F32), S((W, 3 * W), F32), S((W, W), F32), S((tokens, W), BF), S((tokens, W), BF)),
        in_specs=[hbm] * 7, out_specs=(hbm,) * 6,
        scratch_shapes=[V(du.shape, BF), V(dd.shape, BF), V(da.shape, BF), V((W, FF), F32), V((FF, W), F32),
                        V((W, 3 * W), F32), V((W, W), F32), V((tokens, W), F32), V((tokens, W), F32),
                        V((tokens, W), BF), V((tokens, W), BF), dma((2 * n + pairs + 4,)), dma((2 * n + 4 * pairs + 2,))],
        compiler_params=pltpu.CompilerParams(vmem_limit_bytes=62 << 20),
    )(du, dd, da, y, gm, attn, ga)


def on_device(hidden_in, positions, attn_gain, attn_shift, qkv_weight, qkv_bias, dense_weight, dense_bias,
              mlp_gain, mlp_shift, up_weight, up_bias, down_weight, down_bias, out_grad):
    sentences, local_len, width = hidden_in.shape
    sizes = (lax.axis_size("seq"), lax.axis_size("dp"))
    assert sentences == sizes[0]
    freqs = jnp.power(10000.0, -2.0 * jnp.arange(ROT // 2, dtype=F32) / ROT)
    angles = freqs[:, None] * positions.astype(F32)[:, None, :]
    cs = jnp.concatenate([jnp.cos(angles), jnp.sin(angles)], axis=1)
    y, gm, x_s, g_s, cs_s, du, dd, small_m, dbu = mlp_call(
        sizes, hidden_in, out_grad, cs, mlp_gain, mlp_shift, up_weight, up_bias, down_weight, dense_bias + down_bias)
    attn, ga, da, du, dd, small_a, dbq = attn_call(
        sizes, x_s, g_s, cs_s, attn_gain, attn_shift, qkv_weight, qkv_bias, dense_weight, du, dd)
    small = jnp.concatenate([small_a[0], small_a[1], small_m[0], small_m[1], small_m[2], dbq[0], dbu[0]]).reshape(-1, 128)
    da, small, attn, ga = tail_call(sizes, da, small, attn, ga)
    W = width
    dwu, dwd, dwqkv, ddw, layer_out, input_grad = finish_call(du, dd, da, y, gm, attn.reshape(-1, W), ga.reshape(-1, W))
    s = small.reshape(-1)
    db = s[4 * W:5 * W]
    return (layer_out.reshape(hidden_in.shape), input_grad.reshape(hidden_in.shape), s[:W], s[W:2 * W], dwqkv,
            s[5 * W:8 * W], ddw, db, s[2 * W:3 * W], s[3 * W:4 * W], dwu, s[8 * W:], dwd, db)


def solution(mesh):
    act, rep = P("dp", "seq", None), P()
    return jax.shard_map(
        on_device, mesh=mesh,
        in_specs=(act, P("dp", "seq")) + (rep,) * 12 + (act,),
        out_specs=(act, act) + (rep,) * 12,
        check_vma=False)
```

```python
import functools
import jax
import jax.numpy as jnp
from jax import lax
from jax.experimental import pallas as pl
from jax.experimental.pallas import tpu as pltpu
from jax.sharding import PartitionSpec as P

HEADS = 12
HEAD = 64
ROT = 16
EPSILON = 1e-05
NEGATIVE = -1e30
BF, F32 = jnp.bfloat16, jnp.float32
MESH = pl.DeviceIdType.MESH
CHUNK = 256
MOVES = 8


def nn(a, b):
    return lax.dot_general(a, b, (((1,), (0,)), ((), ())), preferred_element_type=F32)


def nt(a, b):
    return lax.dot_general(a, b, (((1,), (1,)), ((), ())), preferred_element_type=F32)


def tn(a, b):
    return lax.dot_general(a, b, (((0,), (0,)), ((), ())), preferred_element_type=F32)


def norm_parts(x):
    center = x - jnp.mean(x, axis=-1, keepdims=True)
    rstd = lax.rsqrt(jnp.mean(center * center, axis=-1, keepdims=True) + EPSILON)
    return center * rstd, rstd


def norm_back(grad, xhat, rstd):
    return rstd * (grad - jnp.mean(grad, axis=-1, keepdims=True) - xhat * jnp.mean(grad * xhat, axis=-1, keepdims=True))


def cdf_pdf(h):
    t = 1.0 / (1.0 + (0.3275911 * 0.5 ** 0.5) * jnp.abs(h))
    ez = jnp.exp(-0.5 * h * h)
    poly = t * (0.5 * 0.254829592 + t * (0.5 * -0.284496736 + t * (
        0.5 * 1.421413741 + t * (0.5 * -1.453152027 + t * (0.5 * 1.061405429)))))
    tail = poly * ez
    return jnp.where(h >= 0, 1.0 - tail, tail), ez * 0.3989422804014327


def mul8(v):
    return pl.multiple_of(v, 16)


class Place:
    def __init__(self, sizes):
        self.seq_n, self.dp_n = sizes
        self.seq = lax.axis_index("seq")
        self.dp = lax.axis_index("dp")
        self.seq_bits, self.dp_bits = [], []
        for b in range(self.seq_n.bit_length() - 1):
            mine = lax.rem(self.seq // (1 << b), 2)
            self.seq_bits.append((mine, (self.seq + (1 << b) * (1 - 2 * mine), self.dp)))
        for b in range(self.dp_n.bit_length() - 1):
            mine = lax.rem(self.dp // (1 << b), 2)
            self.dp_bits.append((mine, (self.seq, self.dp + (1 << b) * (1 - 2 * mine))))
        self.core, self.dp_bits = self.dp_bits[:1], self.dp_bits[1:]

    def seq_first(self, turn):
        mixed = []
        for a, b in zip(self.seq_bits, self.seq_bits[::-1]):
            mine = a[0] + turn * (b[0] - a[0])
            mixed.append((mine, (a[1][0] + turn * (b[1][0] - a[1][0]), self.dp)))
        return self.core + mixed + self.dp_bits

    def seq_last(self):
        return self.core + self.dp_bits + self.seq_bits

    def peer(self, k):
        at = self.seq
        for b, (mine, _) in enumerate(self.seq_bits):
            at = at + (1 << b) * lax.rem(k // (1 << b), 2) * (1 - 2 * mine)
        return at

    def enter(self):
        targets = [(self.peer(jnp.int32(k)), self.dp) for k in range(1, self.seq_n)]
        targets += [bit[1] for bit in self.core + self.dp_bits]
        bar = pltpu.get_barrier_semaphore()
        for t in targets:
            pl.semaphore_signal(bar, inc=1, device_id=t, device_id_type=MESH)
        pl.semaphore_wait(bar, len(targets))


class Halving:
    def __init__(self, rows, bits):
        self.plan = []
        lo, n, off = 0, rows, 0
        for mine, partner in bits:
            halve = n % 32 == 0
            part = n // 2 if halve else n
            keep = lo + mine * part if halve else lo
            give = lo + (1 - mine) * part if halve else lo
            self.plan.append((partner, halve, part, keep, give, off))
            lo, n, off = keep, part, off + part
        self.lo, self.n = lo, n

    @staticmethod
    def land(rows, count):
        n, off = rows, 0
        for _ in range(count):
            n = n // 2 if n % 32 == 0 else n
            off += n
        return off

    def copy(self, i, buf, land, send, recv):
        partner, _, part, _, give, off = self.plan[i]
        return pltpu.make_async_remote_copy(
            buf.at[pl.ds(mul8(give), part)], land.at[pl.ds(off, part)], send.at[i], recv.at[i],
            device_id=partner, device_id_type=MESH)

    def finish(self, i, buf, land, send, recv):
        self.copy(i, buf, land, send, recv).wait()
        _, _, part, keep, _, off = self.plan[i]
        rows = pl.ds(mul8(keep), part)
        buf[rows] = (buf[rows].astype(F32) + land[pl.ds(off, part)].astype(F32)).astype(buf.dtype)

    def own(self, lo=0):
        return (slice(None), pl.ds(mul8(lo + self.lo), self.n))

    def chain(self, buf, send, recv):
        ops = []
        for i in reversed(range(len(self.plan))):
            partner, halve, part, keep, _, _ = self.plan[i]
            if halve:
                at = (slice(None), pl.ds(mul8(keep), part))
                ops.append(pltpu.make_async_remote_copy(
                    buf.at[at], buf.at[at], send.at[i], recv.at[i], device_id=partner, device_id_type=MESH))
        return ops


def advance(ops, k):
    if k > 0:
        ops[k - 1].wait()
    if k < len(ops):
        ops[k].start()


ENDS_M = (1, 3, 5, 6, 7, 8, 9)
ENDS_A = (1, 2, 3, 4, 5, 6, 7)
GAIN_A, SHIFT_A, GAIN_M, SHIFT_M, BIAS, BIAS_QKV, BIAS_UP = 0, 1, 2, 3, 4, 5, 8
SMALL = 16


def layer_kernel(sizes, x_in, g_in, cs_ref, vec_ref, bqkv_ref, wu_in, wd_in, wqkv_in, wo_in,
                 y_out, gm_out, du_out, dd_out, da_out, attn_out, ga_out, small_out,
                 du, dd, land_u, land_d, da, land_x, land_y, xs, gs, css, small, land_s,
                 su, ru, sd, rd, sx, rx, sy, ry, s_u, r_u, s_d, r_d, s_x, r_x, s_y, r_y,
                 s_in, r_in, s_c, r_c, s_out, r_out, s_s, r_s, s_l):
    place = Place(sizes)
    ns = place.seq_n
    _, L, W = x_in.shape
    T = ns * L
    n_chunk, _, C = du.shape
    pairs, R, _ = da.shape
    H2 = R // 2
    hu = Halving(W, place.seq_last())
    steps = len(hu.plan)
    hx = Halving(H2, place.seq_first(0))
    hy = Halving(H2, place.seq_first(1))
    last_m = ENDS_M[steps - 1]
    last_a = ENDS_A[steps - 1]
    t_l = n_chunk
    t_p = t_l + 1
    t_h = t_p + ns
    t_e = t_h + HEADS
    t_g = t_e + 1
    t_s = t_g + ns
    local = iter(range(100))

    place.enter()

    def mlp_pieces(p):
        at = lax.rem(p, 2) * (n_chunk // 2) + p // 2
        hd = Halving(C, place.seq_first(lax.rem(p, 2)))
        return ((hu, (du.at[at], land_u.at[at], su.at[at], ru.at[at])),
                (hd, (dd.at[at], land_d.at[at], sd.at[at], rd.at[at])))

    def attn_pieces(p):
        return ((hx, (da.at[p, pl.ds(0, H2)], land_x.at[p], sx.at[p], rx.at[p])),
                (hy, (da.at[p, pl.ds(H2, H2)], land_y.at[p], sy.at[p], ry.at[p])))

    def begin(pieces):
        for h, refs in pieces:
            h.copy(0, *refs).start()

    def halve(pieces, s):
        for h, refs in pieces:
            h.finish(s, *refs)
            if s + 1 < steps:
                h.copy(s + 1, *refs).start()

    plan = {}

    def spread(at, gaps, srcs):
        for h, src, dst, lo, send, recv in srcs:
            sem = s_l.at[next(local)]
            own = pltpu.make_async_copy(src.at[h.own(lo)], dst.at[h.own(lo)], sem)
            view = dst.at[:, pl.ds(lo, H2)] if src.shape[1] == R and h in (hx, hy) else dst
            ops = h.chain(view, send, recv)
            t = at
            plan.setdefault(t, []).append(own.start)
            t += 1
            plan.setdefault(t, []).append(own.wait)
            for k in range(len(ops) + 1):
                plan.setdefault(t, []).append(functools.partial(advance, ops, k))
                t += gaps[min(k, len(gaps) - 1)]

    half = n_chunk // 2
    third = half // 2
    for gi in range(4):
        turn, lo = gi // 2, (gi // 2) * half + (gi % 2) * third
        made = 2 * ((gi % 2) * third + third - 1) + turn
        grp = pl.ds(lo, third)
        hd = Halving(C, place.seq_first(turn))
        spread(made + last_m, (2, 2, 2, 1, 1), ((hu, du.at[grp], du_out.at[grp], 0, s_u.at[gi], r_u.at[gi]),
                                                (hd, dd.at[grp], dd_out.at[grp], 0, s_d.at[gi], r_d.at[gi])))
    for gi in range(2):
        grp = pl.ds(gi * (pairs // 2), pairs // 2)
        made = t_h + 2 * ((gi + 1) * (pairs // 2) - 1) + 1
        spread(made + last_a, (1,), ((hx, da.at[grp], da_out.at[grp], 0, s_x.at[gi], r_x.at[gi]),
                                     (hy, da.at[grp], da_out.at[grp], H2, s_y.at[gi], r_y.at[gi])))
    for i in range(steps + 1):
        def exchange(i=i):
            def cp(i):
                return pltpu.make_async_remote_copy(small, land_s.at[i], s_s.at[i], r_s.at[i],
                                                    device_id=place.seq_last()[i][1], device_id_type=MESH)
            if i > 0:
                cp(i - 1).wait()
                small[...] += land_s[i - 1]
            if i < steps:
                cp(i).start()
        plan.setdefault(t_s + i, []).append(exchange)
    end = max(plan) + 1

    def tick(t, lo, hi):
        for s in range(steps):
            p = t - ENDS_M[s]

            @pl.when((p >= 0) & (p < n_chunk))
            def _():
                halve(mlp_pieces(p), s)
        if hi > t_h:
            for s in range(steps):
                q = t - t_h - 1 - ENDS_A[s]

                @pl.when((q >= 0) & (q < 2 * pairs) & (lax.rem(q + 2 * pairs, 2) == 0))
                def _():
                    halve(attn_pieces(q // 2), s)
        for at in range(lo, hi):
            if at in plan:
                @pl.when(t == at)
                def _():
                    for act in plan[at]:
                        act()

    part = L // MOVES

    def moves(i):
        out = []
        for a, (src, dst) in enumerate(((x_in, xs), (g_in, gs))):
            for k in range(ns - 1, 0, -1):
                to = place.peer(jnp.int32(k))
                out.append(pltpu.make_async_remote_copy(
                    src.at[to, pl.ds(mul8(i * part), part)], dst.at[pl.ds(mul8(place.seq * L + i * part), part)],
                    s_in.at[a, k, i], r_in.at[a, k, i], device_id=(to, place.dp), device_id_type=MESH))
        return out

    once = []
    me = pl.ds(mul8(place.seq * L), L)
    for k in range(ns - 1, 0, -1):
        to = place.peer(jnp.int32(k))
        once.append(pltpu.make_async_remote_copy(
            cs_ref.at[to], css.at[place.seq], s_c.at[k], r_c.at[k], device_id=(to, place.dp), device_id_type=MESH))
    for src, dst in ((x_in, xs.at[me]), (g_in, gs.at[me]), (cs_ref, css.at[place.seq])):
        once.append(pltpu.make_async_copy(src.at[place.seq], dst, s_l.at[next(local)]))

    def row(i):
        return vec_ref[i:i + 1, :]

    def feed_forward(wu_ref, wd_ref, x_ref, g_ref, xm, xmT, dxm, y, a_s, dh_s):
        loads = [pltpu.make_async_copy(src, dst, s_l.at[next(local)])
                 for src, dst in ((x_in, x_ref), (g_in, g_ref), (wu_in, wu_ref), (wd_in, wd_ref))]
        for m in loads + once + moves(0):
            m.start()
        loads[0].wait()
        small[...] = jnp.zeros_like(small)
        for b in range(ns):
            rows = slice(b * L, (b + 1) * L)
            x = x_ref[b].astype(F32)
            xhat, _ = norm_parts(x)
            v = (xhat * row(2) + row(3)).astype(BF)
            xm[rows, :] = v
            xmT[:, rows] = v.T
            y[rows, :] = x + row(4)
        dxm[...] = jnp.zeros_like(dxm)
        for m in loads[1:]:
            m.wait()

        @pl.loop(0, t_l + 1)
        def _(t):
            c = pl.ds(pl.multiple_of(jnp.minimum(t, n_chunk - 1) * C, C), C)

            @pl.when((t > 0) & (t < 4) | (t > 4) & (t < 2 * MOVES - 4) & (lax.rem(t, 2) == 1))
            def _():
                for m in moves(jnp.where(t < 4, t, (t + 3) // 2)):
                    m.start()

            @pl.when(t < n_chunk)
            def _():
                wu = wu_ref[:, c]
                wd = wd_ref[c, :]
                bu = vec_ref[pl.ds(8 + t // 3, 1), pl.ds(pl.multiple_of(lax.rem(t, 3) * C, C), C)]
                dbu = jnp.zeros((1, C), F32)
                for b in range(ns):
                    rows = slice(b * L, (b + 1) * L)
                    h = nn(xm[rows, :], wu) + bu
                    cdf, pdf = cdf_pdf(h)
                    a_s[rows, :] = (h * cdf).astype(BF)
                    dh = (nt(g_ref[b], wd) * (cdf + h * pdf)).astype(BF)
                    dh_s[rows, :] = dh
                    dbu += jnp.sum(dh.astype(F32), axis=0, keepdims=True)
                small[pl.ds(BIAS_UP + t // 3, 1), pl.ds(pl.multiple_of(lax.rem(t, 3) * C, C), C)] = dbu

            tick(t, 0, t_l + 1)

            @pl.when(t < n_chunk)
            def _():
                wu = wu_ref[:, c]
                wd = wd_ref[c, :]
                dh = dh_s[...]
                a = a_s[...]
                at = lax.rem(t, 2) * (n_chunk // 2) + t // 2
                du[at] = nn(xmT[...], dh).astype(BF)
                dd[at] = tn(a, g_ref[...].reshape(T, W)).astype(BF)
                begin(mlp_pieces(t))
                y[...] += nn(a, wd)
                dxm[...] += nt(dh, wu)

            @pl.when(t == t_l)
            def _():
                store = pltpu.make_async_copy(y, y_out, s_l.at[next(local)])
                store.start()
                for b in range(ns):
                    rows = slice(b * L, (b + 1) * L)
                    xhat, rstd = norm_parts(x_ref[b].astype(F32))
                    dxa = dxm[rows, :]
                    gf = g_ref[b].astype(F32)
                    small[GAIN_M:GAIN_M + 1, :] += jnp.sum(dxa * xhat, axis=0, keepdims=True)
                    small[SHIFT_M:SHIFT_M + 1, :] += jnp.sum(dxa, axis=0, keepdims=True)
                    small[BIAS:BIAS + 1, :] += jnp.sum(gf, axis=0, keepdims=True)
                    dxm[rows, :] = gf + norm_back(dxa * row(2), xhat, rstd)
                back = pltpu.make_async_copy(dxm, gm_out, s_l.at[next(local)])
                back.start()
                store.wait()
                back.wait()

        @pl.loop(0, MOVES)
        def _(i):
            for m in moves(i):
                m.wait()
        for m in once:
            m.wait()

    def attention(wqkv, wo, wT, xaT, qkvT, kn, vn, dOT, obT, attn, ga):
        loads = [pltpu.make_async_copy(src, dst, s_l.at[next(local)]) for src, dst in ((wqkv_in, wqkv), (wo_in, wo))]
        for m in loads:
            m.start()
        for m in loads:
            m.wait()
        for j in range(9):
            wT[j * 256:(j + 1) * 256, :] = wqkv[:, j * 256:(j + 1) * 256].T
        sub = lax.broadcasted_iota(jnp.int32, (L, L), 0)
        lane = lax.broadcasted_iota(jnp.int32, (L, L), 1)
        keep = sub <= lane
        rowid = lax.broadcasted_iota(jnp.int32, (128, 1), 0)

        def back_copy(a, k, src, dst):
            to = place.peer(k)
            return pltpu.make_async_remote_copy(
                src.at[pl.ds(mul8(to * L), L)], dst.at[place.seq], s_out.at[a, k], r_out.at[a, k],
                device_id=(to, place.dp), device_id_type=MESH)

        def own_copy(a, src, dst):
            return pltpu.make_async_copy(src.at[me], dst.at[place.seq], s_out.at[a, 0])

        def unrotate(d, b):
            cos = css[b, :8, :]
            sin = css[b, 8:, :]
            return jnp.concatenate([d[:8] * cos + d[8:16] * sin, d[8:16] * cos - d[:8] * sin, d[16:]], axis=0)

        @pl.loop(t_p, end)
        def _(t):
            tick(t, t_p, end)

            @pl.when(t < t_h)
            def _():
                b = t - t_p
                rows = pl.ds(pl.multiple_of(b * L, L), L)
                xhat, _ = norm_parts(xs[rows, :].astype(F32))
                xa = (xhat * row(0) + row(1)).astype(BF)
                xaT[:, rows] = xa.T
                cos = css[b, :8, :]
                sin = css[b, 8:, :]
                for j in range(9):
                    at = slice(j * 256, (j + 1) * 256)
                    m = nt(wT[at, :], xa) + bqkv_ref[at, :]
                    if j < 6:
                        parts = []
                        for h in range(4):
                            u = m[h * 64:(h + 1) * 64]
                            parts += [u[:8] * cos - u[8:16] * sin, u[8:16] * cos + u[:8] * sin, u[16:]]
                        m = jnp.concatenate(parts, axis=0)
                        if j < 3:
                            m = m * (HEAD ** -0.5)
                    mb = m.astype(BF)
                    qkvT[at, rows] = mb
                    if 3 <= j < 6:
                        kn[rows, (j - 3) * 256:(j - 2) * 256] = mb.T
                    if j >= 6:
                        vn[rows, (j - 6) * 256:(j - 5) * 256] = mb.T
                g = gs[rows, :]
                for j in range(3):
                    at = slice(j * 256, (j + 1) * 256)
                    dOT[at, rows] = nt(wo[at, :], g).astype(BF)

            @pl.when((t >= t_h) & (t < t_e))
            def _():
                head = t - t_h
                pair = head // 2
                r0 = pl.multiple_of(pair * 128, 128)
                cols = pl.ds(r0, 128)
                hr = pl.ds(pl.multiple_of(head * 64, 64), 64)
                kr = pl.ds(pl.multiple_of(W + head * 64, 64), 64)
                vr = pl.ds(pl.multiple_of(2 * W + head * 64, 64), 64)
                msk = rowid // 64 == lax.rem(head, 2)
                dk = [None] * ns
                dv = [None] * ns
                dq = [None] * ns
                for i in range(ns):
                    n = (i + 1) * L
                    qs = slice(i * L, (i + 1) * L)
                    qT2 = jnp.where(msk, qkvT[cols, qs], 0).astype(BF)
                    dO2 = jnp.where(msk, dOT[cols, qs], 0).astype(BF)
                    s = nn(kn[0:n, cols], qT2)
                    d = jnp.where(keep, s[n - L:], NEGATIVE)
                    s = jnp.concatenate([s[:n - L], d], axis=0) if i > 0 else d
                    e = jnp.exp(s - jnp.max(s, axis=0, keepdims=True))
                    inv = 1.0 / jnp.sum(e, axis=0, keepdims=True)
                    p = e.astype(BF)
                    oT = nn(qkvT[vr, 0:n], p) * inv
                    dO = dOT[hr, qs].astype(F32)
                    delta = jnp.sum(dO * oT, axis=0, keepdims=True)
                    obT[hr, qs] = oT.astype(BF)
                    dp = nn(vn[0:n, cols], dO2)
                    ds = (e * ((dp - delta) * inv)).astype(BF)
                    dq[i] = nn(qkvT[kr, 0:n], ds) * (HEAD ** -0.5)
                    dkT = nt(qkvT[hr, qs], ds)
                    dvT = nt((dO * inv).astype(BF), p)
                    for b in range(i + 1):
                        sl = slice(b * L, (b + 1) * L)
                        dk[b] = dkT[:, sl] if dk[b] is None else dk[b] + dkT[:, sl]
                        dv[b] = dvT[:, sl] if dv[b] is None else dv[b] + dvT[:, sl]
                for b in range(ns):
                    sl = slice(b * L, (b + 1) * L)
                    qkvT[hr, sl] = unrotate(dq[b], b).astype(BF)
                    qkvT[kr, sl] = unrotate(dk[b], b).astype(BF)
                    qkvT[vr, sl] = dv[b].astype(BF)

                @pl.when(lax.rem(head, 2) == 1)
                def _():
                    dm = jnp.concatenate([qkvT[cols, :], qkvT[pl.ds(W + r0, 128), :], qkvT[pl.ds(2 * W + r0, 128), :]], axis=0)
                    da[pair, :384, :] = nt(dm, xaT[...]).astype(BF)
                    da[pair, 384:, :] = nn(obT[cols, :], gs[...]).astype(BF)
                    begin(attn_pieces(pair))
                    db = nt(jnp.ones((8, T), BF), dm)
                    for i in range(3):
                        small[BIAS_QKV + i:BIAS_QKV + i + 1, cols] = db[0:1, i * 128:(i + 1) * 128]

            @pl.when(t == t_e)
            def _():
                for k in range(ns - 1, -1, -1):
                    b = place.peer(jnp.int32(k))
                    rows = pl.ds(pl.multiple_of(b * L, L), L)
                    attn[rows, :] = nn(obT[:, rows].T, wo[...]).astype(BF)
                    if k > 0:
                        back_copy(0, k, attn, attn_out).start()
                    else:
                        own_copy(0, attn, attn_out).start()

            @pl.when((t >= t_g) & (t < t_s))
            def _():
                k = t_s - 1 - t
                b = place.peer(k)
                rows = pl.ds(pl.multiple_of(b * L, L), L)
                dxa = nn(wqkv[...], qkvT[:, rows]).T
                xhat, rstd = norm_parts(xs[rows, :].astype(F32))
                small[GAIN_A:GAIN_A + 1, :] += jnp.sum(dxa * xhat, axis=0, keepdims=True)
                small[SHIFT_A:SHIFT_A + 1, :] += jnp.sum(dxa, axis=0, keepdims=True)
                ga[rows, :] = norm_back(dxa * row(0), xhat, rstd).astype(BF)

                @pl.when(k > 0)
                def _():
                    back_copy(1, k, ga, ga_out).start()

                @pl.when(k == 0)
                def _():
                    own_copy(1, ga, ga_out).start()

        for a, (src, dst) in enumerate(((attn, attn_out), (ga, ga_out))):
            for k in range(ns - 1, 0, -1):
                back_copy(a, jnp.int32(k), src, dst).wait()
            own_copy(a, src, dst).wait()
        small_out[...] = small[...]

    V = pltpu.VMEM
    FF = n_chunk * C
    pl.run_scoped(feed_forward, V((W, FF), BF), V((FF, W), BF), V((ns, L, W), BF), V((ns, L, W), BF), V((T, W), BF),
                  V((W, T), BF), V((T, W), F32), V((T, W), F32), V((T, C), BF), V((T, C), BF))
    pl.run_scoped(attention, V((W, 3 * W), BF), V((W, W), BF), V((3 * W, W), BF), V((W, T), BF), V((3 * W, T), BF), V((T, W), BF), V((T, W), BF),
                  V((W, T), BF), V((W, T), BF), V((T, W), BF), V((T, W), BF))


def layer_call(sizes, x, g, cs, vec, bqkv, wu, wd, wqkv, wo):
    ns, L, W = x.shape
    T = ns * L
    FF = wu.shape[1]
    C = CHUNK
    n = FF // C
    pairs, R = HEADS // 2, 4 * 2 * HEAD
    steps = sum(s.bit_length() - 1 for s in sizes)
    vm = pl.BlockSpec(memory_space=pltpu.VMEM)
    hbm = pl.BlockSpec(memory_space=pl.ANY)
    S = jax.ShapeDtypeStruct
    V = pltpu.VMEM
    dma = pltpu.SemaphoreType.DMA
    la = Halving.land(R // 2, steps)
    return pl.pallas_call(
        functools.partial(layer_kernel, sizes),
        out_shape=(S((T, W), F32), S((T, W), F32), S((n, W, C), BF), S((n, C, W), BF), S((pairs, R, W), BF),
                   S((ns, L, W), BF), S((ns, L, W), BF), S((SMALL, W), F32)),
        in_specs=[hbm, hbm, vm, vm, vm, hbm, hbm, hbm, hbm], out_specs=(hbm,) * 7 + (vm,),
        scratch_shapes=[V((n, W, C), BF), V((n, C, W), BF), V((n, Halving.land(W, steps), C), BF),
                        V((n, Halving.land(C, steps), W), BF), V((pairs, R, W), BF), V((pairs, la, W), BF),
                        V((pairs, la, W), BF), V((T, W), BF), V((T, W), BF), V(cs.shape, F32), V((SMALL, W), F32), V((steps, SMALL, W), F32)]
        + [dma((n, steps))] * 4 + [dma((pairs, steps))] * 4 + [dma((4, steps))] * 4 + [dma((2, steps))] * 4
        + [dma((2, ns, MOVES))] * 2 + [dma((ns,))] * 2 + [dma((2, ns))] * 2 + [dma((steps,))] * 2 + [dma((32,))],
        compiler_params=pltpu.CompilerParams(vmem_limit_bytes=62 << 20, collective_id=0, has_side_effects=True),
    )(x, g, cs, vec, bqkv, wu, wd, wqkv, wo)


def finish_kernel(du, dd, da, y, gm, attn, ga, dwu, dwd, dwqkv, ddw, out, grad,
                  vu, vd, va, ou, od, oq, ow, vy, vm, vo, vg, s_in, s_out):
    n, W, C = du.shape
    pairs = da.shape[0]
    ins, outs = [], []

    def fetch(src, dst):
        c = pltpu.make_async_copy(src, dst, s_in.at[len(ins)])
        ins.append(c)
        c.start()
        return c

    def store(src, dst):
        c = pltpu.make_async_copy(src, dst, s_out.at[len(outs)])
        outs.append(c)
        c.start()

    fu = [fetch(du.at[i], vu.at[i]) for i in range(n)]
    fd = [fetch(dd.at[i], vd.at[i]) for i in range(n)]
    fa = [fetch(da.at[i], va.at[i]) for i in range(pairs)]
    fy = [fetch(a, b) for a, b in ((y, vy), (attn, vo), (gm, vm), (ga, vg))]
    for i in range(n):
        j = 2 * i if i < n // 2 else 2 * (i - n // 2) + 1
        c = slice(j * C, (j + 1) * C)
        fu[i].wait()
        ou[:, c] = vu[i].astype(F32)
        store(ou.at[:, c], dwu.at[:, c])
        fd[i].wait()
        od[c, :] = vd[i].astype(F32)
        store(od.at[c, :], dwd.at[c, :])
    for i in range(pairs):
        fa[i].wait()
        for k in range(3):
            c = slice(k * W + i * 128, k * W + (i + 1) * 128)
            oq[:, c] = va[i, k * 128:(k + 1) * 128, :].astype(F32).T
            store(oq.at[:, c], dwqkv.at[:, c])
        c = slice(i * 128, (i + 1) * 128)
        ow[c, :] = va[i, 384:, :].astype(F32)
        store(ow.at[c, :], ddw.at[c, :])
    for f in fy:
        f.wait()
    vo[...] = (vy[...] + vo[...].astype(F32)).astype(BF)
    store(vo, out)
    vg[...] = (vm[...] + vg[...].astype(F32)).astype(BF)
    store(vg, grad)
    for c in outs:
        c.wait()


def finish_call(du, dd, da, y, gm, attn, ga):
    n, W, C = du.shape
    pairs = da.shape[0]
    FF = n * C
    tokens = y.shape[0]
    hbm = pl.BlockSpec(memory_space=pl.ANY)
    S = jax.ShapeDtypeStruct
    V = pltpu.VMEM
    dma = pltpu.SemaphoreType.DMA
    return pl.pallas_call(
        finish_kernel,
        out_shape=(S((W, FF), F32), S((FF, W), F32), S((W, 3 * W), F32), S((W, W), F32), S((tokens, W), BF), S((tokens, W), BF)),
        in_specs=[hbm] * 7, out_specs=(hbm,) * 6,
        scratch_shapes=[V(du.shape, BF), V(dd.shape, BF), V(da.shape, BF), V((W, FF), F32), V((FF, W), F32),
                        V((W, 3 * W), F32), V((W, W), F32), V((tokens, W), F32), V((tokens, W), F32),
                        V((tokens, W), BF), V((tokens, W), BF), dma((2 * n + pairs + 4,)), dma((2 * n + 4 * pairs + 2,))],
        compiler_params=pltpu.CompilerParams(vmem_limit_bytes=62 << 20),
    )(du, dd, da, y, gm, attn, ga)


def on_device(hidden_in, positions, attn_gain, attn_shift, qkv_weight, qkv_bias, dense_weight, dense_bias,
              mlp_gain, mlp_shift, up_weight, up_bias, down_weight, down_bias, out_grad):
    sentences, local_len, W = hidden_in.shape
    sizes = (lax.axis_size("seq"), lax.axis_size("dp"))
    assert sentences == sizes[0]
    freqs = jnp.power(10000.0, -2.0 * jnp.arange(ROT // 2, dtype=F32) / ROT)
    angles = freqs[:, None] * positions.astype(F32)[:, None, :]
    cs = jnp.concatenate([jnp.cos(angles), jnp.sin(angles)], axis=1)
    zero = jnp.zeros((W,), F32)
    vec = jnp.concatenate([attn_gain, attn_shift, mlp_gain, mlp_shift, dense_bias + down_bias, zero, zero, zero,
                           up_bias, zero, zero, zero, zero]).reshape(16, W)
    y, gm, du, dd, da, attn, ga, small = layer_call(
        sizes, hidden_in, out_grad, cs, vec, qkv_bias.reshape(-1, 1), up_weight, down_weight, qkv_weight, dense_weight)
    dwu, dwd, dwqkv, ddw, layer_out, input_grad = finish_call(du, dd, da, y, gm, attn.reshape(-1, W), ga.reshape(-1, W))
    db = small[BIAS]
    return (layer_out.reshape(hidden_in.shape), input_grad.reshape(hidden_in.shape), small[GAIN_A], small[SHIFT_A], dwqkv,
            small[BIAS_QKV:BIAS_UP].reshape(-1), ddw, db, small[GAIN_M], small[SHIFT_M], dwu,
            small[BIAS_UP:BIAS_UP + 4].reshape(-1), dwd, db)


def solution(mesh):
    act, rep = P("dp", "seq", None), P()
    return jax.shard_map(
        on_device, mesh=mesh,
        in_specs=(act, P("dp", "seq")) + (rep,) * 12 + (act,),
        out_specs=(act, act) + (rep,) * 12,
        check_vma=False)
```

```python
import functools
import jax
import jax.numpy as jnp
from jax import lax
from jax.experimental import pallas as pl
from jax.experimental.pallas import tpu as pltpu
from jax.sharding import PartitionSpec as P

HEADS = 12
HEAD = 64
ROT = 16
EPSILON = 1e-05
NEGATIVE = -1e30
BF, F32 = jnp.bfloat16, jnp.float32
MESH = pl.DeviceIdType.MESH
CHUNK = 256
MOVES = 8


def nn(a, b):
    return lax.dot_general(a, b, (((1,), (0,)), ((), ())), preferred_element_type=F32)


def nt(a, b):
    return lax.dot_general(a, b, (((1,), (1,)), ((), ())), preferred_element_type=F32)


def tn(a, b):
    return lax.dot_general(a, b, (((0,), (0,)), ((), ())), preferred_element_type=F32)


def norm_parts(x):
    center = x - jnp.mean(x, axis=-1, keepdims=True)
    rstd = lax.rsqrt(jnp.mean(center * center, axis=-1, keepdims=True) + EPSILON)
    return center * rstd, rstd


def norm_back(grad, xhat, rstd):
    return rstd * (grad - jnp.mean(grad, axis=-1, keepdims=True) - xhat * jnp.mean(grad * xhat, axis=-1, keepdims=True))


def cdf_pdf(h):
    t = 1.0 / (1.0 + (0.3275911 * 0.5 ** 0.5) * jnp.abs(h))
    ez = jnp.exp(-0.5 * h * h)
    poly = t * (0.5 * 0.254829592 + t * (0.5 * -0.284496736 + t * (
        0.5 * 1.421413741 + t * (0.5 * -1.453152027 + t * (0.5 * 1.061405429)))))
    tail = poly * ez
    return jnp.where(h >= 0, 1.0 - tail, tail), ez * 0.3989422804014327


def mul8(v):
    return pl.multiple_of(v, 16)


class Place:
    def __init__(self, sizes):
        self.seq_n, self.dp_n = sizes
        self.seq = lax.axis_index("seq")
        self.dp = lax.axis_index("dp")
        self.seq_bits, self.dp_bits = [], []
        for b in range(self.seq_n.bit_length() - 1):
            mine = lax.rem(self.seq // (1 << b), 2)
            self.seq_bits.append((mine, (self.seq + (1 << b) * (1 - 2 * mine), self.dp)))
        for b in range(self.dp_n.bit_length() - 1):
            mine = lax.rem(self.dp // (1 << b), 2)
            self.dp_bits.append((mine, (self.seq, self.dp + (1 << b) * (1 - 2 * mine))))
        self.core, self.dp_bits = self.dp_bits[:1], self.dp_bits[1:]

    def order(self, name):
        seq = self.seq_bits[::-1] if name.endswith("r") else self.seq_bits
        name = name.rstrip("r")
        first, then = (seq, self.dp_bits) if name[0] == "s" else (self.dp_bits, seq)
        if len(name) == 1:
            return self.core + first + then
        n = min(len(first), len(then))
        return self.core + [b for two in zip(first, then) for b in two] + first[n:] + then[n:]

    def mix(self, a, b, turn):
        return [(m + turn * (n - m), (p[0] + turn * (q[0] - p[0]), p[1] + turn * (q[1] - p[1])))
                for (m, p), (n, q) in zip(self.order(a), self.order(b))]

    def peer(self, k):
        at = self.seq
        for b, (mine, _) in enumerate(self.seq_bits):
            at = at + (1 << b) * lax.rem(k // (1 << b), 2) * (1 - 2 * mine)
        return at

    def others(self, bits):
        out = []
        for c in range(1, 1 << len(bits)):
            sq, dp = self.seq, self.dp
            for j, (_, other) in enumerate(bits):
                if c >> j & 1:
                    sq, dp = sq + other[0] - self.seq, dp + other[1] - self.dp
            out.append((sq, dp))
        return out

    def enter(self):
        targets = [(self.peer(jnp.int32(k)), self.dp) for k in range(1, self.seq_n)]
        targets += [bit[1] for bit in self.core]
        for i in range(0, len(self.dp_bits), 2):
            targets += self.others(self.dp_bits[i:i + 2])
        bar = pltpu.get_barrier_semaphore()
        for t in targets:
            pl.semaphore_signal(bar, inc=1, device_id=t, device_id_type=MESH)
        pl.semaphore_wait(bar, len(targets))


class Halving:
    def __init__(self, rows, bits):
        self.plan = []
        lo, n, off = 0, rows, 0
        for mine, partner in bits:
            halve = n % 32 == 0
            part = n // 2 if halve else n
            keep = lo + mine * part if halve else lo
            give = lo + (1 - mine) * part if halve else lo
            self.plan.append((partner, halve, part, keep, give, off))
            lo, n, off = keep, part, off + part
        self.lo, self.n = lo, n

    @staticmethod
    def land(rows, count):
        n, off = rows, 0
        for _ in range(count):
            n = n // 2 if n % 32 == 0 else n
            off += n
        return off

    def copy(self, i, buf, land, send, recv):
        partner, _, part, _, give, off = self.plan[i]
        return pltpu.make_async_remote_copy(
            buf.at[pl.ds(mul8(give), part)], land.at[pl.ds(off, part)], send.at[i], recv.at[i],
            device_id=partner, device_id_type=MESH)

    def finish(self, i, buf, land, send, recv):
        self.copy(i, buf, land, send, recv).wait()
        _, _, part, keep, _, off = self.plan[i]
        rows = pl.ds(mul8(keep), part)
        buf[rows] = (buf[rows].astype(F32) + land[pl.ds(off, part)].astype(F32)).astype(buf.dtype)

    def own(self, lo=0):
        return (slice(None), pl.ds(mul8(lo + self.lo), self.n))

    def chain(self, buf, send, recv):
        ops = []
        for i in reversed(range(len(self.plan))):
            partner, halve, part, keep, _, _ = self.plan[i]
            if halve:
                at = (slice(None), pl.ds(mul8(keep), part))
                ops.append(pltpu.make_async_remote_copy(
                    buf.at[at], buf.at[at], send.at[i], recv.at[i], device_id=partner, device_id_type=MESH))
        return ops


def advance(ops, k):
    if k > 0:
        ops[k - 1].wait()
    if k < len(ops):
        ops[k].start()


ENDS_M = (1, 3, 5, 8, 10, 11, 12)
ENDS_A = (1, 3, 5, 7, 9, 10, 11)
UP, DOWN = ("s", "szr"), ("zr", "z")
LEFT, RIGHT = ("s", "szr"), ("sr", "zs")
GAPS_U, GAPS_D, GAPS_A = (2, 2, 3, 1, 1), (2, 3, 3, 3, 3), (2, 1, 2, 2)
SPLIT_M = 3
GAIN_A, SHIFT_A, GAIN_M, SHIFT_M, BIAS, BIAS_QKV, BIAS_UP = 0, 1, 2, 3, 4, 5, 8
SMALL = 16


def layer_kernel(sizes, x_in, g_in, cs_ref, vec_ref, wu_in, wd_in, wqkv_in, wo_in,
                 y_out, gm_out, du_out, dd_out, da_out, attn_out, ga_out, small_out,
                 du, dd, land_u, land_d, da, land_x, land_y, xs, gs, css, ob_own, small, land_s,
                 su, ru, sd, rd, sx, rx, sy, ry, s_u, r_u, s_d, r_d, s_x, r_x, s_y, r_y,
                 s_in, r_in, s_c, r_c, s_o, r_o, s_out, r_out, s_s, r_s, s_l):
    place = Place(sizes)
    ns = place.seq_n
    _, L, W = x_in.shape
    T = ns * L
    n_chunk, _, C = du.shape
    pairs, R, _ = da.shape
    H2 = R // 2
    steps = len(place.order("s"))
    last_m = ENDS_M[steps - 1]
    last_a = ENDS_A[steps - 1]
    t_l = n_chunk
    t_p = t_l + 1
    t_h = t_p + ns
    t_g = t_h + HEADS
    t_s = t_g + ns
    t_e = t_s
    local = iter(range(100))

    place.enter()

    def mlp_pieces(p):
        at = lax.rem(p, 2) * (n_chunk // 2) + p // 2
        hu = Halving(W, place.mix(*UP, lax.rem(p, 2)))
        hd = Halving(C, place.mix(*DOWN, lax.rem(p, 2)))
        return ((hu, (du.at[at], land_u.at[at], su.at[at], ru.at[at])),
                (hd, (dd.at[at], land_d.at[at], sd.at[at], rd.at[at])))

    def attn_pieces(p):
        hx = Halving(H2, place.mix(*LEFT, p // (pairs - 2)))
        hy = Halving(H2, place.mix(*RIGHT, p // (pairs - 2)))
        return ((hx, (da.at[p, pl.ds(0, H2)], land_x.at[p], sx.at[p], rx.at[p])),
                (hy, (da.at[p, pl.ds(H2, H2)], land_y.at[p], sy.at[p], ry.at[p])))

    def begin(pieces):
        for h, refs in pieces:
            h.copy(0, *refs).start()

    def halve(pieces, s):
        for h, refs in pieces:
            h.finish(s, *refs)
            if s + 1 < steps:
                h.copy(s + 1, *refs).start()

    plan = {}

    def spread(at, srcs):
        for h, src, dst, lo, send, recv, gaps in srcs:
            sem = s_l.at[next(local)]
            own = pltpu.make_async_copy(src.at[h.own(lo)], dst.at[h.own(lo)], sem)
            view = dst.at[:, pl.ds(lo, H2)] if src.shape[1] == R else dst
            ops = h.chain(view, send, recv)
            t = at
            plan.setdefault(t, []).append(own.start)
            t += 1
            plan.setdefault(t, []).append(own.wait)
            for k in range(len(ops) + 1):
                plan.setdefault(t, []).append(functools.partial(advance, ops, k))
                t += gaps[min(k, len(gaps) - 1)]

    half = n_chunk // 2
    third = half // SPLIT_M
    for gi in range(2 * SPLIT_M):
        turn, lo = gi // SPLIT_M, (gi % SPLIT_M) * third
        made = 2 * (lo + third - 1) + turn
        grp = pl.ds(turn * half + lo, third)
        hu = Halving(W, place.order(UP[turn]))
        hd = Halving(C, place.order(DOWN[turn]))
        spread(made + last_m, ((hu, du.at[grp], du_out.at[grp], 0, s_u.at[gi], r_u.at[gi], GAPS_U),
                               (hd, dd.at[grp], dd_out.at[grp], 0, s_d.at[gi], r_d.at[gi], GAPS_D)))
    for gi in range(3):
        grp = pl.ds(gi * (pairs // 3), pairs // 3)
        made = t_h + 2 * ((gi + 1) * (pairs // 3) - 1) + 1
        hx = Halving(H2, place.order(LEFT[gi // 2]))
        hy = Halving(H2, place.order(RIGHT[gi // 2]))
        spread(made + last_a, ((hx, da.at[grp], da_out.at[grp], 0, s_x.at[gi], r_x.at[gi], GAPS_A),
                               (hy, da.at[grp], da_out.at[grp], H2, s_y.at[gi], r_y.at[gi], GAPS_A)))
    rounds = [place.core] + [bits[i:i + 2] for bits in (place.seq_bits, place.dp_bits) for i in range(0, len(bits), 2)]

    def small_copies(i):
        return [pltpu.make_async_remote_copy(small, land_s.at[i, c + 1], s_s.at[i, c + 1], r_s.at[i, c + 1],
                                             device_id=to, device_id_type=MESH)
                for c, to in enumerate(place.others(rounds[i]))]

    def small_round(i):
        if i > 0:
            bits = rounds[i - 1]
            for m in small_copies(i - 1):
                m.wait()
            parts = {0: small[...]}
            parts.update({c: land_s[i - 1, c] for c in range(1, 1 << len(bits))})
            for j in range(len(bits)):
                parts = {c: parts[c] + parts[c | 1 << j] for c in parts if not c >> j & 1}
            small[...] = parts[0]
        if i < len(rounds):
            for m in small_copies(i):
                m.start()

    assert all(len(bits) <= 2 for bits in rounds)
    for i in range(len(rounds) + 1):
        plan.setdefault(t_s + i, []).append(functools.partial(small_round, i))
    end = max(plan) + 1

    def tick(t, lo, hi):
        for s in range(steps):
            p = t - ENDS_M[s]

            @pl.when((p >= 0) & (p < n_chunk))
            def _():
                halve(mlp_pieces(p), s)
        if hi > t_h:
            for s in range(steps):
                q = t - t_h - 1 - ENDS_A[s]

                @pl.when((q >= 0) & (q < 2 * pairs) & (lax.rem(q + 2 * pairs, 2) == 0))
                def _():
                    halve(attn_pieces(q // 2), s)
        for at in range(lo, hi):
            if at in plan:
                @pl.when(t == at)
                def _():
                    for act in plan[at]:
                        act()

    part = L // MOVES

    def moves(i):
        out = []
        for a, (src, dst) in enumerate(((x_in, xs), (g_in, gs))):
            for k in range(ns - 1, 0, -1):
                to = place.peer(jnp.int32(k))
                out.append(pltpu.make_async_remote_copy(
                    src.at[to, pl.ds(mul8(i * part), part)], dst.at[pl.ds(mul8(place.seq * L + i * part), part)],
                    s_in.at[a, k, i], r_in.at[a, k, i], device_id=(to, place.dp), device_id_type=MESH))
        return out

    once = []
    me = pl.ds(mul8(place.seq * L), L)
    for k in range(ns - 1, 0, -1):
        to = place.peer(jnp.int32(k))
        once.append(pltpu.make_async_remote_copy(
            cs_ref.at[to], css.at[place.seq], s_c.at[k], r_c.at[k], device_id=(to, place.dp), device_id_type=MESH))
    for src, dst in ((x_in, xs.at[me]), (g_in, gs.at[me]), (cs_ref, css.at[place.seq])):
        once.append(pltpu.make_async_copy(src.at[place.seq], dst, s_l.at[next(local)]))

    def row(i):
        return vec_ref[i:i + 1, :]

    def feed_forward(wu_ref, wd_ref, x_ref, g_ref, xm, xmT, dxm, y, a_s, dh_s):
        loads = [pltpu.make_async_copy(src, dst, s_l.at[next(local)])
                 for src, dst in ((x_in, x_ref), (g_in, g_ref), (wu_in, wu_ref), (wd_in, wd_ref))]
        for m in loads + once + moves(0):
            m.start()
        loads[0].wait()
        small[...] = jnp.zeros_like(small)
        for b in range(ns):
            rows = slice(b * L, (b + 1) * L)
            x = x_ref[b].astype(F32)
            xhat, _ = norm_parts(x)
            v = (xhat * row(2) + row(3)).astype(BF)
            xm[rows, :] = v
            xmT[:, rows] = v.T
            y[rows, :] = x + row(4)
        dxm[...] = jnp.zeros_like(dxm)
        for m in loads[1:]:
            m.wait()

        @pl.loop(0, t_l + 1)
        def _(t):
            c = pl.ds(pl.multiple_of(jnp.minimum(t, n_chunk - 1) * C, C), C)

            @pl.when((t > 0) & (t < 4) | (t > 4) & (t < 2 * MOVES - 4) & (lax.rem(t, 2) == 1))
            def _():
                for m in moves(jnp.where(t < 4, t, (t + 3) // 2)):
                    m.start()

            @pl.when(t < n_chunk)
            def _():
                wu = wu_ref[:, c]
                wd = wd_ref[c, :]
                bu = vec_ref[pl.ds(8 + t // 3, 1), pl.ds(pl.multiple_of(lax.rem(t, 3) * C, C), C)]
                dbu = jnp.zeros((1, C), F32)
                for b in range(ns):
                    rows = slice(b * L, (b + 1) * L)
                    h = nn(xm[rows, :], wu) + bu
                    cdf, pdf = cdf_pdf(h)
                    a_s[rows, :] = (h * cdf).astype(BF)
                    dh = (nt(g_ref[b], wd) * (cdf + h * pdf)).astype(BF)
                    dh_s[rows, :] = dh
                    dbu += jnp.sum(dh.astype(F32), axis=0, keepdims=True)
                small[pl.ds(BIAS_UP + t // 3, 1), pl.ds(pl.multiple_of(lax.rem(t, 3) * C, C), C)] = dbu

            tick(t, 0, t_l + 1)

            @pl.when(t < n_chunk)
            def _():
                wu = wu_ref[:, c]
                wd = wd_ref[c, :]
                dh = dh_s[...]
                a = a_s[...]
                at = lax.rem(t, 2) * (n_chunk // 2) + t // 2
                du[at] = nn(xmT[...], dh).astype(BF)
                dd[at] = tn(a, g_ref[...].reshape(T, W)).astype(BF)
                begin(mlp_pieces(t))
                y[...] += nn(a, wd)
                dxm[...] += nt(dh, wu)

            @pl.when(t == t_l)
            def _():
                store = pltpu.make_async_copy(y, y_out, s_l.at[next(local)])
                store.start()
                for b in range(ns):
                    rows = slice(b * L, (b + 1) * L)
                    xhat, rstd = norm_parts(x_ref[b].astype(F32))
                    dxa = dxm[rows, :]
                    gf = g_ref[b].astype(F32)
                    small[GAIN_M:GAIN_M + 1, :] += jnp.sum(dxa * xhat, axis=0, keepdims=True)
                    small[SHIFT_M:SHIFT_M + 1, :] += jnp.sum(dxa, axis=0, keepdims=True)
                    small[BIAS:BIAS + 1, :] += jnp.sum(gf, axis=0, keepdims=True)
                    dxm[rows, :] = gf + norm_back(dxa * row(2), xhat, rstd)
                back = pltpu.make_async_copy(dxm, gm_out, s_l.at[next(local)])
                back.start()
                store.wait()
                back.wait()

        @pl.loop(0, MOVES)
        def _(i):
            for m in moves(i):
                m.wait()
        for m in once:
            m.wait()

    def attention(wqkv, wo, wT, xaT, qkvT, kn, vn, dOT, obT, obn, attn, ga):
        loads = [pltpu.make_async_copy(src, dst, s_l.at[next(local)]) for src, dst in ((wqkv_in, wqkv), (wo_in, wo))]
        for m in loads:
            m.start()
        for m in loads:
            m.wait()
        for j in range(9):
            wT[j * 256:(j + 1) * 256, :] = wqkv[:, j * 256:(j + 1) * 256].T
        sub = lax.broadcasted_iota(jnp.int32, (L, L), 0)
        lane = lax.broadcasted_iota(jnp.int32, (L, L), 1)
        keep = sub <= lane
        rowid = lax.broadcasted_iota(jnp.int32, (128, 1), 0)

        def ga_copy(k):
            to = place.peer(k)
            return pltpu.make_async_remote_copy(
                ga.at[pl.ds(mul8(to * L), L)], ga_out.at[place.seq], s_out.at[k], r_out.at[k],
                device_id=(to, place.dp), device_id_type=MESH)

        ga_own = pltpu.make_async_copy(ga.at[me], ga_out.at[place.seq], s_out.at[0])
        attn_copy = pltpu.make_async_copy(attn, attn_out, r_out.at[0])

        def ob_copy(k, pair):
            to = place.peer(jnp.int32(k))
            cols = pl.ds(pl.multiple_of(pair * 128, 128), 128)
            return pltpu.make_async_remote_copy(
                obn.at[pl.ds(mul8(to * L), L), cols], ob_own.at[place.seq, :, cols], s_o.at[k, pair], r_o.at[k, pair],
                device_id=(to, place.dp), device_id_type=MESH)

        def unrotate(d, b):
            cos = css[b, :8, :]
            sin = css[b, 8:, :]
            return jnp.concatenate([d[:8] * cos + d[8:16] * sin, d[8:16] * cos - d[:8] * sin, d[16:]], axis=0)

        @pl.loop(t_p, end)
        def _(t):
            @pl.when(t < t_h)
            def _():
                b = t - t_p
                rows = pl.ds(pl.multiple_of(b * L, L), L)
                xhat, _ = norm_parts(xs[rows, :].astype(F32))
                xa = (xhat * row(0) + row(1)).astype(BF)
                xaT[:, rows] = xa.T
                cos = css[b, :8, :]
                sin = css[b, 8:, :]
                for j in range(9):
                    at = slice(j * 256, (j + 1) * 256)
                    bq = vec_ref[5 + j // 3:6 + j // 3, (j % 3) * 256:(j % 3 + 1) * 256]
                    m = nt(wT[at, :], xa) + jnp.broadcast_to(bq, (8, 256)).T[:, :1]
                    if j < 6:
                        parts = []
                        for h in range(4):
                            u = m[h * 64:(h + 1) * 64]
                            parts += [u[:8] * cos - u[8:16] * sin, u[8:16] * cos + u[:8] * sin, u[16:]]
                        m = jnp.concatenate(parts, axis=0)
                        if j < 3:
                            m = m * (HEAD ** -0.5)
                    mb = m.astype(BF)
                    qkvT[at, rows] = mb
                    if 3 <= j < 6:
                        kn[rows, (j - 3) * 256:(j - 2) * 256] = mb.T
                    if j >= 6:
                        vn[rows, (j - 6) * 256:(j - 5) * 256] = mb.T
                g = gs[rows, :]
                for j in range(3):
                    at = slice(j * 256, (j + 1) * 256)
                    dOT[at, rows] = nt(wo[at, :], g).astype(BF)

            @pl.when((t >= t_h) & (t < t_g))
            def _():
                head = t - t_h
                pair = head // 2
                r0 = pl.multiple_of(pair * 128, 128)
                cols = pl.ds(r0, 128)
                hr = pl.ds(pl.multiple_of(head * 64, 64), 64)
                kr = pl.ds(pl.multiple_of(W + head * 64, 64), 64)
                vr = pl.ds(pl.multiple_of(2 * W + head * 64, 64), 64)
                msk = rowid // 64 == lax.rem(head, 2)
                dk = [None] * ns
                dv = [None] * ns
                dq = [None] * ns
                for i in range(ns):
                    n = (i + 1) * L
                    qs = slice(i * L, (i + 1) * L)
                    qT2 = jnp.where(msk, qkvT[cols, qs], 0).astype(BF)
                    dO2 = jnp.where(msk, dOT[cols, qs], 0).astype(BF)
                    s = nn(kn[0:n, cols], qT2)
                    d = jnp.where(keep, s[n - L:], NEGATIVE)
                    s = jnp.concatenate([s[:n - L], d], axis=0) if i > 0 else d
                    e = jnp.exp(s - jnp.max(s, axis=0, keepdims=True))
                    inv = 1.0 / jnp.sum(e, axis=0, keepdims=True)
                    p = e.astype(BF)
                    oT = nn(qkvT[vr, 0:n], p) * inv
                    dO = dOT[hr, qs].astype(F32)
                    delta = jnp.sum(dO * oT, axis=0, keepdims=True)
                    obT[hr, qs] = oT.astype(BF)
                    dp = nn(vn[0:n, cols], dO2)
                    ds = (e * ((dp - delta) * inv)).astype(BF)
                    dq[i] = nn(qkvT[kr, 0:n], ds) * (HEAD ** -0.5)
                    dkT = nt(qkvT[hr, qs], ds)
                    dvT = nt((dO * inv).astype(BF), p)
                    for b in range(i + 1):
                        sl = slice(b * L, (b + 1) * L)
                        dk[b] = dkT[:, sl] if dk[b] is None else dk[b] + dkT[:, sl]
                        dv[b] = dvT[:, sl] if dv[b] is None else dv[b] + dvT[:, sl]
                for b in range(ns):
                    sl = slice(b * L, (b + 1) * L)
                    qkvT[hr, sl] = unrotate(dq[b], b).astype(BF)
                    qkvT[kr, sl] = unrotate(dk[b], b).astype(BF)
                    qkvT[vr, sl] = dv[b].astype(BF)

            tick(t, t_p, end)

            @pl.when((t >= t_h) & (t < t_g) & (lax.rem(t - t_h + HEADS, 2) == 1))
            def _():
                pair = (t - t_h) // 2
                r0 = pl.multiple_of(pair * 128, 128)
                cols = pl.ds(r0, 128)
                obn[:, cols] = obT[cols, :].T
                for k in range(ns - 1, 0, -1):
                    ob_copy(k, pair).start()
                dm = jnp.concatenate([qkvT[cols, :], qkvT[pl.ds(W + r0, 128), :], qkvT[pl.ds(2 * W + r0, 128), :]], axis=0)
                da[pair, :384, :] = nt(dm, xaT[...]).astype(BF)
                da[pair, 384:, :] = nn(obT[cols, :], gs[...]).astype(BF)
                begin(attn_pieces(pair))
                db = nt(jnp.ones((8, T), BF), dm)
                for i in range(3):
                    small[BIAS_QKV + i:BIAS_QKV + i + 1, cols] = db[0:1, i * 128:(i + 1) * 128]

            @pl.when((t >= t_g) & (t < t_s))
            def _():
                k = t_s - 1 - t
                b = place.peer(k)
                rows = pl.ds(pl.multiple_of(b * L, L), L)
                dxa = nn(wqkv[...], qkvT[:, rows]).T
                xhat, rstd = norm_parts(xs[rows, :].astype(F32))
                small[GAIN_A:GAIN_A + 1, :] += jnp.sum(dxa * xhat, axis=0, keepdims=True)
                small[SHIFT_A:SHIFT_A + 1, :] += jnp.sum(dxa, axis=0, keepdims=True)
                ga[rows, :] = norm_back(dxa * row(0), xhat, rstd).astype(BF)

                @pl.when(k > 0)
                def _():
                    ga_copy(k).start()

                @pl.when(k == 0)
                def _():
                    ga_own.start()

            @pl.when(t == t_e)
            def _():
                for k in range(1, ns):
                    for i in range(pairs):
                        ob_copy(k, i).wait()

            @pl.when((t >= t_e) & (t < t_e + ns))
            def _():
                b = t - t_e

                @pl.when(b == place.seq)
                def _():
                    ob_own[b] = obn[me, :]
                attn[b] = nn(ob_own[b], wo[...]).astype(BF)

            @pl.when(t == t_e + ns - 1)
            def _():
                attn_copy.start()

        for k in range(ns - 1, 0, -1):
            ga_copy(jnp.int32(k)).wait()
        ga_own.wait()
        attn_copy.wait()
        small_out[...] = small[...]

    V = pltpu.VMEM
    FF = n_chunk * C
    pl.run_scoped(feed_forward, V((W, FF), BF), V((FF, W), BF), V((ns, L, W), BF), V((ns, L, W), BF), V((T, W), BF),
                  V((W, T), BF), V((T, W), F32), V((T, W), F32), V((T, C), BF), V((T, C), BF))
    pl.run_scoped(attention, V((W, 3 * W), BF), V((W, W), BF), V((3 * W, W), BF), V((W, T), BF), V((3 * W, T), BF), V((T, W), BF), V((T, W), BF),
                  V((W, T), BF), V((W, T), BF), V((T, W), BF), V((ns, L, W), BF), V((T, W), BF))


def layer_call(sizes, x, g, cs, vec, wu, wd, wqkv, wo):
    ns, L, W = x.shape
    T = ns * L
    FF = wu.shape[1]
    C = CHUNK
    n = FF // C
    pairs, R = HEADS // 2, 4 * 2 * HEAD
    steps = sum(s.bit_length() - 1 for s in sizes)
    vm = pl.BlockSpec(memory_space=pltpu.VMEM)
    hbm = pl.BlockSpec(memory_space=pl.ANY)
    S = jax.ShapeDtypeStruct
    V = pltpu.VMEM
    dma = pltpu.SemaphoreType.DMA
    la = Halving.land(R // 2, steps)
    return pl.pallas_call(
        functools.partial(layer_kernel, sizes),
        out_shape=(S((T, W), F32), S((T, W), F32), S((n, W, C), BF), S((n, C, W), BF), S((pairs, R, W), BF),
                   S((ns, L, W), BF), S((ns, L, W), BF), S((SMALL, W), F32)),
        in_specs=[hbm, hbm, vm, vm, hbm, hbm, hbm, hbm], out_specs=(hbm,) * 7 + (vm,),
        scratch_shapes=[V((n, W, C), BF), V((n, C, W), BF), V((n, Halving.land(W, steps), C), BF),
                        V((n, Halving.land(C, steps), W), BF), V((pairs, R, W), BF), V((pairs, la, W), BF),
                        V((pairs, la, W), BF), V((T, W), BF), V((T, W), BF), V(cs.shape, F32), V((ns, L, W), BF), V((SMALL, W), F32), V((steps, 4, SMALL, W), F32)]
        + [dma((n, steps))] * 4 + [dma((pairs, steps))] * 4 + [dma((2 * SPLIT_M, steps))] * 4 + [dma((3, steps))] * 4
        + [dma((2, ns, MOVES))] * 2 + [dma((ns,))] * 2 + [dma((ns, pairs))] * 2 + [dma((ns,))] * 2 + [dma((steps, 4))] * 2 + [dma((48,))],
        compiler_params=pltpu.CompilerParams(vmem_limit_bytes=63 << 20, collective_id=0, has_side_effects=True),
    )(x, g, cs, vec, wu, wd, wqkv, wo)


def finish_kernel(du, dd, da, y, gm, attn, ga, dwu, dwd, dwqkv, ddw, out, grad,
                  vu, vd, va, ou, od, oq, ow, vy, vm, vo, vg, s_in, s_out):
    n, W, C = du.shape
    pairs = da.shape[0]
    ins, outs = [], []

    def fetch(src, dst):
        c = pltpu.make_async_copy(src, dst, s_in.at[len(ins)])
        ins.append(c)
        c.start()
        return c

    def store(src, dst):
        c = pltpu.make_async_copy(src, dst, s_out.at[len(outs)])
        outs.append(c)
        c.start()

    fu = [fetch(du.at[i], vu.at[i]) for i in range(n)]
    fd = [fetch(dd.at[i], vd.at[i]) for i in range(n)]
    fa = [fetch(da.at[i], va.at[i]) for i in range(pairs)]
    fy = [fetch(a, b) for a, b in ((y, vy), (attn, vo), (gm, vm), (ga, vg))]
    for i in range(n):
        j = 2 * i if i < n // 2 else 2 * (i - n // 2) + 1
        c = slice(j * C, (j + 1) * C)
        fu[i].wait()
        ou[:, c] = vu[i].astype(F32)
        store(ou.at[:, c], dwu.at[:, c])
        fd[i].wait()
        od[c, :] = vd[i].astype(F32)
        store(od.at[c, :], dwd.at[c, :])
    for i in range(pairs):
        fa[i].wait()
        for k in range(3):
            c = slice(k * W + i * 128, k * W + (i + 1) * 128)
            oq[:, c] = va[i, k * 128:(k + 1) * 128, :].astype(F32).T
            store(oq.at[:, c], dwqkv.at[:, c])
        c = slice(i * 128, (i + 1) * 128)
        ow[c, :] = va[i, 384:, :].astype(F32)
        store(ow.at[c, :], ddw.at[c, :])
    for f in fy:
        f.wait()
    vo[...] = (vy[...] + vo[...].astype(F32)).astype(BF)
    store(vo, out)
    vg[...] = (vm[...] + vg[...].astype(F32)).astype(BF)
    store(vg, grad)
    for c in outs:
        c.wait()


def finish_call(du, dd, da, y, gm, attn, ga):
    n, W, C = du.shape
    pairs = da.shape[0]
    FF = n * C
    tokens = y.shape[0]
    hbm = pl.BlockSpec(memory_space=pl.ANY)
    S = jax.ShapeDtypeStruct
    V = pltpu.VMEM
    dma = pltpu.SemaphoreType.DMA
    return pl.pallas_call(
        finish_kernel,
        out_shape=(S((W, FF), F32), S((FF, W), F32), S((W, 3 * W), F32), S((W, W), F32), S((tokens, W), BF), S((tokens, W), BF)),
        in_specs=[hbm] * 7, out_specs=(hbm,) * 6,
        scratch_shapes=[V(du.shape, BF), V(dd.shape, BF), V(da.shape, BF), V((W, FF), F32), V((FF, W), F32),
                        V((W, 3 * W), F32), V((W, W), F32), V((tokens, W), F32), V((tokens, W), F32),
                        V((tokens, W), BF), V((tokens, W), BF), dma((2 * n + pairs + 4,)), dma((2 * n + 4 * pairs + 2,))],
        compiler_params=pltpu.CompilerParams(vmem_limit_bytes=63 << 20),
    )(du, dd, da, y, gm, attn, ga)


def on_device(hidden_in, positions, attn_gain, attn_shift, qkv_weight, qkv_bias, dense_weight, dense_bias,
              mlp_gain, mlp_shift, up_weight, up_bias, down_weight, down_bias, out_grad):
    sentences, local_len, W = hidden_in.shape
    sizes = (lax.axis_size("seq"), lax.axis_size("dp"))
    assert sentences == sizes[0]
    freqs = jnp.power(10000.0, -2.0 * jnp.arange(ROT // 2, dtype=F32) / ROT)
    angles = freqs[:, None] * positions.astype(F32)[:, None, :]
    cs = jnp.concatenate([jnp.cos(angles), jnp.sin(angles)], axis=1)
    zero = jnp.zeros((W,), F32)
    vec = jnp.concatenate([attn_gain, attn_shift, mlp_gain, mlp_shift, dense_bias + down_bias, qkv_bias,
                           up_bias, zero, zero, zero, zero]).reshape(16, W)
    y, gm, du, dd, da, attn, ga, small = layer_call(
        sizes, hidden_in, out_grad, cs, vec, up_weight, down_weight, qkv_weight, dense_weight)
    dwu, dwd, dwqkv, ddw, layer_out, input_grad = finish_call(du, dd, da, y, gm, attn.reshape(-1, W), ga.reshape(-1, W))
    db = small[BIAS]
    return (layer_out.reshape(hidden_in.shape), input_grad.reshape(hidden_in.shape), small[GAIN_A], small[SHIFT_A], dwqkv,
            small[BIAS_QKV:BIAS_UP].reshape(-1), ddw, db, small[GAIN_M], small[SHIFT_M], dwu,
            small[BIAS_UP:BIAS_UP + 4].reshape(-1), dwd, db)


def solution(mesh):
    act, rep = P("dp", "seq", None), P()
    return jax.shard_map(
        on_device, mesh=mesh,
        in_specs=(act, P("dp", "seq")) + (rep,) * 12 + (act,),
        out_specs=(act, act) + (rep,) * 12,
        check_vma=False)
```

```python
import functools
import jax
import jax.numpy as jnp
from jax import lax
from jax.experimental import pallas as pl
from jax.experimental.pallas import tpu as pltpu
from jax.sharding import PartitionSpec as P

HEADS = 12
HEAD = 64
ROT = 16
EPSILON = 1e-05
NEGATIVE = -1e30
BF, F32 = jnp.bfloat16, jnp.float32
MESH = pl.DeviceIdType.MESH
CHUNK = 256
MOVES = 8


def nn(a, b):
    return lax.dot_general(a, b, (((1,), (0,)), ((), ())), preferred_element_type=F32)


def nt(a, b):
    return lax.dot_general(a, b, (((1,), (1,)), ((), ())), preferred_element_type=F32)


def tn(a, b):
    return lax.dot_general(a, b, (((0,), (0,)), ((), ())), preferred_element_type=F32)


def norm_parts(x):
    center = x - jnp.mean(x, axis=-1, keepdims=True)
    rstd = lax.rsqrt(jnp.mean(center * center, axis=-1, keepdims=True) + EPSILON)
    return center * rstd, rstd


def norm_back(grad, xhat, rstd):
    return rstd * (grad - jnp.mean(grad, axis=-1, keepdims=True) - xhat * jnp.mean(grad * xhat, axis=-1, keepdims=True))


def cdf_pdf(h):
    t = 1.0 / (1.0 + (0.3275911 * 0.5 ** 0.5) * jnp.abs(h))
    ez = jnp.exp(-0.5 * h * h)
    poly = t * (0.5 * 0.254829592 + t * (0.5 * -0.284496736 + t * (
        0.5 * 1.421413741 + t * (0.5 * -1.453152027 + t * (0.5 * 1.061405429)))))
    tail = poly * ez
    return jnp.where(h >= 0, 1.0 - tail, tail), ez * 0.3989422804014327


def mul8(v):
    return pl.multiple_of(v, 16)


class Place:
    def __init__(self, sizes):
        self.seq_n, self.dp_n = sizes
        self.seq = lax.axis_index("seq")
        self.dp = lax.axis_index("dp")
        self.seq_bits, self.dp_bits = [], []
        for b in range(self.seq_n.bit_length() - 1):
            mine = lax.rem(self.seq // (1 << b), 2)
            self.seq_bits.append((mine, (self.seq + (1 << b) * (1 - 2 * mine), self.dp)))
        for b in range(self.dp_n.bit_length() - 1):
            mine = lax.rem(self.dp // (1 << b), 2)
            self.dp_bits.append((mine, (self.seq, self.dp + (1 << b) * (1 - 2 * mine))))
        self.core, self.dp_bits = self.dp_bits[:1], self.dp_bits[1:]

    def order(self, name):
        seq = self.seq_bits[::-1] if name.endswith("r") else self.seq_bits
        name = name.rstrip("r")
        first, then = (seq, self.dp_bits) if name[0] == "s" else (self.dp_bits, seq)
        if len(name) == 1:
            return self.core + first + then
        n = min(len(first), len(then))
        return self.core + [b for two in zip(first, then) for b in two] + first[n:] + then[n:]

    def mix(self, names, turn):
        at = [jnp.where(turn == i, 1, 0) for i in range(len(names))]
        orders = [self.order(name) for name in names]
        return [(sum(w * o[i][0] for w, o in zip(at, orders)),
                 (sum(w * o[i][1][0] for w, o in zip(at, orders)), sum(w * o[i][1][1] for w, o in zip(at, orders))))
                for i in range(len(orders[0]))]

    def peer(self, k):
        at = self.seq
        for b, (mine, _) in enumerate(self.seq_bits):
            at = at + (1 << b) * lax.rem(k // (1 << b), 2) * (1 - 2 * mine)
        return at

    def others(self, bits):
        out = []
        for c in range(1, 1 << len(bits)):
            sq, dp = self.seq, self.dp
            for j, (_, other) in enumerate(bits):
                if c >> j & 1:
                    sq, dp = sq + other[0] - self.seq, dp + other[1] - self.dp
            out.append((sq, dp))
        return out

    def targets(self):
        targets = [(self.peer(jnp.int32(k)), self.dp) for k in range(1, self.seq_n)]
        targets += [bit[1] for bit in self.core]
        for i in range(0, len(self.dp_bits), 2):
            targets += self.others(self.dp_bits[i:i + 2])
        return targets

    def signal(self):
        bar = pltpu.get_barrier_semaphore()
        for t in self.targets():
            pl.semaphore_signal(bar, inc=1, device_id=t, device_id_type=MESH)

    def enter(self):
        pl.semaphore_wait(pltpu.get_barrier_semaphore(), len(self.targets()))


class Halving:
    def __init__(self, rows, bits):
        self.plan = []
        lo, n, off = 0, rows, 0
        for mine, partner in bits:
            halve = n % 32 == 0
            part = n // 2 if halve else n
            keep = lo + mine * part if halve else lo
            give = lo + (1 - mine) * part if halve else lo
            self.plan.append((partner, halve, part, keep, give, off))
            lo, n, off = keep, part, off + part
        self.lo, self.n = lo, n

    @staticmethod
    def land(rows, count):
        n, off = rows, 0
        for _ in range(count):
            n = n // 2 if n % 32 == 0 else n
            off += n
        return off

    def copy(self, i, buf, land, send, recv):
        partner, _, part, _, give, off = self.plan[i]
        return pltpu.make_async_remote_copy(
            buf.at[pl.ds(mul8(give), part)], land.at[pl.ds(off, part)], send.at[i], recv.at[i],
            device_id=partner, device_id_type=MESH)

    def finish(self, i, buf, land, send, recv):
        self.copy(i, buf, land, send, recv).wait()
        _, _, part, keep, _, off = self.plan[i]
        rows = pl.ds(mul8(keep), part)
        buf[rows] = buf[rows] + land[pl.ds(off, part)]

    def own(self, lo=0):
        return (slice(None), pl.ds(mul8(lo + self.lo), self.n))

    def chain(self, buf, send, recv):
        ops = []
        for i in reversed(range(len(self.plan))):
            partner, halve, part, keep, _, _ = self.plan[i]
            if halve:
                at = (slice(None), pl.ds(mul8(keep), part))
                ops.append(pltpu.make_async_remote_copy(
                    buf.at[at], buf.at[at], send.at[i], recv.at[i], device_id=partner, device_id_type=MESH))
        return ops


def advance(ops, k):
    if k > 0:
        ops[k - 1].wait()
    if k < len(ops):
        ops[k].start()


ENDS_M = (2, 5, 7, 9, 11, 12, 13)
ENDS_A = (2, 3, 4, 5, 7, 8, 9)
ENDS_L = (1, 2, 3, 4, 5, 6, 7)
UP, DOWN = ("sz", "zsr"), ("zsr", "sr")
LEFT, RIGHT = ("szr", "s", "sz"), ("sz", "sr", "szr")
GAPS_U, GAPS_D, GAPS_A, GAPS_L = (2, 3, 3, 3, 2), (2, 2, 2, 1, 1), (1, 2, 2, 1), (1,)
WAIT_A = (1, 0, 0)
GA_SENDS = (0, 6, 7)
SPLIT_M = 3
GAIN_A, SHIFT_A, GAIN_M, SHIFT_M, BIAS, BIAS_QKV, BIAS_UP = 0, 1, 2, 3, 4, 5, 8
SMALL = 16


def layer_kernel(sizes, x_in, g_in, cs_ref, ga_v, sa_v, gm_v, sm_v, bo_v, bd_v, bq_v, bu_v, wu_in, wd_in, wqkv_in, wo_in,
                 y_out, gm_out, du_out, dd_out, da_out, attn_out, ga_out, small_out,
                 du, dd, land_u, land_d, da, land_x, land_y, xs, gs, css, ob_own, vec_ref, small, land_s,
                 su, ru, sd, rd, sx, rx, sy, ry, s_u, r_u, s_d, r_d, s_x, r_x, s_y, r_y,
                 s_in, r_in, s_c, r_c, s_o, r_o, s_out, r_out, s_s, r_s, s_l):
    place = Place(sizes)
    ns = place.seq_n
    _, L, W = x_in.shape
    T = ns * L
    n_chunk, _, C = du.shape
    pairs, R, _ = da.shape
    H2 = R // 2
    steps = len(place.order("s"))
    last_m = ENDS_M[steps - 1]
    t_l = n_chunk
    t_p = t_l + 1
    t_h = t_p + ns
    t_g = t_h + HEADS
    t_s = t_g + ns
    t_e = t_s
    local = iter(range(100))
    place.signal()

    def mlp_pieces(p):
        at = lax.rem(p, 2) * (n_chunk // 2) + p // 2
        hu = Halving(W, place.mix(UP, lax.rem(p, 2)))
        hd = Halving(C, place.mix(DOWN, lax.rem(p, 2)))
        return ((hu, (du.at[at], land_u.at[at], su.at[at], ru.at[at])),
                (hd, (dd.at[at], land_d.at[at], sd.at[at], rd.at[at])))

    def attn_pieces(p):
        hx = Halving(H2, place.mix(LEFT, p // 2))
        hy = Halving(H2, place.mix(RIGHT, p // 2))
        return ((hx, (da.at[p, pl.ds(0, H2)], land_x.at[p], sx.at[p], rx.at[p])),
                (hy, (da.at[p, pl.ds(H2, H2)], land_y.at[p], sy.at[p], ry.at[p])))

    def begin(pieces):
        for h, refs in pieces:
            h.copy(0, *refs).start()

    def halve(pieces, s):
        for h, refs in pieces:
            h.finish(s, *refs)
            if s + 1 < steps:
                h.copy(s + 1, *refs).start()

    plan = {}

    def spread(at, srcs):
        for h, src, dst, lo, send, recv, gaps in srcs:
            sem = s_l.at[next(local)]
            own = pltpu.make_async_copy(src.at[h.own(lo)], dst.at[h.own(lo)], sem)
            view = dst.at[:, pl.ds(lo, H2)] if src.shape[1] == R else dst
            ops = h.chain(view, send, recv)
            t = at
            plan.setdefault(t, []).append(own.start)
            t += 1
            plan.setdefault(t, []).append(own.wait)
            for k in range(len(ops) + 1):
                plan.setdefault(t, []).append(functools.partial(advance, ops, k))
                t += gaps[min(k, len(gaps) - 1)]

    half = n_chunk // 2
    third = half // SPLIT_M
    for gi in range(2 * SPLIT_M):
        turn, lo = gi // SPLIT_M, (gi % SPLIT_M) * third
        made = 2 * (lo + third - 1) + turn
        grp = pl.ds(turn * half + lo, third)
        hu = Halving(W, place.order(UP[turn]))
        hd = Halving(C, place.order(DOWN[turn]))
        spread(made + last_m, ((hu, du.at[grp], du_out.at[grp], 0, s_u.at[gi], r_u.at[gi], GAPS_U),
                               (hd, dd.at[grp], dd_out.at[grp], 0, s_d.at[gi], r_d.at[gi], GAPS_D)))
    for gi in range(3):
        grp = pl.ds(2 * gi, 2)
        made = t_h + 4 * gi + 3
        late = gi == 2
        hx = Halving(H2, place.order(LEFT[gi]))
        hy = Halving(H2, place.order(RIGHT[gi]))
        gaps = GAPS_L if late else GAPS_A
        spread(made + (ENDS_L if late else ENDS_A)[steps - 1] + WAIT_A[gi],
               ((hx, da.at[grp], da_out.at[grp], 0, s_x.at[gi], r_x.at[gi], gaps),
                (hy, da.at[grp], da_out.at[grp], H2, s_y.at[gi], r_y.at[gi], gaps)))
    rounds = [place.core] + [bits[i:i + 2] for bits in (place.seq_bits, place.dp_bits) for i in range(0, len(bits), 2)]

    def small_copies(i):
        return [pltpu.make_async_remote_copy(small, land_s.at[i, c + 1], s_s.at[i, c + 1], r_s.at[i, c + 1],
                                             device_id=to, device_id_type=MESH)
                for c, to in enumerate(place.others(rounds[i]))]

    def small_round(i):
        if i > 0:
            bits = rounds[i - 1]
            for m in small_copies(i - 1):
                m.wait()
            parts = {0: small[...]}
            parts.update({c: land_s[i - 1, c] for c in range(1, 1 << len(bits))})
            for j in range(len(bits)):
                parts = {c: parts[c] + parts[c | 1 << j] for c in parts if not c >> j & 1}
            small[...] = parts[0]
        if i < len(rounds):
            for m in small_copies(i):
                m.start()

    assert all(len(bits) <= 2 for bits in rounds)
    for i in range(len(rounds) + 1):
        plan.setdefault(t_s + i, []).append(functools.partial(small_round, i))
    end = max(max(plan), t_g + max(GA_SENDS)) + 1
    assert ns == len(GA_SENDS) + 1 and pairs == 6

    def tick(t, lo, hi):
        for s in range(steps):
            p = t - ENDS_M[s]

            @pl.when((p >= 0) & (p < n_chunk))
            def _():
                halve(mlp_pieces(p), s)
        if hi > t_h:
            for s in range(steps):
                for ends, first, end in ((ENDS_A, 0, 2 * pairs - 4), (ENDS_L, 2 * pairs - 4, 2 * pairs)):
                    q = t - t_h - 1 - ends[s]

                    @pl.when((q >= first) & (q < end) & (lax.rem(q + 2 * pairs, 2) == 0))
                    def _():
                        halve(attn_pieces(q // 2), s)
        for at in range(lo, hi):
            if at in plan:
                @pl.when(t == at)
                def _():
                    for act in plan[at]:
                        act()

    part = L // MOVES

    def moves(i):
        out = []
        for a, (src, dst) in enumerate(((x_in, xs), (g_in, gs))):
            for k in range(ns - 1, 0, -1):
                to = place.peer(jnp.int32(k))
                out.append(pltpu.make_async_remote_copy(
                    src.at[to, pl.ds(mul8(i * part), part)], dst.at[pl.ds(mul8(place.seq * L + i * part), part)],
                    s_in.at[a, k, i], r_in.at[a, k, i], device_id=(to, place.dp), device_id_type=MESH))
        return out

    once = []
    me = pl.ds(mul8(place.seq * L), L)
    for k in range(ns - 1, 0, -1):
        to = place.peer(jnp.int32(k))
        once.append(pltpu.make_async_remote_copy(
            cs_ref.at[to], css.at[place.seq], s_c.at[k], r_c.at[k], device_id=(to, place.dp), device_id_type=MESH))
    for src, dst in ((x_in, xs.at[me]), (g_in, gs.at[me]), (cs_ref, css.at[place.seq])):
        once.append(pltpu.make_async_copy(src.at[place.seq], dst, s_l.at[next(local)]))


    def row(i):
        return vec_ref[i:i + 1, :]

    def feed_forward(wu_ref, wd_ref, x_ref, g_ref, xm, xmT, dxm, y, a_s, dh_s):
        head, rest = pl.ds(0, C), pl.ds(C, FF - C)
        loads = [pltpu.make_async_copy(src, dst, s_l.at[next(local)])
                 for src, dst in ((x_in, x_ref), (g_in, g_ref), (wu_in.at[:, head], wu_ref.at[:, head]),
                                  (wd_in.at[head], wd_ref.at[head]), (wu_in.at[:, rest], wu_ref.at[:, rest]),
                                  (wd_in.at[rest], wd_ref.at[rest]))]
        for m in loads:
            m.start()
        for i, v in enumerate((ga_v, sa_v, gm_v, sm_v)):
            vec_ref[i:i + 1, :] = v[...].reshape(1, W)
        vec_ref[4:5, :] = (bo_v[...] + bd_v[...]).reshape(1, W)
        for i in range(3):
            vec_ref[5 + i:6 + i, :] = bq_v[i * W:(i + 1) * W].reshape(1, W)
        for i in range(FF // W):
            vec_ref[8 + i:9 + i, :] = bu_v[i * W:(i + 1) * W].reshape(1, W)
        loads[0].wait()
        small[...] = jnp.zeros_like(small)
        for b in range(ns):
            rows = slice(b * L, (b + 1) * L)
            x = x_ref[b].astype(F32)
            xhat, _ = norm_parts(x)
            v = (xhat * row(2) + row(3)).astype(BF)
            xm[rows, :] = v
            xmT[:, rows] = v.T
            y[rows, :] = x + row(4)
        dxm[...] = jnp.zeros_like(dxm)
        place.enter()
        for m in once + moves(0):
            m.start()
        for m in loads[1:4]:
            m.wait()

        @pl.loop(0, t_l + 1)
        def _(t):
            c = pl.ds(pl.multiple_of(jnp.minimum(t, n_chunk - 1) * C, C), C)

            @pl.when((t > 0) & (t < 4) | (t > 4) & (t < 2 * MOVES - 4) & (lax.rem(t, 2) == 1))
            def _():
                for m in moves(jnp.where(t < 4, t, (t + 3) // 2)):
                    m.start()

            @pl.when(t < n_chunk)
            def _():
                wu = wu_ref[:, c]
                wd = wd_ref[c, :]
                bu = vec_ref[pl.ds(8 + t // 3, 1), pl.ds(pl.multiple_of(lax.rem(t, 3) * C, C), C)]
                dbu = jnp.zeros((1, C), F32)
                for b in range(ns):
                    rows = slice(b * L, (b + 1) * L)
                    h = nn(xm[rows, :], wu) + bu
                    cdf, pdf = cdf_pdf(h)
                    a_s[rows, :] = (h * cdf).astype(BF)
                    dh = (nt(g_ref[b], wd) * (cdf + h * pdf)).astype(BF)
                    dh_s[rows, :] = dh
                    dbu += jnp.sum(dh.astype(F32), axis=0, keepdims=True)
                small[pl.ds(BIAS_UP + t // 3, 1), pl.ds(pl.multiple_of(lax.rem(t, 3) * C, C), C)] = dbu

            @pl.when(t == 0)
            def _():
                for m in loads[4:]:
                    m.wait()

            tick(t, 0, t_l + 1)

            @pl.when(t < n_chunk)
            def _():
                wu = wu_ref[:, c]
                wd = wd_ref[c, :]
                dh = dh_s[...]
                a = a_s[...]
                at = lax.rem(t, 2) * (n_chunk // 2) + t // 2
                du[at] = nn(xmT[...], dh).astype(BF)
                dd[at] = tn(a, g_ref[...].reshape(T, W)).astype(BF)
                begin(mlp_pieces(t))
                y[...] += nn(a, wd)
                dxm[...] += nt(dh, wu)

            @pl.when(t == t_l)
            def _():
                store = pltpu.make_async_copy(y, y_out, s_l.at[next(local)])
                store.start()
                for b in range(ns):
                    rows = slice(b * L, (b + 1) * L)
                    xhat, rstd = norm_parts(x_ref[b].astype(F32))
                    dxa = dxm[rows, :]
                    gf = g_ref[b].astype(F32)
                    small[GAIN_M:GAIN_M + 1, :] += jnp.sum(dxa * xhat, axis=0, keepdims=True)
                    small[SHIFT_M:SHIFT_M + 1, :] += jnp.sum(dxa, axis=0, keepdims=True)
                    small[BIAS:BIAS + 1, :] += jnp.sum(gf, axis=0, keepdims=True)
                    dxm[rows, :] = gf + norm_back(dxa * row(2), xhat, rstd)
                back = pltpu.make_async_copy(dxm, gm_out, s_l.at[next(local)])
                back.start()
                store.wait()
                back.wait()

        @pl.loop(0, MOVES)
        def _(i):
            for m in moves(i):
                m.wait()
        for m in once:
            m.wait()

    def attention(wqkv, wo, wT, xaT, qkvT, kn, vn, dOT, obT, obn):
        attn, ga = kn, vn
        loads = [pltpu.make_async_copy(src, dst, s_l.at[next(local)]) for src, dst in ((wqkv_in, wqkv), (wo_in, wo))]
        for m in loads:
            m.start()
        loads[0].wait()
        for j in range(9):
            wT[j * 256:(j + 1) * 256, :] = wqkv[:, j * 256:(j + 1) * 256].T
        loads[1].wait()
        sub = lax.broadcasted_iota(jnp.int32, (L, L), 0)
        lane = lax.broadcasted_iota(jnp.int32, (L, L), 1)
        keep = sub <= lane
        rowid = lax.broadcasted_iota(jnp.int32, (128, 1), 0)

        def ga_copy(k):
            to = place.peer(k)
            return pltpu.make_async_remote_copy(
                ga.at[pl.ds(mul8(to * L), L)], ga_out.at[place.seq], s_out.at[k], r_out.at[k],
                device_id=(to, place.dp), device_id_type=MESH)

        ga_own = pltpu.make_async_copy(ga.at[me], ga_out.at[place.seq], s_out.at[0])
        attn_copy = pltpu.make_async_copy(attn, attn_out, r_out.at[0])

        def ob_copy(k, pair):
            to = place.peer(jnp.int32(k))
            cols = pl.ds(pl.multiple_of(pair * 128, 128), 128)
            return pltpu.make_async_remote_copy(
                obn.at[pl.ds(mul8(to * L), L), cols], ob_own.at[place.seq, :, cols], s_o.at[k, pair], r_o.at[k, pair],
                device_id=(to, place.dp), device_id_type=MESH)

        def unrotate(d, b):
            cos = css[b, :8, :]
            sin = css[b, 8:, :]
            return jnp.concatenate([d[:8] * cos + d[8:16] * sin, d[8:16] * cos - d[:8] * sin, d[16:]], axis=0)

        @pl.loop(t_p, end)
        def _(t):
            @pl.when(t < t_h)
            def _():
                b = t - t_p
                rows = pl.ds(pl.multiple_of(b * L, L), L)
                xhat, _ = norm_parts(xs[rows, :].astype(F32))
                xa = (xhat * row(0) + row(1)).astype(BF)
                xaT[:, rows] = xa.T
                cos = css[b, :8, :]
                sin = css[b, 8:, :]
                for j in range(9):
                    at = slice(j * 256, (j + 1) * 256)
                    bq = vec_ref[5 + j // 3:6 + j // 3, (j % 3) * 256:(j % 3 + 1) * 256]
                    m = nt(wT[at, :], xa) + jnp.broadcast_to(bq, (8, 256)).T[:, :1]
                    if j < 6:
                        parts = []
                        for h in range(4):
                            u = m[h * 64:(h + 1) * 64]
                            parts += [u[:8] * cos - u[8:16] * sin, u[8:16] * cos + u[:8] * sin, u[16:]]
                        m = jnp.concatenate(parts, axis=0)
                        if j < 3:
                            m = m * (HEAD ** -0.5)
                    mb = m.astype(BF)
                    qkvT[at, rows] = mb
                    if 3 <= j < 6:
                        kn[rows, (j - 3) * 256:(j - 2) * 256] = mb.T
                    if j >= 6:
                        vn[rows, (j - 6) * 256:(j - 5) * 256] = mb.T
                g = gs[rows, :]
                for j in range(3):
                    at = slice(j * 256, (j + 1) * 256)
                    dOT[at, rows] = nt(wo[at, :], g).astype(BF)

            @pl.when((t >= t_h) & (t < t_g))
            def _():
                head = t - t_h
                pair = head // 2
                r0 = pl.multiple_of(pair * 128, 128)
                cols = pl.ds(r0, 128)
                hr = pl.ds(pl.multiple_of(head * 64, 64), 64)
                kr = pl.ds(pl.multiple_of(W + head * 64, 64), 64)
                vr = pl.ds(pl.multiple_of(2 * W + head * 64, 64), 64)
                msk = rowid // 64 == lax.rem(head, 2)
                dk = [None] * ns
                dv = [None] * ns
                dq = [None] * ns
                for i in range(ns):
                    n = (i + 1) * L
                    qs = slice(i * L, (i + 1) * L)
                    qT2 = jnp.where(msk, qkvT[cols, qs], 0).astype(BF)
                    dO2 = jnp.where(msk, dOT[cols, qs], 0).astype(BF)
                    s = nn(kn[0:n, cols], qT2)
                    d = jnp.where(keep, s[n - L:], NEGATIVE)
                    s = jnp.concatenate([s[:n - L], d], axis=0) if i > 0 else d
                    e = jnp.exp(s - jnp.max(s, axis=0, keepdims=True))
                    inv = 1.0 / jnp.sum(e, axis=0, keepdims=True)
                    p = e.astype(BF)
                    oT = nn(qkvT[vr, 0:n], p) * inv
                    dO = dOT[hr, qs].astype(F32)
                    delta = jnp.sum(dO * oT, axis=0, keepdims=True)
                    obT[hr, qs] = oT.astype(BF)
                    dp = nn(vn[0:n, cols], dO2)
                    ds = (e * ((dp - delta) * inv)).astype(BF)
                    dq[i] = nn(qkvT[kr, 0:n], ds) * (HEAD ** -0.5)
                    dkT = nt(qkvT[hr, qs], ds)
                    dvT = nt((dO * inv).astype(BF), p)
                    for b in range(i + 1):
                        sl = slice(b * L, (b + 1) * L)
                        dk[b] = dkT[:, sl] if dk[b] is None else dk[b] + dkT[:, sl]
                        dv[b] = dvT[:, sl] if dv[b] is None else dv[b] + dvT[:, sl]
                for b in range(ns):
                    sl = slice(b * L, (b + 1) * L)
                    qkvT[hr, sl] = unrotate(dq[b], b).astype(BF)
                    qkvT[kr, sl] = unrotate(dk[b], b).astype(BF)
                    qkvT[vr, sl] = dv[b].astype(BF)

            @pl.when((t >= t_g) & (t < t_s))
            def _():
                k = t_s - 1 - t
                b = place.peer(k)
                rows = pl.ds(pl.multiple_of(b * L, L), L)
                dxa = nn(wqkv[...], qkvT[:, rows]).T
                xhat, rstd = norm_parts(xs[rows, :].astype(F32))
                small[GAIN_A:GAIN_A + 1, :] += jnp.sum(dxa * xhat, axis=0, keepdims=True)
                small[SHIFT_A:SHIFT_A + 1, :] += jnp.sum(dxa, axis=0, keepdims=True)
                ga[rows, :] = norm_back(dxa * row(0), xhat, rstd).astype(BF)

                @pl.when(k == 0)
                def _():
                    ga_own.start()

            tick(t, t_p, end)
            for i, later in enumerate(GA_SENDS):
                @pl.when(t == t_g + later)
                def _():
                    ga_copy(jnp.int32(ns - 1 - i)).start()

            @pl.when((t >= t_h) & (t < t_g) & (lax.rem(t - t_h + HEADS, 2) == 1))
            def _():
                pair = (t - t_h) // 2
                r0 = pl.multiple_of(pair * 128, 128)
                cols = pl.ds(r0, 128)
                obn[:, cols] = obT[cols, :].T
                for k in range(ns - 1, 0, -1):
                    ob_copy(k, pair).start()
                dm = jnp.concatenate([qkvT[cols, :], qkvT[pl.ds(W + r0, 128), :], qkvT[pl.ds(2 * W + r0, 128), :]], axis=0)
                da[pair, :384, :] = nt(dm, xaT[...]).astype(BF)
                da[pair, 384:, :] = nn(obT[cols, :], gs[...]).astype(BF)
                begin(attn_pieces(pair))
                db = nt(jnp.ones((8, T), BF), dm)
                for i in range(3):
                    small[BIAS_QKV + i:BIAS_QKV + i + 1, cols] = db[0:1, i * 128:(i + 1) * 128]

            @pl.when(t == t_e)
            def _():
                for k in range(1, ns):
                    for i in range(pairs):
                        ob_copy(k, i).wait()

            @pl.when((t >= t_e) & (t < t_e + ns))
            def _():
                b = t - t_e

                @pl.when(b == place.seq)
                def _():
                    ob_own[b] = obn[me, :]
                attn[pl.ds(pl.multiple_of(b * L, L), L), :] = nn(ob_own[b], wo[...]).astype(BF)

            @pl.when(t == t_e + ns - 1)
            def _():
                attn_copy.start()

        for k in range(ns - 1, 0, -1):
            ga_copy(jnp.int32(k)).wait()
        ga_own.wait()
        attn_copy.wait()
        small_out[...] = small[...]

    V = pltpu.VMEM
    FF = n_chunk * C
    pl.run_scoped(feed_forward, V((W, FF), BF), V((FF, W), BF), V((ns, L, W), BF), V((ns, L, W), BF), V((T, W), BF),
                  V((W, T), BF), V((T, W), F32), V((T, W), F32), V((T, C), BF), V((T, C), BF))
    pl.run_scoped(attention, V((W, 3 * W), BF), V((W, W), BF), V((3 * W, W), BF), V((W, T), BF), V((3 * W, T), BF), V((T, W), BF), V((T, W), BF),
                  V((W, T), BF), V((W, T), BF), V((T, W), BF))


def layer_call(sizes, x, g, cs, vecs, wu, wd, wqkv, wo):
    ns, L, W = x.shape
    T = ns * L
    FF = wu.shape[1]
    C = CHUNK
    n = FF // C
    pairs, R = HEADS // 2, 4 * 2 * HEAD
    steps = sum(s.bit_length() - 1 for s in sizes)
    vm = pl.BlockSpec(memory_space=pltpu.VMEM)
    hbm = pl.BlockSpec(memory_space=pl.ANY)
    S = jax.ShapeDtypeStruct
    V = pltpu.VMEM
    dma = pltpu.SemaphoreType.DMA
    la = Halving.land(R // 2, steps)
    return pl.pallas_call(
        functools.partial(layer_kernel, sizes),
        out_shape=(S((T, W), F32), S((T, W), F32), S((n, W, C), BF), S((n, C, W), BF), S((pairs, R, W), BF),
                   S((T, W), BF), S((ns, L, W), BF), S((SMALL, W), F32)),
        in_specs=[hbm, hbm, vm] + [vm] * 8 + [hbm] * 4, out_specs=(hbm,) * 7 + (vm,),
        scratch_shapes=[V((n, W, C), BF), V((n, C, W), BF), V((n, Halving.land(W, steps), C), BF),
                        V((n, Halving.land(C, steps), W), BF), V((pairs, R, W), BF), V((pairs, la, W), BF),
                        V((pairs, la, W), BF), V((T, W), BF), V((T, W), BF), V(cs.shape, F32), V((ns, L, W), BF), V((SMALL, W), F32), V((SMALL, W), F32), V((steps, 4, SMALL, W), F32)]
        + [dma((n, steps))] * 4 + [dma((pairs, steps))] * 4 + [dma((2 * SPLIT_M, steps))] * 4 + [dma((3, steps))] * 4
        + [dma((2, ns, MOVES))] * 2 + [dma((ns,))] * 2 + [dma((ns, pairs))] * 2 + [dma((ns,))] * 2 + [dma((steps, 4))] * 2 + [dma((48,))],
        compiler_params=pltpu.CompilerParams(vmem_limit_bytes=63 << 20, collective_id=0, has_side_effects=True),
    )(x, g, cs, *vecs, wu, wd, wqkv, wo)


def finish_kernel(du, dd, da, y, gm, attn, ga, small, dwu, dwd, dwqkv, ddw, out, grad, s0, s1, s2, s3, s4, s4b, s5, s8,
                  vu, vd, va, ou, od, oq, ow, vy, vm, vo, vg, s_in, s_out):
    n, W, C = du.shape
    pairs = da.shape[0]
    ins, outs = [], []

    def fetch(src, dst):
        c = pltpu.make_async_copy(src, dst, s_in.at[len(ins)])
        ins.append(c)
        c.start()
        return c

    def store(src, dst):
        c = pltpu.make_async_copy(src, dst, s_out.at[len(outs)])
        outs.append(c)
        c.start()

    fu = [fetch(du.at[i], vu.at[i]) for i in range(n)]
    fd = [fetch(dd.at[i], vd.at[i]) for i in range(n)]
    fa = [fetch(da.at[i], va.at[i]) for i in range(pairs)]
    fy = [fetch(a, b) for a, b in ((y, vy), (attn, vo), (gm, vm), (ga, vg))]
    for i, v in ((GAIN_A, s0), (SHIFT_A, s1), (GAIN_M, s2), (SHIFT_M, s3), (BIAS, s4), (BIAS, s4b)):
        v[...] = small[i, :]
    for i in range(3):
        s5[i * W:(i + 1) * W] = small[BIAS_QKV + i, :]
    for i in range(n * C // W):
        s8[i * W:(i + 1) * W] = small[BIAS_UP + i, :]
    for i in range(n):
        j = 2 * i if i < n // 2 else 2 * (i - n // 2) + 1
        c = slice(j * C, (j + 1) * C)
        fu[i].wait()
        ou[:, c] = vu[i].astype(F32)
        store(ou.at[:, c], dwu.at[:, c])
        fd[i].wait()
        od[c, :] = vd[i].astype(F32)
        store(od.at[c, :], dwd.at[c, :])
    for i in range(pairs):
        fa[i].wait()
        for k in range(3):
            c = slice(k * W + i * 128, k * W + (i + 1) * 128)
            oq[:, c] = va[i, k * 128:(k + 1) * 128, :].astype(F32).T
            store(oq.at[:, c], dwqkv.at[:, c])
        c = slice(i * 128, (i + 1) * 128)
        ow[c, :] = va[i, 384:, :].astype(F32)
        store(ow.at[c, :], ddw.at[c, :])
    for f in fy:
        f.wait()
    vo[...] = (vy[...] + vo[...].astype(F32)).astype(BF)
    store(vo, out)
    vg[...] = (vm[...] + vg[...].astype(F32)).astype(BF)
    store(vg, grad)
    for c in outs:
        c.wait()


def finish_call(du, dd, da, y, gm, attn, ga, small):
    n, W, C = du.shape
    pairs = da.shape[0]
    FF = n * C
    tokens = y.shape[0]
    vm = pl.BlockSpec(memory_space=pltpu.VMEM)
    hbm = pl.BlockSpec(memory_space=pl.ANY)
    S = jax.ShapeDtypeStruct
    V = pltpu.VMEM
    dma = pltpu.SemaphoreType.DMA
    return pl.pallas_call(
        finish_kernel,
        out_shape=(S((W, FF), F32), S((FF, W), F32), S((W, 3 * W), F32), S((W, W), F32), S((tokens, W), BF), S((tokens, W), BF))
        + (S((W,), F32),) * 6 + (S((3 * W,), F32), S((FF,), F32)),
        in_specs=[hbm] * 7 + [vm], out_specs=(hbm,) * 6 + (vm,) * 8,
        scratch_shapes=[V(du.shape, BF), V(dd.shape, BF), V(da.shape, BF), V((W, FF), F32), V((FF, W), F32),
                        V((W, 3 * W), F32), V((W, W), F32), V((tokens, W), F32), V((tokens, W), F32),
                        V((tokens, W), BF), V((tokens, W), BF), dma((2 * n + pairs + 4,)), dma((2 * n + 4 * pairs + 2,))],
        compiler_params=pltpu.CompilerParams(vmem_limit_bytes=63 << 20),
    )(du, dd, da, y, gm, attn, ga, small)


def on_device(hidden_in, positions, attn_gain, attn_shift, qkv_weight, qkv_bias, dense_weight, dense_bias,
              mlp_gain, mlp_shift, up_weight, up_bias, down_weight, down_bias, out_grad):
    sentences, local_len, W = hidden_in.shape
    sizes = (lax.axis_size("seq"), lax.axis_size("dp"))
    assert sentences == sizes[0]
    freqs = jnp.power(10000.0, -2.0 * jnp.arange(ROT // 2, dtype=F32) / ROT)
    angles = freqs[:, None] * positions.astype(F32)[:, None, :]
    cs = jnp.concatenate([jnp.cos(angles), jnp.sin(angles)], axis=1)
    vecs = (attn_gain, attn_shift, mlp_gain, mlp_shift, dense_bias, down_bias, qkv_bias, up_bias)
    y, gm, du, dd, da, attn, ga, small = layer_call(
        sizes, hidden_in, out_grad, cs, vecs, up_weight, down_weight, qkv_weight, dense_weight)
    dwu, dwd, dwqkv, ddw, layer_out, input_grad, s0, s1, s2, s3, s4, s4b, s5, s8 = finish_call(
        du, dd, da, y, gm, attn, ga.reshape(-1, W), small)
    return (layer_out.reshape(hidden_in.shape), input_grad.reshape(hidden_in.shape), s0, s1, dwqkv, s5, ddw, s4, s2, s3,
            dwu, s8, dwd, s4b)


def solution(mesh):
    act, rep = P("dp", "seq", None), P()
    return jax.shard_map(
        on_device, mesh=mesh,
        in_specs=(act, P("dp", "seq")) + (rep,) * 12 + (act,),
        out_specs=(act, act) + (rep,) * 12,
        check_vma=False)
```

```python
import functools
import jax
import jax.numpy as jnp
from jax import lax
from jax.experimental import pallas as pl
from jax.experimental.pallas import tpu as pltpu
from jax.sharding import PartitionSpec as P

HEADS = 12
HEAD = 64
ROT = 16
EPSILON = 1e-05
NEGATIVE = -1e30
BF, F32 = jnp.bfloat16, jnp.float32
MESH = pl.DeviceIdType.MESH
CHUNK = 256
MOVES = 8


def nn(a, b):
    return lax.dot_general(a, b, (((1,), (0,)), ((), ())), preferred_element_type=F32)


def nt(a, b):
    return lax.dot_general(a, b, (((1,), (1,)), ((), ())), preferred_element_type=F32)


def tn(a, b):
    return lax.dot_general(a, b, (((0,), (0,)), ((), ())), preferred_element_type=F32)


def norm_parts(x):
    center = x - jnp.mean(x, axis=-1, keepdims=True)
    rstd = lax.rsqrt(jnp.mean(center * center, axis=-1, keepdims=True) + EPSILON)
    return center * rstd, rstd


def norm_back(grad, xhat, rstd):
    return rstd * (grad - jnp.mean(grad, axis=-1, keepdims=True) - xhat * jnp.mean(grad * xhat, axis=-1, keepdims=True))


def cdf_pdf(h):
    t = 1.0 / (1.0 + (0.3275911 * 0.5 ** 0.5) * jnp.abs(h))
    ez = jnp.exp(-0.5 * h * h)
    poly = t * (0.5 * 0.254829592 + t * (0.5 * -0.284496736 + t * (
        0.5 * 1.421413741 + t * (0.5 * -1.453152027 + t * (0.5 * 1.061405429)))))
    tail = poly * ez
    return jnp.where(h >= 0, 1.0 - tail, tail), ez * 0.3989422804014327


def mul8(v):
    return pl.multiple_of(v, 16)


class Place:
    def __init__(self, sizes):
        self.seq_n, self.dp_n = sizes
        self.seq = lax.axis_index("seq")
        self.dp = lax.axis_index("dp")
        self.seq_bits, self.dp_bits = [], []
        for b in range(self.seq_n.bit_length() - 1):
            mine = lax.rem(self.seq // (1 << b), 2)
            self.seq_bits.append((mine, (self.seq + (1 << b) * (1 - 2 * mine), self.dp)))
        for b in range(self.dp_n.bit_length() - 1):
            mine = lax.rem(self.dp // (1 << b), 2)
            self.dp_bits.append((mine, (self.seq, self.dp + (1 << b) * (1 - 2 * mine))))
        self.core, self.dp_bits = self.dp_bits[:1], self.dp_bits[1:]

    def order(self, name):
        seq = self.seq_bits[::-1] if name.endswith("r") else self.seq_bits
        name = name.rstrip("r")
        first, then = (seq, self.dp_bits) if name[0] == "s" else (self.dp_bits, seq)
        if len(name) == 1:
            return self.core + first + then
        n = min(len(first), len(then))
        return self.core + [b for two in zip(first, then) for b in two] + first[n:] + then[n:]

    def mix(self, names, turn):
        at = [jnp.where(turn == i, 1, 0) for i in range(len(names))]
        orders = [self.order(name) for name in names]
        return [(sum(w * o[i][0] for w, o in zip(at, orders)),
                 (sum(w * o[i][1][0] for w, o in zip(at, orders)), sum(w * o[i][1][1] for w, o in zip(at, orders))))
                for i in range(len(orders[0]))]

    def peer(self, k):
        at = self.seq
        for b, (mine, _) in enumerate(self.seq_bits):
            at = at + (1 << b) * lax.rem(k // (1 << b), 2) * (1 - 2 * mine)
        return at

    def others(self, bits):
        out = []
        for c in range(1, 1 << len(bits)):
            sq, dp = self.seq, self.dp
            for j, (_, other) in enumerate(bits):
                if c >> j & 1:
                    sq, dp = sq + other[0] - self.seq, dp + other[1] - self.dp
            out.append((sq, dp))
        return out

    def targets(self):
        targets = [(self.peer(jnp.int32(k)), self.dp) for k in range(1, self.seq_n)]
        targets += [bit[1] for bit in self.core]
        for i in range(0, len(self.dp_bits), 2):
            targets += self.others(self.dp_bits[i:i + 2])
        return targets

    def signal(self):
        bar = pltpu.get_barrier_semaphore()
        for t in self.targets():
            pl.semaphore_signal(bar, inc=1, device_id=t, device_id_type=MESH)

    def enter(self):
        pl.semaphore_wait(pltpu.get_barrier_semaphore(), len(self.targets()))


class Halving:
    def __init__(self, rows, bits):
        self.plan = []
        lo, n, off = 0, rows, 0
        for mine, partner in bits:
            halve = n % 32 == 0
            part = n // 2 if halve else n
            keep = lo + mine * part if halve else lo
            give = lo + (1 - mine) * part if halve else lo
            self.plan.append((partner, halve, part, keep, give, off))
            lo, n, off = keep, part, off + part
        self.lo, self.n = lo, n

    @staticmethod
    def land(rows, count):
        n, off = rows, 0
        for _ in range(count):
            n = n // 2 if n % 32 == 0 else n
            off += n
        return off

    def copy(self, i, buf, land, send, recv):
        partner, _, part, _, give, off = self.plan[i]
        return pltpu.make_async_remote_copy(
            buf.at[pl.ds(mul8(give), part)], land.at[pl.ds(off, part)], send.at[i], recv.at[i],
            device_id=partner, device_id_type=MESH)

    def finish(self, i, buf, land, send, recv):
        self.copy(i, buf, land, send, recv).wait()
        _, _, part, keep, _, off = self.plan[i]
        rows = pl.ds(mul8(keep), part)
        buf[rows] = buf[rows] + land[pl.ds(off, part)]

    def own(self, lo=0):
        return (slice(None), pl.ds(mul8(lo + self.lo), self.n))

    def chain(self, buf, send, recv):
        ops = []
        for i in reversed(range(len(self.plan))):
            partner, halve, part, keep, _, _ = self.plan[i]
            if halve:
                at = (slice(None), pl.ds(mul8(keep), part))
                ops.append(pltpu.make_async_remote_copy(
                    buf.at[at], buf.at[at], send.at[i], recv.at[i], device_id=partner, device_id_type=MESH))
        return ops


def advance(ops, k):
    if k > 0:
        ops[k - 1].wait()
    if k < len(ops):
        ops[k].start()


ENDS_M = (1, 3, 6, 9, 12, 13, 14)
ENDS_A = (1, 3, 6, 9, 11, 12, 13)
ENDS_L = (1, 2, 4, 5, 7, 8, 9)
UP, DOWN = ('zs', 'szr'), ('z', 's')
LEFT, RIGHT = ('sr', 'sz', 'sr'), ('s', 'szr', 's')
GAPS_U, GAPS_D, GAPS_A, GAPS_L = (3, 2, 4, 2, 4), (3, 2, 4, 3, 2), (2, 2, 2, 1), (1, 1, 2, 2)
WAIT_A = (2, 0, 0)
GA_SENDS = (1, 4, 4)
SMALL_TICKS = (0, 2, 4, 6)
SPLIT_M = 3
GAIN_A, SHIFT_A, GAIN_M, SHIFT_M, BIAS, BIAS_QKV, BIAS_UP = 0, 1, 2, 3, 4, 5, 8
SMALL = 16


def layer_kernel(sizes, x_in, g_in, cs_ref, ga_v, sa_v, gm_v, sm_v, bo_v, bd_v, bq_v, bu_v, wu_in, wd_in, wqkv_in, wo_in,
                 y_out, gm_out, du_out, dd_out, da_out, attn_out, ga_out, small_out,
                 du, dd, land_u, land_d, da, land_x, land_y, xs, gs, css, ob_own, vec_ref, small, land_s,
                 su, ru, sd, rd, sx, rx, sy, ry, s_u, r_u, s_d, r_d, s_x, r_x, s_y, r_y,
                 s_in, r_in, s_c, r_c, s_o, r_o, s_out, r_out, s_s, r_s, s_l):
    place = Place(sizes)
    ns = place.seq_n
    _, L, W = x_in.shape
    T = ns * L
    n_chunk, _, C = du.shape
    pairs, R, _ = da.shape
    H2 = R // 2
    steps = len(place.order("s"))
    last_m = ENDS_M[steps - 1]
    t_l = n_chunk
    t_p = t_l + 1
    t_h = t_p + ns
    t_g = t_h + HEADS
    t_s = t_g + ns
    t_e = t_s
    local = iter(range(100))
    place.signal()

    def mlp_pieces(p):
        at = lax.rem(p, 2) * (n_chunk // 2) + p // 2
        hu = Halving(W, place.mix(UP, lax.rem(p, 2)))
        hd = Halving(C, place.mix(DOWN, lax.rem(p, 2)))
        return ((hu, (du.at[at], land_u.at[at], su.at[at], ru.at[at])),
                (hd, (dd.at[at], land_d.at[at], sd.at[at], rd.at[at])))

    def attn_pieces(p):
        hx = Halving(H2, place.mix(LEFT, p // 2))
        hy = Halving(H2, place.mix(RIGHT, p // 2))
        return ((hx, (da.at[p, pl.ds(0, H2)], land_x.at[p], sx.at[p], rx.at[p])),
                (hy, (da.at[p, pl.ds(H2, H2)], land_y.at[p], sy.at[p], ry.at[p])))

    def begin(pieces):
        for h, refs in pieces:
            h.copy(0, *refs).start()

    def halve(pieces, s):
        for h, refs in pieces:
            h.finish(s, *refs)
            if s + 1 < steps:
                h.copy(s + 1, *refs).start()

    plan = {}

    def spread(at, srcs):
        for h, src, dst, lo, send, recv, gaps in srcs:
            sem = s_l.at[next(local)]
            own = pltpu.make_async_copy(src.at[h.own(lo)], dst.at[h.own(lo)], sem)
            view = dst.at[:, pl.ds(lo, H2)] if src.shape[1] == R else dst
            ops = h.chain(view, send, recv)
            t = at
            plan.setdefault(t, []).append(own.start)
            t += 1
            plan.setdefault(t, []).append(own.wait)
            for k in range(len(ops) + 1):
                plan.setdefault(t, []).append(functools.partial(advance, ops, k))
                t += gaps[min(k, len(gaps) - 1)]

    half = n_chunk // 2
    third = half // SPLIT_M
    for gi in range(2 * SPLIT_M):
        turn, lo = gi // SPLIT_M, (gi % SPLIT_M) * third
        made = 2 * (lo + third - 1) + turn
        grp = pl.ds(turn * half + lo, third)
        hu = Halving(W, place.order(UP[turn]))
        hd = Halving(C, place.order(DOWN[turn]))
        spread(made + last_m, ((hu, du.at[grp], du_out.at[grp], 0, s_u.at[gi], r_u.at[gi], GAPS_U),
                               (hd, dd.at[grp], dd_out.at[grp], 0, s_d.at[gi], r_d.at[gi], GAPS_D)))
    for gi in range(3):
        grp = pl.ds(2 * gi, 2)
        made = t_h + 4 * gi + 3
        late = gi == 2
        hx = Halving(H2, place.order(LEFT[gi]))
        hy = Halving(H2, place.order(RIGHT[gi]))
        gaps = GAPS_L if late else GAPS_A
        spread(made + (ENDS_L if late else ENDS_A)[steps - 1] + WAIT_A[gi],
               ((hx, da.at[grp], da_out.at[grp], 0, s_x.at[gi], r_x.at[gi], gaps),
                (hy, da.at[grp], da_out.at[grp], H2, s_y.at[gi], r_y.at[gi], gaps)))
    rounds = [place.core] + [bits[i:i + 2] for bits in (place.seq_bits, place.dp_bits) for i in range(0, len(bits), 2)]

    def small_copies(i):
        return [pltpu.make_async_remote_copy(small, land_s.at[i, c + 1], s_s.at[i, c + 1], r_s.at[i, c + 1],
                                             device_id=to, device_id_type=MESH)
                for c, to in enumerate(place.others(rounds[i]))]

    def small_round(i):
        if i > 0:
            bits = rounds[i - 1]
            for m in small_copies(i - 1):
                m.wait()
            parts = {0: small[...]}
            parts.update({c: land_s[i - 1, c] for c in range(1, 1 << len(bits))})
            for j in range(len(bits)):
                parts = {c: parts[c] + parts[c | 1 << j] for c in parts if not c >> j & 1}
            small[...] = parts[0]
        if i < len(rounds):
            for m in small_copies(i):
                m.start()

    assert all(len(bits) <= 2 for bits in rounds)
    for i in range(len(rounds) + 1):
        plan.setdefault(t_s + (SMALL_TICKS[i] if len(rounds) == 3 else i), []).append(functools.partial(small_round, i))
    end = max(max(plan), t_g + max(GA_SENDS)) + 1
    assert ns == len(GA_SENDS) + 1 and pairs == 6

    def tick(t, lo, hi):
        for s in range(steps):
            p = t - ENDS_M[s]

            @pl.when((p >= 0) & (p < n_chunk))
            def _():
                halve(mlp_pieces(p), s)
        if hi > t_h:
            for s in range(steps):
                for ends, first, end in ((ENDS_A, 0, 2 * pairs - 4), (ENDS_L, 2 * pairs - 4, 2 * pairs)):
                    q = t - t_h - 1 - ends[s]

                    @pl.when((q >= first) & (q < end) & (lax.rem(q + 2 * pairs, 2) == 0))
                    def _():
                        halve(attn_pieces(q // 2), s)
        for at in range(lo, hi):
            if at in plan:
                @pl.when(t == at)
                def _():
                    for act in plan[at]:
                        act()

    part = L // MOVES

    def moves(i):
        out = []
        for a, (src, dst) in enumerate(((x_in, xs), (g_in, gs))):
            for k in range(ns - 1, 0, -1):
                to = place.peer(jnp.int32(k))
                out.append(pltpu.make_async_remote_copy(
                    src.at[to, pl.ds(mul8(i * part), part)], dst.at[pl.ds(mul8(place.seq * L + i * part), part)],
                    s_in.at[a, k, i], r_in.at[a, k, i], device_id=(to, place.dp), device_id_type=MESH))
        return out

    once = []
    me = pl.ds(mul8(place.seq * L), L)
    for k in range(ns - 1, 0, -1):
        to = place.peer(jnp.int32(k))
        once.append(pltpu.make_async_remote_copy(
            cs_ref.at[to], css.at[place.seq], s_c.at[k], r_c.at[k], device_id=(to, place.dp), device_id_type=MESH))
    for src, dst in ((x_in, xs.at[me]), (g_in, gs.at[me]), (cs_ref, css.at[place.seq])):
        once.append(pltpu.make_async_copy(src.at[place.seq], dst, s_l.at[next(local)]))


    def row(i):
        return vec_ref[i:i + 1, :]

    def feed_forward(wu_ref, wd_ref, x_ref, g_ref, xm, xmT, dxm, y, a_s, dh_s):
        head, rest = pl.ds(0, C), pl.ds(C, FF - C)
        loads = [pltpu.make_async_copy(src, dst, s_l.at[next(local)])
                 for src, dst in ((x_in, x_ref), (g_in, g_ref), (wu_in.at[:, head], wu_ref.at[:, head]),
                                  (wd_in.at[head], wd_ref.at[head]), (wu_in.at[:, rest], wu_ref.at[:, rest]),
                                  (wd_in.at[rest], wd_ref.at[rest]))]
        for m in loads:
            m.start()
        for i, v in enumerate((ga_v, sa_v, gm_v, sm_v)):
            vec_ref[i:i + 1, :] = v[...].reshape(1, W)
        vec_ref[4:5, :] = (bo_v[...] + bd_v[...]).reshape(1, W)
        for i in range(3):
            vec_ref[5 + i:6 + i, :] = bq_v[i * W:(i + 1) * W].reshape(1, W)
        for i in range(FF // W):
            vec_ref[8 + i:9 + i, :] = bu_v[i * W:(i + 1) * W].reshape(1, W)
        loads[0].wait()
        small[...] = jnp.zeros_like(small)
        for b in range(ns):
            rows = slice(b * L, (b + 1) * L)
            x = x_ref[b].astype(F32)
            xhat, _ = norm_parts(x)
            v = (xhat * row(2) + row(3)).astype(BF)
            xm[rows, :] = v
            xmT[:, rows] = v.T
            y[rows, :] = x + row(4)
        dxm[...] = jnp.zeros_like(dxm)
        place.enter()
        for m in once + moves(0):
            m.start()
        for m in loads[1:4]:
            m.wait()

        @pl.loop(0, t_l + 1)
        def _(t):
            c = pl.ds(pl.multiple_of(jnp.minimum(t, n_chunk - 1) * C, C), C)

            @pl.when((t > 0) & (t < 4) | (t > 4) & (t < 2 * MOVES - 4) & (lax.rem(t, 2) == 1))
            def _():
                for m in moves(jnp.where(t < 4, t, (t + 3) // 2)):
                    m.start()

            @pl.when(t < n_chunk)
            def _():
                wu = wu_ref[:, c]
                wd = wd_ref[c, :]
                bu = vec_ref[pl.ds(8 + t // 3, 1), pl.ds(pl.multiple_of(lax.rem(t, 3) * C, C), C)]
                dbu = jnp.zeros((1, C), F32)
                for b in range(ns):
                    rows = slice(b * L, (b + 1) * L)
                    h = nn(xm[rows, :], wu) + bu
                    cdf, pdf = cdf_pdf(h)
                    a_s[rows, :] = (h * cdf).astype(BF)
                    dh = (nt(g_ref[b], wd) * (cdf + h * pdf)).astype(BF)
                    dh_s[rows, :] = dh
                    dbu += jnp.sum(dh.astype(F32), axis=0, keepdims=True)
                small[pl.ds(BIAS_UP + t // 3, 1), pl.ds(pl.multiple_of(lax.rem(t, 3) * C, C), C)] = dbu

            @pl.when(t == 0)
            def _():
                for m in loads[4:]:
                    m.wait()

            tick(t, 0, t_l + 1)

            @pl.when(t < n_chunk)
            def _():
                wu = wu_ref[:, c]
                wd = wd_ref[c, :]
                dh = dh_s[...]
                a = a_s[...]
                at = lax.rem(t, 2) * (n_chunk // 2) + t // 2
                du[at] = nn(xmT[...], dh).astype(BF)
                dd[at] = tn(a, g_ref[...].reshape(T, W)).astype(BF)
                begin(mlp_pieces(t))
                y[...] += nn(a, wd)
                dxm[...] += nt(dh, wu)

            @pl.when(t == t_l)
            def _():
                for b in range(ns):
                    rows = slice(b * L, (b + 1) * L)
                    xm[rows, :] = y[rows, :].astype(BF)
                store = pltpu.make_async_copy(xm, y_out, s_l.at[next(local)])
                store.start()
                for b in range(ns):
                    rows = slice(b * L, (b + 1) * L)
                    xhat, rstd = norm_parts(x_ref[b].astype(F32))
                    dxa = dxm[rows, :]
                    gf = g_ref[b].astype(F32)
                    small[GAIN_M:GAIN_M + 1, :] += jnp.sum(dxa * xhat, axis=0, keepdims=True)
                    small[SHIFT_M:SHIFT_M + 1, :] += jnp.sum(dxa, axis=0, keepdims=True)
                    small[BIAS:BIAS + 1, :] += jnp.sum(gf, axis=0, keepdims=True)
                    x_ref[b] = (gf + norm_back(dxa * row(2), xhat, rstd)).astype(BF)
                back = pltpu.make_async_copy(x_ref, gm_out, s_l.at[next(local)])
                back.start()
                store.wait()
                back.wait()

        @pl.loop(0, MOVES)
        def _(i):
            for m in moves(i):
                m.wait()
        for m in once:
            m.wait()

    def attention(wqkv, wo, wT, xaT, qkvT, kn, vn, dOT, obT, obn):
        attn, ga = kn, vn
        loads = [pltpu.make_async_copy(src, dst, s_l.at[next(local)]) for src, dst in ((wqkv_in, wqkv), (wo_in, wo))]
        for m in loads:
            m.start()
        loads[0].wait()
        for j in range(9):
            wT[j * 256:(j + 1) * 256, :] = wqkv[:, j * 256:(j + 1) * 256].T
        loads[1].wait()
        sub = lax.broadcasted_iota(jnp.int32, (L, L), 0)
        lane = lax.broadcasted_iota(jnp.int32, (L, L), 1)
        keep = sub <= lane
        rowid = lax.broadcasted_iota(jnp.int32, (128, 1), 0)

        def ga_copy(k):
            to = place.peer(k)
            return pltpu.make_async_remote_copy(
                ga.at[pl.ds(mul8(to * L), L)], ga_out.at[place.seq], s_out.at[k], r_out.at[k],
                device_id=(to, place.dp), device_id_type=MESH)

        ga_own = pltpu.make_async_copy(ga.at[me], ga_out.at[place.seq], s_out.at[0])
        attn_copy = pltpu.make_async_copy(attn, attn_out, r_out.at[0])

        def ob_copy(k, pair):
            to = place.peer(jnp.int32(k))
            cols = pl.ds(pl.multiple_of(pair * 128, 128), 128)
            return pltpu.make_async_remote_copy(
                obn.at[pl.ds(mul8(to * L), L), cols], ob_own.at[place.seq, :, cols], s_o.at[k, pair], r_o.at[k, pair],
                device_id=(to, place.dp), device_id_type=MESH)

        def unrotate(d, b):
            cos = css[b, :8, :]
            sin = css[b, 8:, :]
            return jnp.concatenate([d[:8] * cos + d[8:16] * sin, d[8:16] * cos - d[:8] * sin, d[16:]], axis=0)

        @pl.loop(t_p, end)
        def _(t):
            @pl.when(t < t_h)
            def _():
                b = t - t_p
                rows = pl.ds(pl.multiple_of(b * L, L), L)
                xhat, _ = norm_parts(xs[rows, :].astype(F32))
                xa = (xhat * row(0) + row(1)).astype(BF)
                xaT[:, rows] = xa.T
                cos = css[b, :8, :]
                sin = css[b, 8:, :]
                for j in range(9):
                    at = slice(j * 256, (j + 1) * 256)
                    bq = vec_ref[5 + j // 3:6 + j // 3, (j % 3) * 256:(j % 3 + 1) * 256]
                    m = nt(wT[at, :], xa) + jnp.broadcast_to(bq, (8, 256)).T[:, :1]
                    if j < 6:
                        parts = []
                        for h in range(4):
                            u = m[h * 64:(h + 1) * 64]
                            parts += [u[:8] * cos - u[8:16] * sin, u[8:16] * cos + u[:8] * sin, u[16:]]
                        m = jnp.concatenate(parts, axis=0)
                        if j < 3:
                            m = m * (HEAD ** -0.5)
                    mb = m.astype(BF)
                    qkvT[at, rows] = mb
                    if 3 <= j < 6:
                        kn[rows, (j - 3) * 256:(j - 2) * 256] = mb.T
                    if j >= 6:
                        vn[rows, (j - 6) * 256:(j - 5) * 256] = mb.T
                g = gs[rows, :]
                for j in range(3):
                    at = slice(j * 256, (j + 1) * 256)
                    dOT[at, rows] = nt(wo[at, :], g).astype(BF)

            @pl.when((t >= t_h) & (t < t_g))
            def _():
                head = t - t_h
                pair = head // 2
                r0 = pl.multiple_of(pair * 128, 128)
                cols = pl.ds(r0, 128)
                hr = pl.ds(pl.multiple_of(head * 64, 64), 64)
                kr = pl.ds(pl.multiple_of(W + head * 64, 64), 64)
                vr = pl.ds(pl.multiple_of(2 * W + head * 64, 64), 64)
                msk = rowid // 64 == lax.rem(head, 2)
                dk = [None] * ns
                dv = [None] * ns
                dq = [None] * ns
                for i in range(ns):
                    n = (i + 1) * L
                    qs = slice(i * L, (i + 1) * L)
                    qT2 = jnp.where(msk, qkvT[cols, qs], 0).astype(BF)
                    dO2 = jnp.where(msk, dOT[cols, qs], 0).astype(BF)
                    s = nn(kn[0:n, cols], qT2)
                    d = jnp.where(keep, s[n - L:], NEGATIVE)
                    s = jnp.concatenate([s[:n - L], d], axis=0) if i > 0 else d
                    e = jnp.exp(s - jnp.max(s, axis=0, keepdims=True))
                    inv = 1.0 / jnp.sum(e, axis=0, keepdims=True)
                    p = e.astype(BF)
                    oT = nn(qkvT[vr, 0:n], p) * inv
                    dO = dOT[hr, qs].astype(F32)
                    delta = jnp.sum(dO * oT, axis=0, keepdims=True)
                    obT[hr, qs] = oT.astype(BF)
                    dp = nn(vn[0:n, cols], dO2)
                    ds = (e * ((dp - delta) * inv)).astype(BF)
                    dq[i] = nn(qkvT[kr, 0:n], ds) * (HEAD ** -0.5)
                    dkT = nt(qkvT[hr, qs], ds)
                    dvT = nt((dO * inv).astype(BF), p)
                    for b in range(i + 1):
                        sl = slice(b * L, (b + 1) * L)
                        dk[b] = dkT[:, sl] if dk[b] is None else dk[b] + dkT[:, sl]
                        dv[b] = dvT[:, sl] if dv[b] is None else dv[b] + dvT[:, sl]
                for b in range(ns):
                    sl = slice(b * L, (b + 1) * L)
                    qkvT[hr, sl] = unrotate(dq[b], b).astype(BF)
                    qkvT[kr, sl] = unrotate(dk[b], b).astype(BF)
                    qkvT[vr, sl] = dv[b].astype(BF)

            @pl.when((t >= t_g) & (t < t_s))
            def _():
                k = t_s - 1 - t
                b = place.peer(k)
                rows = pl.ds(pl.multiple_of(b * L, L), L)
                dxa = nn(wqkv[...], qkvT[:, rows]).T
                xhat, rstd = norm_parts(xs[rows, :].astype(F32))
                small[GAIN_A:GAIN_A + 1, :] += jnp.sum(dxa * xhat, axis=0, keepdims=True)
                small[SHIFT_A:SHIFT_A + 1, :] += jnp.sum(dxa, axis=0, keepdims=True)
                ga[rows, :] = norm_back(dxa * row(0), xhat, rstd).astype(BF)

                @pl.when(k == 0)
                def _():
                    ga_own.start()

            tick(t, t_p, end)
            for i, later in enumerate(GA_SENDS):
                @pl.when(t == t_g + later)
                def _():
                    ga_copy(jnp.int32(ns - 1 - i)).start()

            @pl.when((t >= t_h) & (t < t_g) & (lax.rem(t - t_h + HEADS, 2) == 1))
            def _():
                pair = (t - t_h) // 2
                r0 = pl.multiple_of(pair * 128, 128)
                cols = pl.ds(r0, 128)
                obn[:, cols] = obT[cols, :].T
                for k in range(ns - 1, 0, -1):
                    ob_copy(k, pair).start()
                dm = jnp.concatenate([qkvT[cols, :], qkvT[pl.ds(W + r0, 128), :], qkvT[pl.ds(2 * W + r0, 128), :]], axis=0)
                da[pair, :384, :] = nt(dm, xaT[...]).astype(BF)
                da[pair, 384:, :] = nn(obT[cols, :], gs[...]).astype(BF)
                begin(attn_pieces(pair))
                db = nt(jnp.ones((8, T), BF), dm)
                for i in range(3):
                    small[BIAS_QKV + i:BIAS_QKV + i + 1, cols] = db[0:1, i * 128:(i + 1) * 128]

            @pl.when(t == t_e)
            def _():
                for k in range(1, ns):
                    for i in range(pairs):
                        ob_copy(k, i).wait()

            @pl.when((t >= t_e) & (t < t_e + ns))
            def _():
                b = t - t_e

                @pl.when(b == place.seq)
                def _():
                    ob_own[b] = obn[me, :]
                attn[pl.ds(pl.multiple_of(b * L, L), L), :] = nn(ob_own[b], wo[...]).astype(BF)

            @pl.when(t == t_e + ns - 1)
            def _():
                attn_copy.start()

        for k in range(ns - 1, 0, -1):
            ga_copy(jnp.int32(k)).wait()
        ga_own.wait()
        attn_copy.wait()
        small_out[...] = small[...]

    V = pltpu.VMEM
    FF = n_chunk * C
    pl.run_scoped(feed_forward, V((W, FF), BF), V((FF, W), BF), V((ns, L, W), BF), V((ns, L, W), BF), V((T, W), BF),
                  V((W, T), BF), V((T, W), F32), V((T, W), F32), V((T, C), BF), V((T, C), BF))
    pl.run_scoped(attention, V((W, 3 * W), BF), V((W, W), BF), V((3 * W, W), BF), V((W, T), BF), V((3 * W, T), BF), V((T, W), BF), V((T, W), BF),
                  V((W, T), BF), V((W, T), BF), V((T, W), BF))


def layer_call(sizes, x, g, cs, vecs, wu, wd, wqkv, wo):
    ns, L, W = x.shape
    T = ns * L
    FF = wu.shape[1]
    C = CHUNK
    n = FF // C
    pairs, R = HEADS // 2, 4 * 2 * HEAD
    steps = sum(s.bit_length() - 1 for s in sizes)
    vm = pl.BlockSpec(memory_space=pltpu.VMEM)
    hbm = pl.BlockSpec(memory_space=pl.ANY)
    S = jax.ShapeDtypeStruct
    V = pltpu.VMEM
    dma = pltpu.SemaphoreType.DMA
    la = Halving.land(R // 2, steps)
    return pl.pallas_call(
        functools.partial(layer_kernel, sizes),
        out_shape=(S((T, W), BF), S((ns, L, W), BF), S((n, W, C), BF), S((n, C, W), BF), S((pairs, R, W), BF),
                   S((T, W), BF), S((ns, L, W), BF), S((SMALL, W), F32)),
        in_specs=[hbm, hbm, vm] + [vm] * 8 + [hbm] * 4, out_specs=(hbm,) * 7 + (vm,),
        scratch_shapes=[V((n, W, C), BF), V((n, C, W), BF), V((n, Halving.land(W, steps), C), BF),
                        V((n, Halving.land(C, steps), W), BF), V((pairs, R, W), BF), V((pairs, la, W), BF),
                        V((pairs, la, W), BF), V((T, W), BF), V((T, W), BF), V(cs.shape, F32), V((ns, L, W), BF), V((SMALL, W), F32), V((SMALL, W), F32), V((steps, 4, SMALL, W), F32)]
        + [dma((n, steps))] * 4 + [dma((pairs, steps))] * 4 + [dma((2 * SPLIT_M, steps))] * 4 + [dma((3, steps))] * 4
        + [dma((2, ns, MOVES))] * 2 + [dma((ns,))] * 2 + [dma((ns, pairs))] * 2 + [dma((ns,))] * 2 + [dma((steps, 4))] * 2 + [dma((48,))],
        compiler_params=pltpu.CompilerParams(vmem_limit_bytes=255 << 18, collective_id=0, has_side_effects=True),
    )(x, g, cs, *vecs, wu, wd, wqkv, wo)


def finish_kernel(du, dd, da, y, gm, attn, ga, small, dwu, dwd, dwqkv, ddw, out, grad, s0, s1, s2, s3, s4, s4b, s5, s8,
                  vu, vd, va, ou, od, oq, ow, vy, vm, vo, vg, s_in, s_out):
    n, W, C = du.shape
    pairs = da.shape[0]
    ins, outs = [], []

    def fetch(src, dst):
        c = pltpu.make_async_copy(src, dst, s_in.at[len(ins)])
        ins.append(c)
        c.start()
        return c

    def store(src, dst):
        c = pltpu.make_async_copy(src, dst, s_out.at[len(outs)])
        outs.append(c)
        c.start()

    fd = [fetch(dd.at[i], vd.at[i]) for i in range(n)]
    fu = [fetch(du.at[i], vu.at[i]) for i in range(n)]
    fa = [fetch(da.at[i], va.at[i]) for i in range(pairs)]
    fy = [fetch(a, b) for a, b in ((y, vy), (attn, vo), (gm, vm), (ga, vg))]
    for i, v in ((GAIN_A, s0), (SHIFT_A, s1), (GAIN_M, s2), (SHIFT_M, s3), (BIAS, s4), (BIAS, s4b)):
        v[...] = small[i, :]
    for i in range(3):
        s5[i * W:(i + 1) * W] = small[BIAS_QKV + i, :]
    for i in range(n * C // W):
        s8[i * W:(i + 1) * W] = small[BIAS_UP + i, :]

    def chunk(i):
        j = 2 * i if i < n // 2 else 2 * (i - n // 2) + 1
        return slice(j * C, (j + 1) * C)

    for i in range(n):
        c = chunk(i)
        fd[i].wait()
        od[c, :] = vd[i].astype(F32)
        store(od.at[c, :], dwd.at[c, :])
    for i in range(n):
        fu[i].wait()
        ou[:, chunk(i)] = vu[i].astype(F32)
    for i in range(8):
        rows = slice(i * W // 8, (i + 1) * W // 8)
        store(ou.at[rows], dwu.at[rows])
    for i in range(pairs):
        fa[i].wait()
        c = slice(i * 128, (i + 1) * 128)
        ow[c, :] = va[i, 384:, :].astype(F32)
        store(ow.at[c, :], ddw.at[c, :])
        for k in range(3):
            oq[:, k * W + i * 128:k * W + (i + 1) * 128] = va[i, k * 128:(k + 1) * 128, :].astype(F32).T
    for i in range(8):
        rows = slice(i * W // 8, (i + 1) * W // 8)
        store(oq.at[rows], dwqkv.at[rows])
    for f in fy:
        f.wait()
    vo[...] = (vy[...].astype(F32) + vo[...].astype(F32)).astype(BF)
    store(vo, out)
    vg[...] = (vm[...].astype(F32) + vg[...].astype(F32)).astype(BF)
    store(vg, grad)
    for c in outs:
        c.wait()


def finish_call(du, dd, da, y, gm, attn, ga, small):
    n, W, C = du.shape
    pairs = da.shape[0]
    FF = n * C
    tokens = y.shape[0]
    vm = pl.BlockSpec(memory_space=pltpu.VMEM)
    hbm = pl.BlockSpec(memory_space=pl.ANY)
    S = jax.ShapeDtypeStruct
    V = pltpu.VMEM
    dma = pltpu.SemaphoreType.DMA
    return pl.pallas_call(
        finish_kernel,
        out_shape=(S((W, FF), F32), S((FF, W), F32), S((W, 3 * W), F32), S((W, W), F32), S((tokens, W), BF), S((tokens, W), BF))
        + (S((W,), F32),) * 6 + (S((3 * W,), F32), S((FF,), F32)),
        in_specs=[hbm] * 7 + [vm], out_specs=(hbm,) * 6 + (vm,) * 8,
        scratch_shapes=[V(du.shape, BF), V(dd.shape, BF), V(da.shape, BF), V((W, FF), F32), V((FF, W), F32),
                        V((W, 3 * W), F32), V((W, W), F32), V((tokens, W), BF), V((tokens, W), BF),
                        V((tokens, W), BF), V((tokens, W), BF), dma((2 * n + pairs + 4,)), dma((2 * n + 4 * pairs + 2,))],
        compiler_params=pltpu.CompilerParams(vmem_limit_bytes=63 << 20),
    )(du, dd, da, y, gm, attn, ga, small)


def on_device(hidden_in, positions, attn_gain, attn_shift, qkv_weight, qkv_bias, dense_weight, dense_bias,
              mlp_gain, mlp_shift, up_weight, up_bias, down_weight, down_bias, out_grad):
    sentences, local_len, W = hidden_in.shape
    sizes = (lax.axis_size("seq"), lax.axis_size("dp"))
    assert sentences == sizes[0]
    freqs = jnp.power(10000.0, -2.0 * jnp.arange(ROT // 2, dtype=F32) / ROT)
    angles = freqs[:, None] * positions.astype(F32)[:, None, :]
    cs = jnp.concatenate([jnp.cos(angles), jnp.sin(angles)], axis=1)
    vecs = (attn_gain, attn_shift, mlp_gain, mlp_shift, dense_bias, down_bias, qkv_bias, up_bias)
    y, gm, du, dd, da, attn, ga, small = layer_call(
        sizes, hidden_in, out_grad, cs, vecs, up_weight, down_weight, qkv_weight, dense_weight)
    dwu, dwd, dwqkv, ddw, layer_out, input_grad, s0, s1, s2, s3, s4, s4b, s5, s8 = finish_call(
        du, dd, da, y, gm.reshape(-1, W), attn, ga.reshape(-1, W), small)
    return (layer_out.reshape(hidden_in.shape), input_grad.reshape(hidden_in.shape), s0, s1, dwqkv, s5, ddw, s4, s2, s3,
            dwu, s8, dwd, s4b)


def solution(mesh):
    act, rep = P("dp", "seq", None), P()
    return jax.shard_map(
        on_device, mesh=mesh,
        in_specs=(act, P("dp", "seq")) + (rep,) * 12 + (act,),
        out_specs=(act, act) + (rep,) * 12,
        check_vma=False)
```

```python
import functools
import jax
import jax.numpy as jnp
from jax import lax
from jax.experimental import pallas as pl
from jax.experimental.pallas import tpu as pltpu
from jax.sharding import PartitionSpec as P

HEADS = 12
HEAD = 64
ROT = 16
EPSILON = 1e-05
NEGATIVE = -1e30
BF, F32 = jnp.bfloat16, jnp.float32
MESH = pl.DeviceIdType.MESH
CHUNK = 256
MOVES = 8


def nn(a, b):
    return lax.dot_general(a, b, (((1,), (0,)), ((), ())), preferred_element_type=F32)


def nt(a, b):
    return lax.dot_general(a, b, (((1,), (1,)), ((), ())), preferred_element_type=F32)


def tn(a, b):
    return lax.dot_general(a, b, (((0,), (0,)), ((), ())), preferred_element_type=F32)


def norm_parts(x):
    center = x - jnp.mean(x, axis=-1, keepdims=True)
    rstd = lax.rsqrt(jnp.mean(center * center, axis=-1, keepdims=True) + EPSILON)
    return center * rstd, rstd


def norm_back(grad, xhat, rstd):
    return rstd * (grad - jnp.mean(grad, axis=-1, keepdims=True) - xhat * jnp.mean(grad * xhat, axis=-1, keepdims=True))


def cdf_pdf(h):
    t = 1.0 / (1.0 + (0.3275911 * 0.5 ** 0.5) * jnp.abs(h))
    ez = jnp.exp(-0.5 * h * h)
    poly = t * (0.5 * 0.254829592 + t * (0.5 * -0.284496736 + t * (
        0.5 * 1.421413741 + t * (0.5 * -1.453152027 + t * (0.5 * 1.061405429)))))
    tail = poly * ez
    return jnp.where(h >= 0, 1.0 - tail, tail), ez * 0.3989422804014327


def mul8(v):
    return pl.multiple_of(v, 16)


class Place:
    def __init__(self, sizes):
        self.seq_n, self.dp_n = sizes
        self.seq = lax.axis_index("seq")
        self.dp = lax.axis_index("dp")
        self.seq_bits, self.dp_bits = [], []
        for b in range(self.seq_n.bit_length() - 1):
            mine = lax.rem(self.seq // (1 << b), 2)
            self.seq_bits.append((mine, (self.seq + (1 << b) * (1 - 2 * mine), self.dp)))
        for b in range(self.dp_n.bit_length() - 1):
            mine = lax.rem(self.dp // (1 << b), 2)
            self.dp_bits.append((mine, (self.seq, self.dp + (1 << b) * (1 - 2 * mine))))
        self.core, self.dp_bits = self.dp_bits[:1], self.dp_bits[1:]

    def order(self, name):
        seq = self.seq_bits[::-1] if name.endswith("r") else self.seq_bits
        name = name.rstrip("r")
        first, then = (seq, self.dp_bits) if name[0] == "s" else (self.dp_bits, seq)
        if len(name) == 1:
            return self.core + first + then
        n = min(len(first), len(then))
        return self.core + [b for two in zip(first, then) for b in two] + first[n:] + then[n:]

    def mix(self, names, turn):
        at = [jnp.where(turn == i, 1, 0) for i in range(len(names))]
        orders = [self.order(name) for name in names]
        return [(sum(w * o[i][0] for w, o in zip(at, orders)),
                 (sum(w * o[i][1][0] for w, o in zip(at, orders)), sum(w * o[i][1][1] for w, o in zip(at, orders))))
                for i in range(len(orders[0]))]

    def peer(self, k):
        at = self.seq
        for b, (mine, _) in enumerate(self.seq_bits):
            at = at + (1 << b) * lax.rem(k // (1 << b), 2) * (1 - 2 * mine)
        return at

    def others(self, bits):
        out = []
        for c in range(1, 1 << len(bits)):
            sq, dp = self.seq, self.dp
            for j, (_, other) in enumerate(bits):
                if c >> j & 1:
                    sq, dp = sq + other[0] - self.seq, dp + other[1] - self.dp
            out.append((sq, dp))
        return out

    def targets(self):
        targets = [(self.peer(jnp.int32(k)), self.dp) for k in range(1, self.seq_n)]
        targets += [bit[1] for bit in self.core]
        for i in range(0, len(self.dp_bits), 2):
            targets += self.others(self.dp_bits[i:i + 2])
        return targets

    def signal(self):
        bar = pltpu.get_barrier_semaphore()
        for t in self.targets():
            pl.semaphore_signal(bar, inc=1, device_id=t, device_id_type=MESH)

    def enter(self):
        pl.semaphore_wait(pltpu.get_barrier_semaphore(), len(self.targets()))


class Halving:
    def __init__(self, rows, bits):
        self.plan = []
        lo, n, off = 0, rows, 0
        for mine, partner in bits:
            halve = n % 32 == 0
            part = n // 2 if halve else n
            keep = lo + mine * part if halve else lo
            give = lo + (1 - mine) * part if halve else lo
            self.plan.append((partner, halve, part, keep, give, off))
            lo, n, off = keep, part, off + part
        self.lo, self.n = lo, n

    @staticmethod
    def land(rows, count):
        n, off = rows, 0
        for _ in range(count):
            n = n // 2 if n % 32 == 0 else n
            off += n
        return off

    def copy(self, i, buf, land, send, recv):
        partner, _, part, _, give, off = self.plan[i]
        return pltpu.make_async_remote_copy(
            buf.at[pl.ds(mul8(give), part)], land.at[pl.ds(off, part)], send.at[i], recv.at[i],
            device_id=partner, device_id_type=MESH)

    def finish(self, i, buf, land, send, recv):
        self.copy(i, buf, land, send, recv).wait()
        _, _, part, keep, _, off = self.plan[i]
        rows = pl.ds(mul8(keep), part)
        buf[rows] = buf[rows] + land[pl.ds(off, part)]

    def own(self, lo=0):
        return (slice(None), pl.ds(mul8(lo + self.lo), self.n))

    def chain(self, buf, send, recv):
        ops = []
        for i in reversed(range(len(self.plan))):
            partner, halve, part, keep, _, _ = self.plan[i]
            if halve:
                at = (slice(None), pl.ds(mul8(keep), part))
                ops.append(pltpu.make_async_remote_copy(
                    buf.at[at], buf.at[at], send.at[i], recv.at[i], device_id=partner, device_id_type=MESH))
        return ops


def advance(ops, k):
    if k > 0:
        ops[k - 1].wait()
    if k < len(ops):
        ops[k].start()


ENDS_M = (1, 3, 6, 9, 12, 13, 14)
ENDS_A = (1, 3, 6, 9, 11, 12, 13)
ENDS_L = (1, 2, 4, 5, 7, 8, 9)
UP, DOWN = ('zs', 'szr'), ('z', 's')
LEFT, RIGHT = ('sr', 'sz', 'sr'), ('s', 'szr', 's')
GAPS_U, GAPS_D, GAPS_A, GAPS_L = (3, 2, 4, 2, 4), (3, 2, 4, 3, 2), (2, 2, 2, 1), (1, 1, 2, 2)
WAIT_A = (2, 0, 0)
GA_SENDS = (1, 4, 4)
SMALL_TICKS = (0, 2, 4, 6)
SPLIT_M = 3
GAIN_A, SHIFT_A, GAIN_M, SHIFT_M, BIAS, BIAS_QKV, BIAS_UP = 0, 1, 2, 3, 4, 5, 8
SMALL = 16


def layer_kernel(sizes, x_in, g_in, cs_ref, ga_v, sa_v, gm_v, sm_v, bo_v, bd_v, bq_v, bu_v, wu_in, wd_in, wqkv_in, wo_in,
                 y_out, gm_out, du_out, dd_out, da_out, attn_out, ga_out, small_out,
                 du, dd, land_u, land_d, da, land_x, land_y, xs, gs, css, ob_own, vec_ref, small, land_s,
                 su, ru, sd, rd, sx, rx, sy, ry, s_u, r_u, s_d, r_d, s_x, r_x, s_y, r_y,
                 s_in, r_in, s_c, r_c, s_o, r_o, s_out, r_out, s_s, r_s, s_l):
    place = Place(sizes)
    ns = place.seq_n
    _, L, W = x_in.shape
    T = ns * L
    n_chunk, _, C = du.shape
    pairs, R, _ = da.shape
    H2 = R // 2
    steps = len(place.order("s"))
    last_m = ENDS_M[steps - 1]
    t_l = n_chunk
    t_p = t_l + 1
    t_h = t_p + ns
    t_g = t_h + HEADS
    t_s = t_g + ns
    t_e = t_s
    local = iter(range(100))
    place.signal()

    def mlp_pieces(p):
        at = lax.rem(p, 2) * (n_chunk // 2) + p // 2
        hu = Halving(W, place.mix(UP, lax.rem(p, 2)))
        hd = Halving(C, place.mix(DOWN, lax.rem(p, 2)))
        return ((hu, (du.at[at], land_u.at[at], su.at[at], ru.at[at])),
                (hd, (dd.at[at], land_d.at[at], sd.at[at], rd.at[at])))

    def attn_pieces(p):
        hx = Halving(H2, place.mix(LEFT, p // 2))
        hy = Halving(H2, place.mix(RIGHT, p // 2))
        return ((hx, (da.at[p, pl.ds(0, H2)], land_x.at[p], sx.at[p], rx.at[p])),
                (hy, (da.at[p, pl.ds(H2, H2)], land_y.at[p], sy.at[p], ry.at[p])))

    def begin(pieces):
        for h, refs in pieces:
            h.copy(0, *refs).start()

    def halve(pieces, s):
        for h, refs in pieces:
            h.finish(s, *refs)
            if s + 1 < steps:
                h.copy(s + 1, *refs).start()

    plan = {}

    def spread(at, srcs):
        for h, src, dst, lo, send, recv, gaps in srcs:
            sem = s_l.at[next(local)]
            own = pltpu.make_async_copy(src.at[h.own(lo)], dst.at[h.own(lo)], sem)
            view = dst.at[:, pl.ds(lo, H2)] if src.shape[1] == R else dst
            ops = h.chain(view, send, recv)
            t = at
            plan.setdefault(t, []).append(own.start)
            t += 1
            plan.setdefault(t, []).append(own.wait)
            for k in range(len(ops) + 1):
                plan.setdefault(t, []).append(functools.partial(advance, ops, k))
                t += gaps[min(k, len(gaps) - 1)]

    half = n_chunk // 2
    third = half // SPLIT_M
    for gi in range(2 * SPLIT_M):
        turn, lo = gi // SPLIT_M, (gi % SPLIT_M) * third
        made = 2 * (lo + third - 1) + turn
        grp = pl.ds(turn * half + lo, third)
        hu = Halving(W, place.order(UP[turn]))
        hd = Halving(C, place.order(DOWN[turn]))
        spread(made + last_m, ((hu, du.at[grp], du_out.at[grp], 0, s_u.at[gi], r_u.at[gi], GAPS_U),
                               (hd, dd.at[grp], dd_out.at[grp], 0, s_d.at[gi], r_d.at[gi], GAPS_D)))
    for gi in range(3):
        grp = pl.ds(2 * gi, 2)
        made = t_h + 4 * gi + 3
        late = gi == 2
        hx = Halving(H2, place.order(LEFT[gi]))
        hy = Halving(H2, place.order(RIGHT[gi]))
        gaps = GAPS_L if late else GAPS_A
        spread(made + (ENDS_L if late else ENDS_A)[steps - 1] + WAIT_A[gi],
               ((hx, da.at[grp], da_out.at[grp], 0, s_x.at[gi], r_x.at[gi], gaps),
                (hy, da.at[grp], da_out.at[grp], H2, s_y.at[gi], r_y.at[gi], gaps)))
    rounds = [place.core] + [bits[i:i + 2] for bits in (place.seq_bits, place.dp_bits) for i in range(0, len(bits), 2)]

    def small_copies(i):
        return [pltpu.make_async_remote_copy(small, land_s.at[i, c + 1], s_s.at[i, c + 1], r_s.at[i, c + 1],
                                             device_id=to, device_id_type=MESH)
                for c, to in enumerate(place.others(rounds[i]))]

    def small_round(i):
        if i > 0:
            bits = rounds[i - 1]
            for m in small_copies(i - 1):
                m.wait()
            parts = {0: small[...]}
            parts.update({c: land_s[i - 1, c] for c in range(1, 1 << len(bits))})
            for j in range(len(bits)):
                parts = {c: parts[c] + parts[c | 1 << j] for c in parts if not c >> j & 1}
            small[...] = parts[0]
        if i < len(rounds):
            for m in small_copies(i):
                m.start()

    assert all(len(bits) <= 2 for bits in rounds)
    for i in range(len(rounds) + 1):
        plan.setdefault(t_s + (SMALL_TICKS[i] if len(rounds) == 3 else i), []).append(functools.partial(small_round, i))
    end = max(max(plan), t_g + max(GA_SENDS)) + 1
    assert ns == len(GA_SENDS) + 1 and pairs == 6

    def tick(t, lo, hi):
        for s in range(steps):
            p = t - ENDS_M[s]

            @pl.when((p >= 0) & (p < n_chunk))
            def _():
                halve(mlp_pieces(p), s)
        if hi > t_h:
            for s in range(steps):
                for ends, first, end in ((ENDS_A, 0, 2 * pairs - 4), (ENDS_L, 2 * pairs - 4, 2 * pairs)):
                    q = t - t_h - 1 - ends[s]

                    @pl.when((q >= first) & (q < end) & (lax.rem(q + 2 * pairs, 2) == 0))
                    def _():
                        halve(attn_pieces(q // 2), s)
        for at in range(lo, hi):
            if at in plan:
                @pl.when(t == at)
                def _():
                    for act in plan[at]:
                        act()

    part = L // MOVES

    def moves(i):
        out = []
        for a, (src, dst) in enumerate(((x_in, xs), (g_in, gs))):
            for k in range(ns - 1, 0, -1):
                to = place.peer(jnp.int32(k))
                out.append(pltpu.make_async_remote_copy(
                    src.at[to, pl.ds(mul8(i * part), part)], dst.at[pl.ds(mul8(place.seq * L + i * part), part)],
                    s_in.at[a, k, i], r_in.at[a, k, i], device_id=(to, place.dp), device_id_type=MESH))
        return out

    once = []
    me = pl.ds(mul8(place.seq * L), L)
    for k in range(ns - 1, 0, -1):
        to = place.peer(jnp.int32(k))
        once.append(pltpu.make_async_remote_copy(
            cs_ref.at[to], css.at[place.seq], s_c.at[k], r_c.at[k], device_id=(to, place.dp), device_id_type=MESH))
    for src, dst in ((x_in, xs.at[me]), (g_in, gs.at[me]), (cs_ref, css.at[place.seq])):
        once.append(pltpu.make_async_copy(src.at[place.seq], dst, s_l.at[next(local)]))


    def row(i):
        return vec_ref[i:i + 1, :]

    def feed_forward(wu_ref, wd_ref, x_ref, g_ref, xm, xmT, dxm, y, a_s, dh_s):
        head, rest = pl.ds(0, C), pl.ds(C, FF - C)
        loads = [pltpu.make_async_copy(src, dst, s_l.at[next(local)])
                 for src, dst in ((x_in, x_ref), (g_in, g_ref), (wu_in.at[:, head], wu_ref.at[:, head]),
                                  (wd_in.at[head], wd_ref.at[head]), (wu_in.at[:, rest], wu_ref.at[:, rest]),
                                  (wd_in.at[rest], wd_ref.at[rest]))]
        for m in loads:
            m.start()
        for i, v in enumerate((ga_v, sa_v, gm_v, sm_v)):
            vec_ref[i:i + 1, :] = v[...].reshape(1, W)
        vec_ref[4:5, :] = (bo_v[...] + bd_v[...]).reshape(1, W)
        for i in range(3):
            vec_ref[5 + i:6 + i, :] = bq_v[i * W:(i + 1) * W].reshape(1, W)
        for i in range(FF // W):
            vec_ref[8 + i:9 + i, :] = bu_v[i * W:(i + 1) * W].reshape(1, W)
        loads[0].wait()
        small[...] = jnp.zeros_like(small)
        for b in range(ns):
            rows = slice(b * L, (b + 1) * L)
            x = x_ref[b].astype(F32)
            xhat, _ = norm_parts(x)
            v = (xhat * row(2) + row(3)).astype(BF)
            xm[rows, :] = v
            xmT[:, rows] = v.T
            y[rows, :] = x + row(4)
        dxm[...] = jnp.zeros_like(dxm)
        place.enter()
        for m in once + moves(0):
            m.start()
        for m in loads[1:4]:
            m.wait()

        stores = [pltpu.make_async_copy(src, dst, s_l.at[next(local)]) for src, dst in ((xm, y_out), (x_ref, gm_out))]

        @pl.loop(0, t_l + 1)
        def _(t):
            c = pl.ds(pl.multiple_of(jnp.minimum(t, n_chunk - 1) * C, C), C)

            @pl.when((t > 0) & (t < 4) | (t > 4) & (t < 2 * MOVES - 4) & (lax.rem(t, 2) == 1))
            def _():
                for m in moves(jnp.where(t < 4, t, (t + 3) // 2)):
                    m.start()

            @pl.when(t < n_chunk)
            def _():
                wu = wu_ref[:, c]
                wd = wd_ref[c, :]
                bu = vec_ref[pl.ds(8 + t // 3, 1), pl.ds(pl.multiple_of(lax.rem(t, 3) * C, C), C)]
                dbu = jnp.zeros((1, C), F32)
                for b in range(ns):
                    rows = slice(b * L, (b + 1) * L)
                    h = nn(xm[rows, :], wu) + bu
                    cdf, pdf = cdf_pdf(h)
                    a_s[rows, :] = (h * cdf).astype(BF)
                    dh = (nt(g_ref[b], wd) * (cdf + h * pdf)).astype(BF)
                    dh_s[rows, :] = dh
                    dbu += jnp.sum(dh.astype(F32), axis=0, keepdims=True)
                small[pl.ds(BIAS_UP + t // 3, 1), pl.ds(pl.multiple_of(lax.rem(t, 3) * C, C), C)] = dbu

            @pl.when(t == 0)
            def _():
                for m in loads[4:]:
                    m.wait()

            tick(t, 0, t_l + 1)

            @pl.when(t < n_chunk)
            def _():
                wu = wu_ref[:, c]
                wd = wd_ref[c, :]
                dh = dh_s[...]
                a = a_s[...]
                at = lax.rem(t, 2) * (n_chunk // 2) + t // 2
                du[at] = nn(xmT[...], dh).astype(BF)
                dd[at] = tn(a, g_ref[...].reshape(T, W)).astype(BF)
                begin(mlp_pieces(t))
                y[...] += nn(a, wd)
                dxm[...] += nt(dh, wu)

            @pl.when(t == t_l)
            def _():
                for b in range(ns):
                    rows = slice(b * L, (b + 1) * L)
                    xm[rows, :] = y[rows, :].astype(BF)
                stores[0].start()
                for b in range(ns):
                    rows = slice(b * L, (b + 1) * L)
                    xhat, rstd = norm_parts(x_ref[b].astype(F32))
                    dxa = dxm[rows, :]
                    gf = g_ref[b].astype(F32)
                    small[GAIN_M:GAIN_M + 1, :] += jnp.sum(dxa * xhat, axis=0, keepdims=True)
                    small[SHIFT_M:SHIFT_M + 1, :] += jnp.sum(dxa, axis=0, keepdims=True)
                    small[BIAS:BIAS + 1, :] += jnp.sum(gf, axis=0, keepdims=True)
                    x_ref[b] = (gf + norm_back(dxa * row(2), xhat, rstd)).astype(BF)
                stores[1].start()

        @pl.loop(0, MOVES)
        def _(i):
            for m in moves(i):
                m.wait()
        for m in once + stores:
            m.wait()

    def attention(wqkv, wo, wT, xaT, qkvT, kn, vn, dOT, obT, obn):
        attn, ga = kn, vn
        loads = [pltpu.make_async_copy(src, dst, s_l.at[next(local)]) for src, dst in ((wqkv_in, wqkv), (wo_in, wo))]
        for m in loads:
            m.start()
        loads[0].wait()
        for j in range(9):
            wT[j * 256:(j + 1) * 256, :] = wqkv[:, j * 256:(j + 1) * 256].T
        loads[1].wait()
        sub = lax.broadcasted_iota(jnp.int32, (L, L), 0)
        lane = lax.broadcasted_iota(jnp.int32, (L, L), 1)
        keep = sub <= lane
        rowid = lax.broadcasted_iota(jnp.int32, (128, 1), 0)

        def ga_copy(k):
            to = place.peer(k)
            return pltpu.make_async_remote_copy(
                ga.at[pl.ds(mul8(to * L), L)], ga_out.at[place.seq], s_out.at[k], r_out.at[k],
                device_id=(to, place.dp), device_id_type=MESH)

        ga_own = pltpu.make_async_copy(ga.at[me], ga_out.at[place.seq], s_out.at[0])
        attn_copy = pltpu.make_async_copy(attn, attn_out, r_out.at[0])

        def ob_copy(k, pair):
            to = place.peer(jnp.int32(k))
            cols = pl.ds(pl.multiple_of(pair * 128, 128), 128)
            return pltpu.make_async_remote_copy(
                obn.at[pl.ds(mul8(to * L), L), cols], ob_own.at[place.seq, :, cols], s_o.at[k, pair], r_o.at[k, pair],
                device_id=(to, place.dp), device_id_type=MESH)

        def unrotate(d, b):
            cos = css[b, :8, :]
            sin = css[b, 8:, :]
            return jnp.concatenate([d[:8] * cos + d[8:16] * sin, d[8:16] * cos - d[:8] * sin, d[16:]], axis=0)

        @pl.loop(t_p, end)
        def _(t):
            @pl.when(t < t_h)
            def _():
                b = t - t_p
                rows = pl.ds(pl.multiple_of(b * L, L), L)
                xhat, _ = norm_parts(xs[rows, :].astype(F32))
                xa = (xhat * row(0) + row(1)).astype(BF)
                xaT[:, rows] = xa.T
                cos = css[b, :8, :]
                sin = css[b, 8:, :]
                for j in range(9):
                    at = slice(j * 256, (j + 1) * 256)
                    bq = vec_ref[5 + j // 3:6 + j // 3, (j % 3) * 256:(j % 3 + 1) * 256]
                    m = nt(wT[at, :], xa) + jnp.broadcast_to(bq, (8, 256)).T[:, :1]
                    if j < 6:
                        parts = []
                        for h in range(4):
                            u = m[h * 64:(h + 1) * 64]
                            parts += [u[:8] * cos - u[8:16] * sin, u[8:16] * cos + u[:8] * sin, u[16:]]
                        m = jnp.concatenate(parts, axis=0)
                        if j < 3:
                            m = m * (HEAD ** -0.5)
                    mb = m.astype(BF)
                    qkvT[at, rows] = mb
                    if 3 <= j < 6:
                        kn[rows, (j - 3) * 256:(j - 2) * 256] = mb.T
                    if j >= 6:
                        vn[rows, (j - 6) * 256:(j - 5) * 256] = mb.T
                g = gs[rows, :]
                for j in range(3):
                    at = slice(j * 256, (j + 1) * 256)
                    dOT[at, rows] = nt(wo[at, :], g).astype(BF)

            @pl.when((t >= t_h) & (t < t_g))
            def _():
                head = t - t_h
                pair = head // 2
                r0 = pl.multiple_of(pair * 128, 128)
                cols = pl.ds(r0, 128)
                hr = pl.ds(pl.multiple_of(head * 64, 64), 64)
                kr = pl.ds(pl.multiple_of(W + head * 64, 64), 64)
                vr = pl.ds(pl.multiple_of(2 * W + head * 64, 64), 64)
                msk = rowid // 64 == lax.rem(head, 2)
                dk = [None] * ns
                dv = [None] * ns
                dq = [None] * ns
                for i in range(ns):
                    n = (i + 1) * L
                    qs = slice(i * L, (i + 1) * L)
                    qT2 = jnp.where(msk, qkvT[cols, qs], 0).astype(BF)
                    dO2 = jnp.where(msk, dOT[cols, qs], 0).astype(BF)
                    s = nn(kn[0:n, cols], qT2)
                    d = jnp.where(keep, s[n - L:], NEGATIVE)
                    s = jnp.concatenate([s[:n - L], d], axis=0) if i > 0 else d
                    e = jnp.exp(s - jnp.max(s, axis=0, keepdims=True))
                    inv = 1.0 / jnp.sum(e, axis=0, keepdims=True)
                    p = e.astype(BF)
                    oT = nn(qkvT[vr, 0:n], p) * inv
                    dO = dOT[hr, qs].astype(F32)
                    delta = jnp.sum(dO * oT, axis=0, keepdims=True)
                    obT[hr, qs] = oT.astype(BF)
                    dp = nn(vn[0:n, cols], dO2)
                    ds = (e * (dp - delta)).astype(BF)
                    dq[i] = nn(qkvT[kr, 0:n], ds) * (inv * HEAD ** -0.5)
                    dkT = nt((qkvT[hr, qs].astype(F32) * inv).astype(BF), ds)
                    dvT = nt((dO * inv).astype(BF), p)
                    for b in range(i + 1):
                        sl = slice(b * L, (b + 1) * L)
                        dk[b] = dkT[:, sl] if dk[b] is None else dk[b] + dkT[:, sl]
                        dv[b] = dvT[:, sl] if dv[b] is None else dv[b] + dvT[:, sl]
                for b in range(ns):
                    sl = slice(b * L, (b + 1) * L)
                    qkvT[hr, sl] = unrotate(dq[b], b).astype(BF)
                    qkvT[kr, sl] = unrotate(dk[b], b).astype(BF)
                    qkvT[vr, sl] = dv[b].astype(BF)

            @pl.when((t >= t_g) & (t < t_s))
            def _():
                k = t_s - 1 - t
                b = place.peer(k)
                rows = pl.ds(pl.multiple_of(b * L, L), L)
                dxa = nn(wqkv[...], qkvT[:, rows]).T
                xhat, rstd = norm_parts(xs[rows, :].astype(F32))
                small[GAIN_A:GAIN_A + 1, :] += jnp.sum(dxa * xhat, axis=0, keepdims=True)
                small[SHIFT_A:SHIFT_A + 1, :] += jnp.sum(dxa, axis=0, keepdims=True)
                ga[rows, :] = norm_back(dxa * row(0), xhat, rstd).astype(BF)

                @pl.when(k == 0)
                def _():
                    ga_own.start()

            tick(t, t_p, end)
            for i, later in enumerate(GA_SENDS):
                @pl.when(t == t_g + later)
                def _():
                    ga_copy(jnp.int32(ns - 1 - i)).start()

            @pl.when((t >= t_h) & (t < t_g) & (lax.rem(t - t_h + HEADS, 2) == 1))
            def _():
                pair = (t - t_h) // 2
                r0 = pl.multiple_of(pair * 128, 128)
                cols = pl.ds(r0, 128)
                obn[:, cols] = obT[cols, :].T
                for k in range(ns - 1, 0, -1):
                    ob_copy(k, pair).start()
                dm = jnp.concatenate([qkvT[cols, :], qkvT[pl.ds(W + r0, 128), :], qkvT[pl.ds(2 * W + r0, 128), :]], axis=0)
                da[pair, :384, :] = nt(dm, xaT[...]).astype(BF)
                da[pair, 384:, :] = nn(obT[cols, :], gs[...]).astype(BF)
                begin(attn_pieces(pair))
                db = nt(jnp.ones((8, T), BF), dm)
                for i in range(3):
                    small[BIAS_QKV + i:BIAS_QKV + i + 1, cols] = db[0:1, i * 128:(i + 1) * 128]

            @pl.when(t == t_e)
            def _():
                for k in range(1, ns):
                    for i in range(pairs):
                        ob_copy(k, i).wait()

            @pl.when((t >= t_e) & (t < t_e + ns))
            def _():
                b = t - t_e

                @pl.when(b == place.seq)
                def _():
                    ob_own[b] = obn[me, :]
                attn[pl.ds(pl.multiple_of(b * L, L), L), :] = nn(ob_own[b], wo[...]).astype(BF)

            @pl.when(t == t_e + ns - 1)
            def _():
                attn_copy.start()

        for k in range(ns - 1, 0, -1):
            ga_copy(jnp.int32(k)).wait()
        ga_own.wait()
        attn_copy.wait()
        small_out[...] = small[...]

    V = pltpu.VMEM
    FF = n_chunk * C
    pl.run_scoped(feed_forward, V((W, FF), BF), V((FF, W), BF), V((ns, L, W), BF), V((ns, L, W), BF), V((T, W), BF),
                  V((W, T), BF), V((T, W), F32), V((T, W), F32), V((T, C), BF), V((T, C), BF))
    pl.run_scoped(attention, V((W, 3 * W), BF), V((W, W), BF), V((3 * W, W), BF), V((W, T), BF), V((3 * W, T), BF), V((T, W), BF), V((T, W), BF),
                  V((W, T), BF), V((W, T), BF), V((T, W), BF))


def layer_call(sizes, x, g, cs, vecs, wu, wd, wqkv, wo):
    ns, L, W = x.shape
    T = ns * L
    FF = wu.shape[1]
    C = CHUNK
    n = FF // C
    pairs, R = HEADS // 2, 4 * 2 * HEAD
    steps = sum(s.bit_length() - 1 for s in sizes)
    vm = pl.BlockSpec(memory_space=pltpu.VMEM)
    hbm = pl.BlockSpec(memory_space=pl.ANY)
    S = jax.ShapeDtypeStruct
    V = pltpu.VMEM
    dma = pltpu.SemaphoreType.DMA
    la = Halving.land(R // 2, steps)
    return pl.pallas_call(
        functools.partial(layer_kernel, sizes),
        out_shape=(S((T, W), BF), S((ns, L, W), BF), S((n, W, C), BF), S((n, C, W), BF), S((pairs, R, W), BF),
                   S((T, W), BF), S((ns, L, W), BF), S((SMALL, W), F32)),
        in_specs=[hbm, hbm, vm] + [vm] * 8 + [hbm] * 4, out_specs=(hbm,) * 7 + (vm,),
        scratch_shapes=[V((n, W, C), BF), V((n, C, W), BF), V((n, Halving.land(W, steps), C), BF),
                        V((n, Halving.land(C, steps), W), BF), V((pairs, R, W), BF), V((pairs, la, W), BF),
                        V((pairs, la, W), BF), V((T, W), BF), V((T, W), BF), V(cs.shape, F32), V((ns, L, W), BF), V((SMALL, W), F32), V((SMALL, W), F32), V((steps, 4, SMALL, W), F32)]
        + [dma((n, steps))] * 4 + [dma((pairs, steps))] * 4 + [dma((2 * SPLIT_M, steps))] * 4 + [dma((3, steps))] * 4
        + [dma((2, ns, MOVES))] * 2 + [dma((ns,))] * 2 + [dma((ns, pairs))] * 2 + [dma((ns,))] * 2 + [dma((steps, 4))] * 2 + [dma((48,))],
        compiler_params=pltpu.CompilerParams(vmem_limit_bytes=255 << 18, collective_id=0, has_side_effects=True),
    )(x, g, cs, *vecs, wu, wd, wqkv, wo)


def finish_kernel(du, dd, da, y, gm, attn, ga, small, dwu, dwd, dwqkv, ddw, out, grad, s0, s1, s2, s3, s4, s4b, s5, s8,
                  vu, vd, va, ou, od, oq, ow, vy, vm, vo, vg, s_in, s_out):
    n, W, C = du.shape
    pairs = da.shape[0]
    ins, outs = [], []

    def fetch(src, dst):
        c = pltpu.make_async_copy(src, dst, s_in.at[len(ins)])
        ins.append(c)
        c.start()
        return c

    def store(src, dst):
        c = pltpu.make_async_copy(src, dst, s_out.at[len(outs)])
        outs.append(c)
        c.start()

    fd = [fetch(dd.at[i], vd.at[i]) for i in range(n)]
    fu = [fetch(du.at[i], vu.at[i]) for i in range(n)]
    fa = [fetch(da.at[i], va.at[i]) for i in range(pairs)]
    fy = [fetch(a, b) for a, b in ((y, vy), (attn, vo), (gm, vm), (ga, vg))]
    for i, v in ((GAIN_A, s0), (SHIFT_A, s1), (GAIN_M, s2), (SHIFT_M, s3), (BIAS, s4), (BIAS, s4b)):
        v[...] = small[i, :]
    for i in range(3):
        s5[i * W:(i + 1) * W] = small[BIAS_QKV + i, :]
    for i in range(n * C // W):
        s8[i * W:(i + 1) * W] = small[BIAS_UP + i, :]

    def chunk(i):
        j = 2 * i if i < n // 2 else 2 * (i - n // 2) + 1
        return slice(j * C, (j + 1) * C)

    for i in range(n):
        c = chunk(i)
        fd[i].wait()
        od[c, :] = vd[i].astype(F32)
        store(od.at[c, :], dwd.at[c, :])
    for i in range(n):
        fu[i].wait()
        ou[:, chunk(i)] = vu[i].astype(F32)
    for i in range(8):
        rows = slice(i * W // 8, (i + 1) * W // 8)
        store(ou.at[rows], dwu.at[rows])
    for i in range(pairs):
        fa[i].wait()
        c = slice(i * 128, (i + 1) * 128)
        ow[c, :] = va[i, 384:, :].astype(F32)
        store(ow.at[c, :], ddw.at[c, :])
        for k in range(3):
            oq[:, k * W + i * 128:k * W + (i + 1) * 128] = va[i, k * 128:(k + 1) * 128, :].astype(F32).T
    for i in range(8):
        rows = slice(i * W // 8, (i + 1) * W // 8)
        store(oq.at[rows], dwqkv.at[rows])
    for f in fy:
        f.wait()
    vo[...] = (vy[...].astype(F32) + vo[...].astype(F32)).astype(BF)
    store(vo, out)
    vg[...] = (vm[...].astype(F32) + vg[...].astype(F32)).astype(BF)
    store(vg, grad)
    for c in outs:
        c.wait()


def finish_call(du, dd, da, y, gm, attn, ga, small):
    n, W, C = du.shape
    pairs = da.shape[0]
    FF = n * C
    tokens = y.shape[0]
    vm = pl.BlockSpec(memory_space=pltpu.VMEM)
    hbm = pl.BlockSpec(memory_space=pl.ANY)
    S = jax.ShapeDtypeStruct
    V = pltpu.VMEM
    dma = pltpu.SemaphoreType.DMA
    return pl.pallas_call(
        finish_kernel,
        out_shape=(S((W, FF), F32), S((FF, W), F32), S((W, 3 * W), F32), S((W, W), F32), S((tokens, W), BF), S((tokens, W), BF))
        + (S((W,), F32),) * 6 + (S((3 * W,), F32), S((FF,), F32)),
        in_specs=[hbm] * 7 + [vm], out_specs=(hbm,) * 6 + (vm,) * 8,
        scratch_shapes=[V(du.shape, BF), V(dd.shape, BF), V(da.shape, BF), V((W, FF), F32), V((FF, W), F32),
                        V((W, 3 * W), F32), V((W, W), F32), V((tokens, W), BF), V((tokens, W), BF),
                        V((tokens, W), BF), V((tokens, W), BF), dma((2 * n + pairs + 4,)), dma((2 * n + 4 * pairs + 2,))],
        compiler_params=pltpu.CompilerParams(vmem_limit_bytes=63 << 20),
    )(du, dd, da, y, gm, attn, ga, small)


def on_device(hidden_in, positions, attn_gain, attn_shift, qkv_weight, qkv_bias, dense_weight, dense_bias,
              mlp_gain, mlp_shift, up_weight, up_bias, down_weight, down_bias, out_grad):
    sentences, local_len, W = hidden_in.shape
    sizes = (lax.axis_size("seq"), lax.axis_size("dp"))
    assert sentences == sizes[0]
    freqs = jnp.power(10000.0, -2.0 * jnp.arange(ROT // 2, dtype=F32) / ROT)
    angles = freqs[:, None] * positions.astype(F32)[:, None, :]
    cs = jnp.concatenate([jnp.cos(angles), jnp.sin(angles)], axis=1)
    vecs = (attn_gain, attn_shift, mlp_gain, mlp_shift, dense_bias, down_bias, qkv_bias, up_bias)
    y, gm, du, dd, da, attn, ga, small = layer_call(
        sizes, hidden_in, out_grad, cs, vecs, up_weight, down_weight, qkv_weight, dense_weight)
    dwu, dwd, dwqkv, ddw, layer_out, input_grad, s0, s1, s2, s3, s4, s4b, s5, s8 = finish_call(
        du, dd, da, y, gm.reshape(-1, W), attn, ga.reshape(-1, W), small)
    return (layer_out.reshape(hidden_in.shape), input_grad.reshape(hidden_in.shape), s0, s1, dwqkv, s5, ddw, s4, s2, s3,
            dwu, s8, dwd, s4b)


def solution(mesh):
    act, rep = P("dp", "seq", None), P()
    return jax.shard_map(
        on_device, mesh=mesh,
        in_specs=(act, P("dp", "seq")) + (rep,) * 12 + (act,),
        out_specs=(act, act) + (rep,) * 12,
        check_vma=False)
```
